32 devices in a mesh: phi: 2 (over x), row: 4 (over y, core), mass: 4 (over z).
Axes of the slice: x: 2, y: 2, z: 4, core: 2. Of those that a mesh axis runs over, the one named last changes fastest.
Arguments:
- density: float32 [256, 64, 512], P('mass', 'phi', 'row'), may hold values from 0.05 to 1
- cotangent: float32 [256, 64, 512], P('mass', 'phi', 'row'), may hold values from -6 to 6
- drift_in: float32 [256, 512], P('mass'), may hold values from 0.02 to 0.3
- drift_out: float32 [256, 512], P('mass'), may hold values from 0.02 to 0.3
- spread: float32 [256], P('mass'), may hold values from 0.01 to 0.15
- dest_bins: int32 [256], replicated, may hold values from 1 to 254, as said below
- bott_split: float32 [256], replicated, may hold values from 0.05 to 0.95
- coag_rate: float32 [256], replicated, may hold values from 0.05 to 0.3
- frag_pairs: int32 [4, 4], replicated, may hold values from 0 to 1, as said below
- frag_gain: float32 [256, 256], replicated, may hold values from 0.001 to 0.02
- frag_rate: float32 [256], replicated, may hold values from 0.02 to 0.2
- collide_speed: float32 [64, 512], P('phi', 'row'), may hold values from 0.2 to 5
- frag_speed: float32 [512], P('row'), may hold values from 0.5 to 2
- regime: int32 [64, 512], P('phi', 'row'), may hold values 0 or 1
Outputs:
- density_adjoint: float32 [256, 64, 512], P('mass', 'phi', 'row')
- speed_gradient: float32 [512], P('row')
The draws below stay inside these ranges and needn't reach their ends.
Inputs may be any that keep to these rules, and one draw needn't show every extreme that they name: dest_bins[j] lies between j + 1 and j + 6, but never above 254; dest_bins[0] is 1 and the top bins map to 254. frag_pairs is 1 on the diagonal and in the first row, 0 below the diagonal.
All inputs are finite; a program needn't handle non-finite values. No bound on the sum of `regime` on one device may be relied on, other than what follows from the above.
Results may differ from the reference program's by a relative error of at most 0.000078.
Values sent between devices are 32-bit elements; how exact they have to be, the bound alone decides.
No kernel may reach another device: no remote copies, remote signals or barrier semaphores. Data moves between devices by JAX's collectives and lax.ppermute only.
A program may use at most 128 MiB of HBM per device.

```python
import math
import jax
import jax.numpy as jnp
from jax import lax

MB = 256
RANGE = 64
NB = 4
NA = 64
NR = 512


def draw_dest_bins(key, part):
    offsets = jax.random.randint(key, (MB,), 0, 6, dtype=jnp.int32)
    bin_ids = jnp.arange(MB, dtype=jnp.int32)
    offsets = jnp.where(bin_ids == 0, 0, offsets)
    return jnp.minimum(bin_ids + 1 + offsets, MB - 2).astype(jnp.int32)


def draw_frag_pairs(key, part):
    source_ids = jnp.arange(NB, dtype=jnp.int32)[None, :]
    target_ids = jnp.arange(NB, dtype=jnp.int32)[:, None]
    random_bits = jax.random.randint(key, (NB, NB), 0, 2, dtype=jnp.int32)
    always_on = jnp.logical_or(target_ids == source_ids, target_ids == 0)
    chosen = jnp.where(always_on, 1, random_bits)
    return jnp.where(source_ids < target_ids, 0, chosen).astype(jnp.int32)


def set_ends(array, own_key, low, high):
    spot = [jax.random.randint(jax.random.fold_in(own_key, axis), (), 0, length) for axis, length in enumerate(array.shape)]
    longest = array.shape.index(max(array.shape))
    next_to = spot[:longest] + [(spot[longest] + 1) % array.shape[longest]] + spot[longest + 1:]
    return array.at[tuple(spot)].set(low).at[tuple(next_to)].set(high)


def shard_levels(stream_key, extent, cuts, least, high):
    factor_of = 1.0
    for dim, blocks in cuts:
        draws = jax.random.uniform(jax.random.fold_in(jax.random.fold_in(stream_key, 6), dim), (blocks,), jnp.float32, least / len(cuts), high / len(cuts))
        factor_of = factor_of * jnp.repeat(jnp.exp(draws), extent[dim] // blocks).reshape((-1,) + (1,) * (len(extent) - 1 - dim))
    return factor_of


def normal_values(own_key, dims, deviation, bound, shards=(), kind=jnp.bfloat16):
    result = jax.random.normal(own_key, dims, jnp.float32) * deviation
    if len(shards) > 0:
        result = shard_levels(own_key, dims, shards, -0.22, 0.18) * result
    return jnp.clip(result, min=-bound, max=bound).astype(kind)


def setup_inputs(seed: int = 0) -> dict:
    splits = jax.random.split(jax.random.key(seed), 15)
    return {
        "density": jnp.clip(jnp.exp(math.log(1.0) - 2.9957323 * jax.random.uniform(splits[0], (MB, NA, NR), jnp.float32) ** shard_levels(splits[0], (MB, NA, NR), ((0, 4), (1, 2), (2, 4)), -0.2, 0.2)), 0.05, 1.0),
        "cotangent": normal_values(splits[1], (MB, NA, NR), 1.0, 6.0, ((0, 4), (1, 2), (2, 4)), jnp.float32),
        "drift_in": jnp.clip(jnp.exp(math.log(0.3) - 2.7080503 * jax.random.uniform(splits[2], (MB, NR), jnp.float32) ** shard_levels(splits[2], (MB, NR), ((0, 4),), -0.2, 0.2)), 0.02, 0.3),
        "drift_out": jnp.clip(jnp.exp(math.log(0.3) - 2.7080503 * jax.random.uniform(splits[3], (MB, NR), jnp.float32) ** shard_levels(splits[3], (MB, NR), ((0, 4),), -0.2, 0.2)), 0.02, 0.3),
        "spread": jnp.clip(jnp.exp(math.log(0.15) - 2.7080503 * jax.random.uniform(splits[4], (MB,), jnp.float32) ** shard_levels(splits[4], (MB,), ((0, 4),), -0.2, 0.2)), 0.01, 0.15),
        "dest_bins": draw_dest_bins(jax.random.fold_in(splits[14], 71), 0),
        "bott_split": jnp.clip(jax.random.uniform(splits[6], (MB,), jnp.float32, 0.05, 0.95), 0.05, 0.95),
        "coag_rate": jnp.clip(jnp.exp(jax.random.uniform(splits[7], (MB,), jnp.float32, math.log(0.05), math.log(0.3))), 0.05, 0.3),
        "frag_pairs": draw_frag_pairs(jax.random.fold_in(splits[14], 71), 0),
        "frag_gain": jnp.clip(jnp.exp(jax.random.uniform(splits[9], (MB, MB), jnp.float32, math.log(0.001), math.log(0.02))), 0.001, 0.02),
        "frag_rate": jnp.clip(jnp.exp(jax.random.uniform(splits[10], (MB,), jnp.float32, math.log(0.02), math.log(0.2))), 0.02, 0.2),
        "collide_speed": jnp.clip(jnp.exp(math.log(5.0) - 3.218876 * jax.random.uniform(splits[11], (NA, NR), jnp.float32) ** shard_levels(splits[11], (NA, NR), ((0, 2), (1, 4)), -0.2, 0.2)), 0.2, 5.0),
        "frag_speed": jnp.clip(0.5 + 1.5 * jax.random.uniform(splits[12], (NR,), jnp.float32) ** shard_levels(splits[12], (NR,), ((0, 4),), -0.2, 0.2), 0.5, 2.0),
        "regime": set_ends((jax.random.randint(splits[13], (NA, NR), 0, 4) < 3).astype(jnp.int32), jax.random.fold_in(splits[13], 1), 0, 1),
    }


gate_width = 0.5
highest = lax.Precision.HIGHEST


def coag_matrix(dest_bins, bott_split, coag_rate):
    number = dest_bins.shape[0]
    row_ids = jnp.arange(number, dtype=jnp.int32)[:, None]
    col_ids = jnp.arange(number, dtype=jnp.int32)[None, :]
    target = dest_bins[None, :]
    lower_part = (row_ids == target).astype(jnp.float32) * (1.0 - bott_split)[None, :]
    upper_part = (row_ids == target + 1).astype(jnp.float32) * bott_split[None, :]
    keeper = (row_ids == col_ids).astype(jnp.float32)
    return (lower_part + upper_part - keeper) * coag_rate[None, :]


def frag_matrix(frag_pairs, frag_gain, frag_rate):
    number = frag_gain.shape[0]
    blocks = jnp.repeat(jnp.repeat(frag_pairs, RANGE, axis=0), RANGE, axis=1).astype(jnp.float32)
    row_ids = jnp.arange(number, dtype=jnp.int32)[:, None]
    col_ids = jnp.arange(number, dtype=jnp.int32)[None, :]
    below_diag = (row_ids <= col_ids).astype(jnp.float32)
    keeper = (row_ids == col_ids).astype(jnp.float32)
    return frag_gain * blocks * below_diag - keeper * frag_rate[None, :]


def transport(field, drift_in, drift_out, spread):
    center = 1.0 - drift_in - drift_out - 2.0 * spread[:, None]
    padded = jnp.pad(field, ((0, 0), (0, 0), (1, 1)))
    in_pad = jnp.pad(drift_in, ((0, 0), (1, 1)))
    out_pad = jnp.pad(drift_out, ((0, 0), (1, 1)))
    beside_all = jnp.roll(field, 1, axis=1) + jnp.roll(field, -1, axis=1)
    return (center[:, None, :] * field + in_pad[:, None, 2:] * padded[:, :, 2:]
            + out_pad[:, None, :-2] * padded[:, :, :-2] + spread[:, None, None] * beside_all)


def transport_back(field, drift_in, drift_out, spread):
    center = 1.0 - drift_in - drift_out - 2.0 * spread[:, None]
    padded = jnp.pad(field, ((0, 0), (0, 0), (1, 1)))
    beside_all = jnp.roll(field, 1, axis=1) + jnp.roll(field, -1, axis=1)
    return (center[:, None, :] * field + drift_in[:, None, :] * padded[:, :, :-2]
            + drift_out[:, None, :] * padded[:, :, 2:] + spread[:, None, None] * beside_all)


def bins_apply(matrix, field):
    layout = field.shape
    flat_field = field.reshape(layout[0], -1)
    return jnp.dot(matrix, flat_field, precision=highest, preferred_element_type=jnp.float32).reshape(layout)


def reference(density, cotangent, drift_in, drift_out, spread, dest_bins, bott_split, coag_rate, frag_pairs, frag_gain, frag_rate, collide_speed, frag_speed, regime):
    coag_full = coag_matrix(dest_bins, bott_split, coag_rate)
    frag_full = frag_matrix(frag_pairs, frag_gain, frag_rate)
    sigma = jax.nn.sigmoid((collide_speed - frag_speed[None, :]) / gate_width)
    flagged = regime.astype(jnp.float32)
    frag_gate = flagged * sigma
    gate_slope = -flagged * sigma * (1.0 - sigma) / gate_width
    moved_first = transport(density, drift_in, drift_out, spread)
    mixed_first = bins_apply(coag_full, moved_first) + bins_apply(frag_full, frag_gate[None] * moved_first)
    state_first = moved_first + mixed_first
    moved_second = transport(state_first, drift_in, drift_out, spread)
    coag_second = bins_apply(coag_full.T, cotangent)
    frag_second = bins_apply(frag_full.T, cotangent)
    weight_second = cotangent + (coag_second + frag_gate[None] * frag_second)
    adjoint_first = transport_back(weight_second, drift_in, drift_out, spread)
    coag_first = bins_apply(coag_full.T, adjoint_first)
    frag_first = bins_apply(frag_full.T, adjoint_first)
    weight_first = adjoint_first + (coag_first + frag_gate[None] * frag_first)
    density_adjoint = transport_back(weight_first, drift_in, drift_out, spread)
    products = jnp.sum(moved_first * frag_first + moved_second * frag_second, axis=0)
    speed_gradient = jnp.sum(gate_slope * products, axis=0)
    return density_adjoint, speed_gradient
```

```python
import functools
import math

import jax
import jax.numpy as jnp
from jax import lax
from jax.experimental import pallas as pl
from jax.experimental.pallas import tpu as pltpu
from jax.sharding import PartitionSpec as P

RANGE = 64
LANES = 128
GROUPS = 4
EDGE = 16
gate_width = 0.5
first_dims = (((0,), (0,)), ((), ()))
VMEM_LIMIT = 56 * 2**20


def coag_matrix(dest_bins, bott_split, coag_rate):
    number = dest_bins.shape[0]
    row_ids = jnp.arange(number, dtype=jnp.int32)[:, None]
    col_ids = jnp.arange(number, dtype=jnp.int32)[None, :]
    target = dest_bins[None, :]
    lower_part = (row_ids == target).astype(jnp.float32) * (1.0 - bott_split)[None, :]
    upper_part = (row_ids == target + 1).astype(jnp.float32) * bott_split[None, :]
    keeper = (row_ids == col_ids).astype(jnp.float32)
    return (lower_part + upper_part - keeper) * coag_rate[None, :] + keeper


def frag_matrix(frag_pairs, frag_gain, frag_rate):
    number = frag_gain.shape[0]
    blocks = jnp.repeat(jnp.repeat(frag_pairs, RANGE, axis=0), RANGE, axis=1).astype(jnp.float32)
    row_ids = jnp.arange(number, dtype=jnp.int32)[:, None]
    col_ids = jnp.arange(number, dtype=jnp.int32)[None, :]
    below_diag = (row_ids <= col_ids).astype(jnp.float32)
    keeper = (row_ids == col_ids).astype(jnp.float32)
    return frag_gain * blocks * below_diag - keeper * frag_rate[None, :]


def halves(matrix):
    high = lax.reduce_precision(matrix, 8, 7)
    return high.astype(jnp.bfloat16), (matrix - high).astype(jnp.bfloat16)


def split(value):
    high = value.astype(jnp.bfloat16)
    return high, (value - high.astype(jnp.float32)).astype(jnp.bfloat16)


def product(value, high_ref, low_ref, dims=(((1,), (0,)), ((), ()))):
    high, low = split(value)
    dot = functools.partial(lax.dot_general, dimension_numbers=dims, preferred_element_type=jnp.float32)
    return dot(high, high_ref[...]) + (dot(high, low_ref[...]) + dot(low, high_ref[...]))


def stencil(slab, index, center, lower, upper, side, start, size):
    rows = pl.ds(start, size)
    return (
        center * slab[(*index(0), rows)]
        + lower * slab[(*index(0), pl.ds(start - 1, size))]
        + upper * slab[(*index(0), pl.ds(start + 1, size))]
        + side * (slab[(*index(-1), rows)] + slab[(*index(1), rows)])
    )


def forward_kernel(
    azimuth,
    radial,
    own_ref,
    next_ref,
    own_az_ref,
    next_az_ref,
    strip_ref,
    gate_ref,
    slope_ref,
    center_ref,
    lower_ref,
    upper_ref,
    side_ref,
    high_ref,
    low_ref,
    moved_ref,
    second_ref,
    slab,
    mixed,
):
    inner = pl.ds(EDGE, radial)
    wide = radial + 16

    def place(row, source, other, start, stride):
        bins = jnp.concatenate(
            [source[pl.ds(start, RANGE, stride=stride), :], other[pl.ds(start, RANGE, stride=stride), :]], axis=0
        )
        slab[row, inner, :] = bins.T
        tile = strip_ref[row]
        slab[row, pl.ds(EDGE - 8, 8), :] = tile
        slab[row, pl.ds(EDGE + radial, 8), :] = tile

    for row, k in ((0, 0), (1, 1), (azimuth + 2, 2), (azimuth + 3, 3)):
        place(row, own_az_ref, next_az_ref, k, 4)

    @pl.loop(0, azimuth)
    def _(a):
        place(a + 2, own_ref, next_ref, a, azimuth)

    def move(a):
        moved = stencil(
            slab,
            lambda d: (a + d,),
            center_ref[1, pl.ds(8, wide), :],
            lower_ref[1, pl.ds(8, wide), :],
            upper_ref[1, pl.ds(8, wide), :],
            side_ref[1:2, :],
            8,
            wide,
        )
        gated = gate_ref[a, pl.ds(8, wide), :] * moved
        result = product(jnp.concatenate([moved, gated], axis=1), high_ref, low_ref)
        mixed[a, 0, pl.ds(8, wide), :] = result[:, :LANES]
        mixed[a, 1, pl.ds(8, wide), :] = result[:, LANES:]
        return moved[8 : 8 + radial]

    move(1)
    move(azimuth + 2)

    @pl.loop(0, azimuth)
    def _(a):
        moved_ref[a] = slope_ref[a] * move(a + 2)

    @pl.loop(0, azimuth)
    def _(a):
        for t in range(2):
            second = stencil(
                mixed,
                lambda d: (a + 2 + d, t),
                center_ref[t, inner, :],
                lower_ref[t, inner, :],
                upper_ref[t, inner, :],
                side_ref[t : t + 1, :],
                EDGE,
                radial,
            )
            second_ref[a, t] = slope_ref[a] * second


def adjoint_kernel(azimuth, radial, low_row, high_row, *refs):
    first, last = low_row == 0, high_row == azimuth + 4
    refs = list(refs)

    def take(number):
        taken = refs[:number]
        del refs[:number]
        return taken

    slots = take(4)
    sides = take(4) if first or last else None
    strip_ref, gate_ref, second_ref, moved_ref = take(4)
    center_ref, lower_ref, upper_ref, side_ref = take(4)
    high1_ref, low1_ref, high2_ref, low2_ref = take(4)
    carry_second, carry_first, carry_sum = (None, None, None) if first else take(3)
    own_out, next_out, sum_out = take(3)
    keep_second, keep_first = (None, None) if last else take(2)
    second, initial = take(2)

    inner = pl.ds(EDGE, radial)
    wide = radial + 16
    outer = pl.ds(8, wide)
    base = low_row if first else low_row - 2
    first_low, first_high = (1 if first else low_row - 1), high_row - 1
    first_base = first_low if first else first_low - 2
    out_low, out_high = first_base + 1, first_high - 1

    if first:
        sum_out[...] = jnp.zeros_like(sum_out)
    else:
        second[pl.ds(0, 2)] = carry_second[...]
        initial[pl.ds(0, 2)] = carry_first[...]
        sum_out[...] = carry_sum[...]

    rows = high_row - low_row
    strips = product(strip_ref[pl.ds(low_row, rows)].reshape(rows * 8, 4 * RANGE), high1_ref, low1_ref)
    for i in range(rows):
        piece = strips[i * 8 : i * 8 + 8]
        for start in (EDGE - 8, EDGE + radial):
            gate = gate_ref[low_row + i, pl.ds(start, 8), :]
            for t in range(2):
                second[low_row + i - base, t, pl.ds(start, 8), :] = (
                    piece[:, t * LANES : (t + 1) * LANES] + gate * piece[:, (t + 2) * LANES : (t + 3) * LANES]
                )

    def weigh(row, sources, start, stride):
        bins = jnp.concatenate([source[pl.ds(start, RANGE, stride=stride), :] for source in sources], axis=0)
        result = product(bins, high1_ref, low1_ref, first_dims)
        gate = gate_ref[row, inner, :]
        frag = (result[:, 2 * LANES : 3 * LANES], result[:, 3 * LANES :])
        for t in range(2):
            second[row - base, t, inner, :] = result[:, t * LANES : (t + 1) * LANES] + gate * frag[t]
        return frag

    own_low, own_high = max(low_row, 2), min(high_row, azimuth + 2)

    if first:
        weigh(0, sides, 0, 4)
        weigh(1, sides, 1, 4)

    @pl.loop(own_low, own_high)
    def _(row):
        frag = weigh(row, slots, row - own_low, own_high - own_low)
        sum_out[...] += second_ref[row - 2, 0] * frag[0] + second_ref[row - 2, 1] * frag[1]

    if last:
        weigh(azimuth + 2, sides, 2, 4)
        weigh(azimuth + 3, sides, 3, 4)

    def adjoin(row):
        parts = [
            stencil(
                second,
                lambda d: (row - base + d, t),
                center_ref[t, outer, :],
                lower_ref[t, outer, :],
                upper_ref[t, outer, :],
                side_ref[t : t + 1, :],
                8,
                wide,
            )
            for t in range(2)
        ]
        result = product(jnp.concatenate(parts, axis=1), high2_ref, low2_ref)
        frag = result[:, LANES:]
        initial[row - first_base, outer, :] = result[:, :LANES] + gate_ref[row, outer, :] * frag
        return frag[8 : 8 + radial]

    if first:
        adjoin(1)

    @pl.loop(max(first_low, 2), min(first_high, azimuth + 2))
    def _(row):
        sum_out[...] += moved_ref[row - 2] * adjoin(row)

    if last:
        adjoin(azimuth + 2)

    @pl.loop(out_low, out_high)
    def _(row):
        result = stencil(
            initial,
            lambda d: (row - first_base + d,),
            center_ref[1, inner, :],
            lower_ref[1, inner, :],
            upper_ref[1, inner, :],
            side_ref[1:2, :],
            EDGE,
            radial,
        ).T
        own_out[row - out_low] = result[:RANGE]
        next_out[row - out_low] = result[RANGE:]

    if not last:
        keep_second[...] = second[pl.ds(high_row - 2 - base, 2)]
        keep_first[...] = initial[pl.ds(first_high - 2 - first_base, 2)]


def call(kernel, outs, scratch, flops, operands):
    size = sum(x.size * x.dtype.itemsize for x in operands) + sum(4 * math.prod(o) for o in outs)
    vmem = pl.BlockSpec(memory_space=pltpu.VMEM)
    return pl.pallas_call(
        kernel,
        out_shape=[jax.ShapeDtypeStruct(o, jnp.float32) for o in outs],
        in_specs=[vmem] * len(operands),
        out_specs=[vmem] * len(outs),
        scratch_shapes=[pltpu.VMEM(s, jnp.float32) for s in scratch],
        compiler_params=pltpu.CompilerParams(vmem_limit_bytes=VMEM_LIMIT),
        cost_estimate=pl.CostEstimate(flops=flops, bytes_accessed=size, transcendentals=0),
    )(*operands)


def per_device(
    density,
    cotangent,
    drift_in,
    drift_out,
    spread,
    dest_bins,
    bott_split,
    coag_rate,
    frag_pairs,
    frag_gain,
    frag_rate,
    collide_speed,
    frag_speed,
    regime,
):
    own_bins, azimuth, radial = density.shape
    ranges = lax.axis_size("mass")
    place = lax.axis_index("mass")
    row_index = lax.axis_index("row")
    phis, rows = lax.axis_size("phi"), lax.axis_size("row")
    up = [(i, i + 1) for i in range(ranges - 2)]
    up_two = [(i, i + 2) for i in range(ranges - 3)]
    down = [(i + 1, i) for i in range(ranges - 1)]
    ending = [(ranges - 1, ranges - 2)]
    returning = [(ranges - 2, ranges - 1)]

    cuts = [azimuth * k // GROUPS for k in range(GROUPS + 1)]
    pieces = [cotangent[:, i:j] for i, j in zip(cuts, cuts[1:])]
    gathered = [
        [
            lax.ppermute(piece, "mass", up_two),
            lax.ppermute(piece, "mass", up),
            piece,
            lax.ppermute(piece, "mass", down),
        ]
        for piece in pieces
    ]
    density_next = lax.ppermute(density, "mass", ending)

    sigma = jax.nn.sigmoid((collide_speed - frag_speed[None, :]) / gate_width)
    flagged = regime.astype(jnp.float32)
    frag_gate = flagged * sigma
    gate_slope = -flagged * sigma * (1.0 - sigma) / gate_width
    gate_slope = gate_slope * (place < ranges - 1).astype(jnp.float32)

    def band(low, high):
        return jnp.concatenate([cotangent[:, low:high], density[:, low:high], frag_gate[None, low:high]], axis=0)

    ring = [(i, (i + 1) % phis) for i in range(phis)]
    back = [(j, i) for i, j in ring]
    before = lax.ppermute(band(azimuth - 2, azimuth), "phi", ring)
    after = lax.ppermute(band(0, 2), "phi", back)

    def columns(low, high):
        body = band(0, azimuth)[:, :, low:high]
        whole = jnp.concatenate([before[:, :, low:high], body, after[:, :, low:high]], axis=1)
        return whole.transpose(1, 2, 0).reshape(2 * (azimuth + 4), 2 * own_bins + 1)

    line = [(i, i + 1) for i in range(rows - 1)]
    left = lax.ppermute(columns(radial - 2, radial), "row", line).reshape(azimuth + 4, 2, -1)
    right = lax.ppermute(columns(0, 2), "row", [(j, i) for i, j in line]).reshape(azimuth + 4, 2, -1)

    gates = jnp.concatenate([before[-1], frag_gate, after[-1]], axis=0)
    gap = jnp.zeros((azimuth + 4, EDGE - 2), jnp.float32)
    gates = jnp.concatenate([gap, left[:, :, -1], gates, right[:, :, -1], gap], axis=1)
    gate_wide = jnp.broadcast_to(gates[:, :, None], gates.shape + (LANES,))
    slope_wide = jnp.broadcast_to(gate_slope[:, :, None], gate_slope.shape + (LANES,))

    def window(drift):
        padded = jnp.pad(drift, ((0, 0), (EDGE, EDGE)))
        wide = lax.dynamic_slice_in_dim(padded, row_index * radial, radial + 2 * EDGE, 1)
        return wide.T

    drifts = jnp.concatenate([window(drift_in), window(drift_out)], axis=0)
    spreads = jnp.broadcast_to(spread[None, :], (8, own_bins))
    edges = jnp.concatenate([left[:, :, :-1], right[:, :, :-1]], axis=1).reshape(4 * (azimuth + 4), 2 * own_bins)
    sides = jnp.concatenate([before[:-1], after[:-1]], axis=1)
    edges_cot, edges_den = edges[:, :own_bins], edges[:, own_bins:]
    sides_cot, sides_den = sides[:own_bins], sides[own_bins:]

    def packed(parts):
        return jnp.concatenate([p.reshape(-1, LANES) for p in parts], axis=0)

    def unpacked(message, parts):
        out, at = [], 0
        for p in parts:
            size = p.size // LANES
            out.append(message[at : at + size].reshape(p.shape))
            at += size
        return out

    own_parts = [edges_cot, sides_cot, drifts, spreads]
    message = packed(own_parts)
    far = unpacked(lax.ppermute(message, "mass", up_two), own_parts)
    near = unpacked(lax.ppermute(message, "mass", up), own_parts)
    over = unpacked(lax.ppermute(message, "mass", down), own_parts)
    den_parts = [edges_den, sides_den]
    den_over = unpacked(lax.ppermute(packed(den_parts), "mass", ending), den_parts)

    def strip_of(edge_list):
        wide = jnp.concatenate(edge_list, axis=1).reshape(azimuth + 4, 4, -1)
        blank = jnp.zeros((azimuth + 4, 4, wide.shape[2]), jnp.float32)
        return jnp.concatenate([wide[:, 2:], blank, wide[:, :2]], axis=1)

    by_slot = [far, near, own_parts, over]
    strip_cot = strip_of([s[0] for s in by_slot])
    strip_den = strip_of([edges_den, den_over[0]])
    sides_by_slot = [s[1].reshape(own_bins * 4, radial) for s in by_slot]

    def tiled(wide):
        return wide.reshape(wide.shape[0], 2, LANES).transpose(1, 0, 2)

    length = radial + 2 * EDGE
    drift_wide = tiled(jnp.concatenate([s[2] for s in by_slot], axis=1))
    inward, outward = drift_wide[:, :length], drift_wide[:, length:]
    side = tiled(jnp.concatenate([s[3] for s in by_slot], axis=1)[:1])[:, 0]
    center = 1.0 - inward - outward - 2.0 * side[:, None, :]
    inward_next = jnp.concatenate([inward[:, 1:], inward[:, :1]], axis=1)
    outward_last = jnp.concatenate([outward[:, -1:], outward[:, :-1]], axis=1)

    def related(matrix):
        padded = jnp.pad(matrix, ((2 * RANGE, RANGE), (2 * RANGE, RANGE)))
        return lax.dynamic_slice(padded, (place * RANGE, place * RANGE), (4 * RANGE, 4 * RANGE))

    coag = related(coag_matrix(dest_bins, bott_split, coag_rate))
    frag = related(frag_matrix(frag_pairs, frag_gain, frag_rate))
    both = halves(jnp.concatenate([coag, frag], axis=1))
    upper_half = jnp.concatenate([coag[:, 2 * RANGE :], frag[:, 2 * RANGE :]], axis=1)
    own_cols = halves(upper_half)
    own_rows = halves(upper_half.T)

    moved, second = call(
        functools.partial(forward_kernel, azimuth, radial),
        [(azimuth, radial, LANES), (azimuth, 2, radial, LANES)],
        [(azimuth + 4, length, LANES), (azimuth + 4, 2, length, LANES)],
        6 * (azimuth + 2) * (radial + 16) * 256 * 256,
        [
            density.reshape(own_bins * azimuth, radial),
            density_next.reshape(own_bins * azimuth, radial),
            sides_den.reshape(own_bins * 4, radial),
            den_over[1].reshape(own_bins * 4, radial),
            strip_den,
            gate_wide,
            slope_wide,
            center,
            outward_last,
            inward_next,
            side,
            *own_rows,
        ],
    )

    own_outs, next_outs, carry = [], [], []
    for g in range(GROUPS):
        first, last = g == 0, g == GROUPS - 1
        low_row = 0 if first else cuts[g] + 2
        high_row = azimuth + 4 if last else cuts[g + 1] + 2
        new = high_row - low_row
        n_out = (azimuth + 2 if last else high_row - 2) - (2 if first else low_row - 2)
        operands = [x.reshape(-1, radial) for x in gathered[g]]
        if first or last:
            operands += sides_by_slot
        operands += [strip_cot, gate_wide, second, moved, center, inward, outward, side, *both, *own_cols, *carry]
        outs = [(n_out, RANGE, radial), (n_out, RANGE, radial), (radial, LANES)]
        if not last:
            outs += [(2, 2, length, LANES), (2, length, LANES)]
        own_out, next_out, total, *kept = call(
            functools.partial(adjoint_kernel, azimuth, radial, low_row, high_row),
            outs,
            [(new + 2, 2, length, LANES), (new + 2, length, LANES)],
            6 * new * (radial + 16) * 256 * 768,
            operands,
        )
        carry = [*kept, total]
        own_outs.append(own_out)
        next_outs.append(lax.ppermute(next_out, "mass", returning))
    is_last = place == ranges - 1
    result = jnp.concatenate(
        [jnp.where(is_last, there, here) for here, there in zip(own_outs, next_outs)], axis=0
    ).transpose(1, 0, 2)
    speed_gradient = lax.psum(jnp.sum(total, axis=1), ("phi", "mass"))
    return (result, speed_gradient)


def solution(mesh):
    in_specs = (
        P("mass", "phi", "row"),
        P("mass", "phi", "row"),
        P("mass", None),
        P("mass", None),
        P("mass"),
        P(),
        P(),
        P(),
        P(),
        P(),
        P(),
        P("phi", "row"),
        P("row"),
        P("phi", "row"),
    )
    out_specs = (P("mass", "phi", "row"), P("row"))
    return jax.shard_map(
        per_device, mesh=mesh, in_specs=in_specs, out_specs=out_specs, check_vma=False
    )
```

```python
import functools
import math

import jax
import jax.numpy as jnp
from jax import lax
from jax.experimental import pallas as pl
from jax.experimental.pallas import tpu as pltpu
from jax.sharding import PartitionSpec as P

RANGE = 64
LANES = 128
EDGE = 16
gate_width = 0.5
BATCH = 4
VMEM_LIMIT = 56 * 2**20


def coag_matrix(dest_bins, bott_split, coag_rate):
    number = dest_bins.shape[0]
    row_ids = jnp.arange(number, dtype=jnp.int32)[:, None]
    col_ids = jnp.arange(number, dtype=jnp.int32)[None, :]
    target = dest_bins[None, :]
    lower_part = (row_ids == target).astype(jnp.float32) * (1.0 - bott_split)[None, :]
    upper_part = (row_ids == target + 1).astype(jnp.float32) * bott_split[None, :]
    keeper = (row_ids == col_ids).astype(jnp.float32)
    return (lower_part + upper_part - keeper) * coag_rate[None, :] + keeper


def frag_matrix(frag_pairs, frag_gain, frag_rate):
    number = frag_gain.shape[0]
    blocks = jnp.repeat(jnp.repeat(frag_pairs, RANGE, axis=0), RANGE, axis=1).astype(jnp.float32)
    row_ids = jnp.arange(number, dtype=jnp.int32)[:, None]
    col_ids = jnp.arange(number, dtype=jnp.int32)[None, :]
    below_diag = (row_ids <= col_ids).astype(jnp.float32)
    keeper = (row_ids == col_ids).astype(jnp.float32)
    return frag_gain * blocks * below_diag - keeper * frag_rate[None, :]


def stacked(matrix):
    high = lax.reduce_precision(matrix, 8, 7)
    return jnp.concatenate([high, high, matrix - high], axis=0).astype(jnp.bfloat16)


def split(value):
    high = value.astype(jnp.bfloat16)
    return high, (value - high.astype(jnp.float32)).astype(jnp.bfloat16)


def product(value, table_ref, axis=1):
    high, low = split(value)
    return lax.dot_general(
        jnp.concatenate([high, low, high], axis=axis),
        table_ref[...],
        (((axis,), (0,)), ((), ())),
        preferred_element_type=jnp.float32,
    )


def stencil(slab, index, center, lower, upper, side, start, size):
    rows = pl.ds(start, size)
    return (
        center * slab[(*index(0), rows)]
        + lower * slab[(*index(0), pl.ds(start - 1, size))]
        + upper * slab[(*index(0), pl.ds(start + 1, size))]
        + side * (slab[(*index(-1), rows)] + slab[(*index(1), rows)])
    )


def batches(low, high):
    return [range(i, min(i + BATCH, high)) for i in range(low, high, BATCH)]


def edge_kernel(azimuth, radial, cot_ref, den_ref, sides_ref, first_ref, last_ref):
    def put(row, cot, den):
        wide = jnp.concatenate([cot, den], axis=0).T
        first_ref[row] = wide[:2]
        last_ref[row] = wide[radial - 2 :]

    for row, k in ((0, 0), (1, 1), (azimuth + 2, 2), (azimuth + 3, 3)):
        both = sides_ref[pl.ds(k, 2 * RANGE, stride=4), :]
        put(row, both[:RANGE], both[RANGE:])

    @pl.loop(0, azimuth // BATCH)
    def _(b):
        for k in range(BATCH):
            a = b * BATCH + k
            put(
                a + 2,
                cot_ref[pl.ds(a, RANGE, stride=azimuth), :],
                den_ref[pl.ds(a, RANGE, stride=azimuth), :],
            )


def forward_kernel(azimuth, radial, cuts, *refs):
    own_ref, next_ref, own_az_ref, next_az_ref, strip_ref, gate_ref, slope_ref = refs[:7]
    center_ref, lower_ref, upper_ref, side_ref, table_ref = refs[7:12]
    moved_refs, second_refs = refs[12 : 12 + len(cuts) - 1], refs[12 + len(cuts) - 1 : -2]
    slab, mixed = refs[-2:]
    inner = pl.ds(EDGE, radial)
    wide = radial + 16
    outer = pl.ds(8, wide)

    def place(row, source, other, start, stride):
        bins = jnp.concatenate(
            [source[pl.ds(start, RANGE, stride=stride), :], other[pl.ds(start, RANGE, stride=stride), :]], axis=0
        )
        slab[row, inner, :] = bins.T
        tile = strip_ref[row]
        slab[row, pl.ds(EDGE - 8, 8), :] = tile
        slab[row, pl.ds(EDGE + radial, 8), :] = tile

    for row, k in ((0, 0), (1, 1), (azimuth + 2, 2), (azimuth + 3, 3)):
        place(row, own_az_ref, next_az_ref, k, 4)

    @pl.loop(0, azimuth // BATCH)
    def _(b):
        for k in range(BATCH):
            place(b * BATCH + k + 2, own_ref, next_ref, b * BATCH + k, azimuth)

    def move(rows):
        parts = []
        for a in rows:
            moved = stencil(
                slab,
                lambda d: (a + d,),
                center_ref[1, outer, :],
                lower_ref[1, outer, :],
                upper_ref[1, outer, :],
                side_ref[1:2, :],
                8,
                wide,
            )
            parts.append(jnp.concatenate([moved, gate_ref[a, outer, :] * moved], axis=1))
        result = product(jnp.concatenate(parts, axis=0), table_ref)
        for k, a in enumerate(rows):
            mixed[a, 0, outer, :] = result[k * wide : (k + 1) * wide, :LANES]
            mixed[a, 1, outer, :] = result[k * wide : (k + 1) * wide, LANES:]
        return [part[8 : 8 + radial, :LANES] for part in parts]

    move([1, azimuth + 2])

    for g, (low, high) in enumerate(zip(cuts, cuts[1:])):

        @pl.loop(0, (high - low) // BATCH)
        def _(b):
            rows = [low + b * BATCH + k for k in range(BATCH)]
            for a, moved in zip(rows, move([a + 2 for a in rows])):
                moved_refs[g][a - low] = slope_ref[a] * moved

    for g, (low, high) in enumerate(zip(cuts, cuts[1:])):

        @pl.loop(low, high)
        def _(a):
            for t in range(2):
                second = stencil(
                    mixed,
                    lambda d: (a + 2 + d, t),
                    center_ref[t, inner, :],
                    lower_ref[t, inner, :],
                    upper_ref[t, inner, :],
                    side_ref[t : t + 1, :],
                    EDGE,
                    radial,
                )
                second_refs[g][a - low, t] = slope_ref[a] * second


def adjoint_kernel(azimuth, radial, low_row, high_row, *refs):
    first, last = low_row == 0, high_row == azimuth + 4
    refs = list(refs)

    def take(number):
        taken = refs[:number]
        del refs[:number]
        return taken

    slots = take(4)
    sides = take(4) if first or last else None
    strip_ref, gate_ref, second_ref, moved_ref = take(4)
    center_ref, lower_ref, upper_ref, side_ref = take(4)
    table1_ref, table2_ref = take(2)
    carry_second, carry_first, carry_sum, moved_before = (None, None, None, None) if first else take(4)
    own_out, next_out, sum_out = take(3)
    keep_second, keep_first = (None, None) if last else take(2)
    second, initial = take(2)

    inner = pl.ds(EDGE, radial)
    wide = radial + 16
    outer = pl.ds(8, wide)
    base = low_row if first else low_row - 2
    first_low, first_high = (1 if first else low_row - 1), high_row - 1
    first_base = first_low if first else first_low - 2
    out_low, out_high = first_base + 1, first_high - 1
    own_low, own_high = max(low_row, 2), min(high_row, azimuth + 2)
    gate_low = max(low_row - 1, 0)

    if not first:
        second[pl.ds(0, 2)] = carry_second[...]
        initial[pl.ds(0, 2)] = carry_first[...]

    rows = high_row - low_row
    strips = product(strip_ref[...].reshape(rows * 8, 4 * RANGE), table1_ref)
    for i in range(rows):
        piece = strips[i * 8 : i * 8 + 8]
        for start in (EDGE - 8, EDGE + radial):
            gate = gate_ref[low_row + i - gate_low, pl.ds(start, 8), :]
            for t in range(2):
                second[low_row + i - base, t, pl.ds(start, 8), :] = (
                    piece[:, t * LANES : (t + 1) * LANES] + gate * piece[:, (t + 2) * LANES : (t + 3) * LANES]
                )

    def bins_of(row):
        if row < 2 or row >= azimuth + 2:
            sources, start, stride = sides, (row if row < 2 else row - azimuth), 4
        else:
            sources, start, stride = slots, row - own_low, own_high - own_low
        return jnp.concatenate([source[pl.ds(start, RANGE, stride=stride), :] for source in sources], axis=0)

    total = jnp.zeros((radial, LANES), jnp.float32) if first else carry_sum[...]
    for group in batches(low_row, high_row):
        result = product(jnp.concatenate([bins_of(row) for row in group], axis=1), table1_ref, 0)
        for k, row in enumerate(group):
            part = result[k * radial : (k + 1) * radial]
            gate = gate_ref[row - gate_low, inner, :]
            for t in range(2):
                frag = part[:, (t + 2) * LANES : (t + 3) * LANES]
                second[row - base, t, inner, :] = part[:, t * LANES : (t + 1) * LANES] + gate * frag
                if own_low <= row < own_high:
                    total += second_ref[row - own_low, t] * frag

    for group in batches(first_low, first_high):
        parts = []
        for row in group:
            halves = [
                stencil(
                    second,
                    lambda d: (row - base + d, t),
                    center_ref[t, outer, :],
                    lower_ref[t, outer, :],
                    upper_ref[t, outer, :],
                    side_ref[t : t + 1, :],
                    8,
                    wide,
                )
                for t in range(2)
            ]
            parts.append(jnp.concatenate(halves, axis=1))
        result = product(jnp.concatenate(parts, axis=0), table2_ref)
        for k, row in enumerate(group):
            part = result[k * wide : (k + 1) * wide]
            frag = part[:, LANES:]
            initial[row - first_base, outer, :] = part[:, :LANES] + gate_ref[row - gate_low, outer, :] * frag
            if own_low <= row < own_high:
                total += moved_ref[row - own_low] * frag[8 : 8 + radial]
            elif 2 <= row < own_low:
                total += moved_before[0] * frag[8 : 8 + radial]
    sum_out[...] = total

    for row in range(out_low, out_high):
        result = stencil(
            initial,
            lambda d: (row - first_base + d,),
            center_ref[1, inner, :],
            lower_ref[1, inner, :],
            upper_ref[1, inner, :],
            side_ref[1:2, :],
            EDGE,
            radial,
        ).T
        own_out[row - out_low] = result[:RANGE]
        next_out[row - out_low] = result[RANGE:]

    if not last:
        keep_second[...] = second[pl.ds(high_row - 2 - base, 2)]
        keep_first[...] = initial[pl.ds(first_high - 2 - first_base, 2)]


def call(kernel, outs, scratch, flops, operands):
    size = sum(x.size * x.dtype.itemsize for x in operands) + sum(4 * math.prod(o) for o in outs)
    vmem = pl.BlockSpec(memory_space=pltpu.VMEM)
    return pl.pallas_call(
        kernel,
        out_shape=[jax.ShapeDtypeStruct(o, jnp.float32) for o in outs],
        in_specs=[vmem] * len(operands),
        out_specs=[vmem] * len(outs),
        scratch_shapes=[pltpu.VMEM(s, jnp.float32) for s in scratch],
        compiler_params=pltpu.CompilerParams(vmem_limit_bytes=VMEM_LIMIT),
        cost_estimate=pl.CostEstimate(flops=flops, bytes_accessed=size, transcendentals=0),
    )(*operands)


def per_device(
    density,
    cotangent,
    drift_in,
    drift_out,
    spread,
    dest_bins,
    bott_split,
    coag_rate,
    frag_pairs,
    frag_gain,
    frag_rate,
    collide_speed,
    frag_speed,
    regime,
):
    own_bins, azimuth, radial = density.shape
    place = lax.axis_index("mass")
    row_index = lax.axis_index("row")
    phis, rows = lax.axis_size("phi"), lax.axis_size("row")
    cuts = [0, azimuth // 2, 3 * azimuth // 4, azimuth]
    spans = list(zip(cuts, cuts[1:]))

    def far(x):
        return lax.ppermute(x, "mass", [(0, 2), (2, 1), (1, 0)])

    def near(x):
        return lax.ppermute(x, "mass", [(0, 1), (1, 2)])

    def ending(x):
        return lax.ppermute(x, "mass", [(3, 2)])

    def returning(x):
        return lax.ppermute(x, "mass", [(2, 3)])

    slot_ranges = [
        jnp.where(place == 2, 0, jnp.where(place == 3, 4, place + 1)),
        jnp.where((place == 1) | (place == 2), place - 1, 4),
        place,
        jnp.where(place == 2, 3, 4),
    ]

    density_next = ending(density)
    pieces = [cotangent[:, i:j] for i, j in spans]
    gathered = [[far(piece), near(piece), piece, ending(piece)] for piece in pieces]

    sigma = jax.nn.sigmoid((collide_speed - frag_speed[None, :]) / gate_width)
    flagged = regime.astype(jnp.float32)
    frag_gate = flagged * sigma
    gate_slope = -flagged * sigma * (1.0 - sigma) / gate_width
    gate_slope = gate_slope * (place < 3).astype(jnp.float32)

    def band(low, high):
        gate_rows = jnp.broadcast_to(frag_gate[None, low:high], (8, high - low, radial))
        return jnp.concatenate([cotangent[:, low:high], density[:, low:high], gate_rows], axis=0)

    upper_band, lower_band = band(azimuth - 2, azimuth), band(0, 2)
    if phis == 2:
        other = lax.ppermute(jnp.concatenate([upper_band, lower_band], axis=1), "phi", [(0, 1), (1, 0)])
    else:
        ring = [(i, (i + 1) % phis) for i in range(phis)]
        other = jnp.concatenate(
            [lax.ppermute(upper_band, "phi", ring), lax.ppermute(lower_band, "phi", [(j, i) for i, j in ring])], axis=1
        )
    sides = other[: 2 * own_bins]
    sides_cot, sides_den = sides[:own_bins], sides[own_bins:]
    gates = jnp.concatenate([other[-1, :2], frag_gate, other[-1, 2:]], axis=0)

    first_cols, last_cols = call(
        functools.partial(edge_kernel, azimuth, radial),
        [(azimuth + 4, 2, LANES)] * 2,
        [],
        10**7,
        [
            cotangent.reshape(own_bins * azimuth, radial),
            density.reshape(own_bins * azimuth, radial),
            sides.reshape(2 * own_bins * 4, radial),
        ],
    )
    count = azimuth + 4

    def with_gate(cols, gate_cols):
        flat = jnp.pad(gate_cols.reshape(-1), (0, LANES - 2 * count)).reshape(1, LANES)
        return jnp.concatenate([cols.reshape(2 * count, LANES), jnp.broadcast_to(flat, (8, LANES))], axis=0)

    line = [(i, i + 1) for i in range(rows - 1)]
    left = lax.ppermute(with_gate(last_cols, gates[:, radial - 2 :]), "row", line)
    right = lax.ppermute(with_gate(first_cols, gates[:, :2]), "row", [(j, i) for i, j in line])
    left_cols, right_cols = (x[: 2 * count].reshape(count, 2, LANES) for x in (left, right))
    left_gate, right_gate = (x[2 * count, : 2 * count].reshape(count, 2) for x in (left, right))

    gap = jnp.zeros((count, EDGE - 2), jnp.float32)
    gates = jnp.concatenate([gap, left_gate, gates, right_gate, gap], axis=1)
    gate_wide = jnp.broadcast_to(gates[:, :, None], gates.shape + (LANES,))
    slope_wide = jnp.broadcast_to(gate_slope[:, :, None], gate_slope.shape + (LANES,))

    drift_in, drift_out, spread, frag_gain, other = lax.optimization_barrier(
        (drift_in, drift_out, spread, frag_gain, other)
    )

    def window(drift):
        padded = jnp.pad(drift, ((0, 0), (EDGE, EDGE)))
        wide = lax.dynamic_slice_in_dim(padded, row_index * radial, radial + 2 * EDGE, 1)
        return wide.T

    length = radial + 2 * EDGE
    drifts = jnp.concatenate([window(drift_in), window(drift_out)], axis=0)
    spreads = jnp.broadcast_to(spread[None, :], (8, own_bins))
    edges = jnp.concatenate([left_cols, right_cols], axis=1)
    edges_cot, edges_den = edges[:, :, :own_bins], edges[:, :, own_bins:]

    def packed(parts):
        return jnp.concatenate([p.reshape(-1, LANES) for p in parts], axis=0)

    def unpacked(message, parts):
        out, at = [], 0
        for p in parts:
            size = p.size // LANES
            out.append(message[at : at + size].reshape(p.shape))
            at += size
        return out

    own_parts = [edges_cot, sides_cot, drifts, spreads]
    den_parts = [edges_den, sides_den]
    message = packed(own_parts)
    *over, den_edges, den_sides = unpacked(ending(packed(own_parts + den_parts)), own_parts + den_parts)
    by_slot = [unpacked(far(message), own_parts), unpacked(near(message), own_parts), own_parts, over]

    def strip_of(edge_list):
        wide = jnp.concatenate(edge_list, axis=2)
        blank = jnp.zeros((count, 4, wide.shape[2]), jnp.float32)
        return jnp.concatenate([wide[:, 2:], blank, wide[:, :2]], axis=1)

    strip_cot = strip_of([s[0] for s in by_slot])
    strip_den = strip_of([edges_den, den_edges])
    sides_by_slot = [s[1].reshape(own_bins * 4, radial) for s in by_slot]

    def tiled(wide):
        return wide.reshape(wide.shape[0], 2, LANES).transpose(1, 0, 2)

    drift_wide = tiled(jnp.concatenate([s[2] for s in by_slot], axis=1))
    inward, outward = drift_wide[:, :length], drift_wide[:, length:]
    side = tiled(jnp.concatenate([s[3] for s in by_slot], axis=1)[:1])[:, 0]
    center = 1.0 - inward - outward - 2.0 * side[:, None, :]
    inward_next = jnp.concatenate([inward[:, 1:], inward[:, :1]], axis=1)
    outward_last = jnp.concatenate([outward[:, -1:], outward[:, :-1]], axis=1)

    def chosen(matrix, axis):
        return jnp.concatenate(
            [lax.dynamic_slice_in_dim(matrix, r * RANGE, RANGE, axis) for r in slot_ranges], axis=axis
        )

    def related(matrix):
        return chosen(chosen(jnp.pad(matrix, ((0, RANGE), (0, RANGE))), 0), 1)

    coag = related(coag_matrix(dest_bins, bott_split, coag_rate))
    frag = related(frag_matrix(frag_pairs, frag_gain, frag_rate))
    both = stacked(jnp.concatenate([coag, frag], axis=1))
    upper_half = jnp.concatenate([coag[:, 2 * RANGE :], frag[:, 2 * RANGE :]], axis=1)
    own_cols = stacked(upper_half)
    own_rows = stacked(upper_half.T)

    products = call(
        functools.partial(forward_kernel, azimuth, radial, cuts),
        [(j - i, radial, LANES) for i, j in spans] + [(j - i, 2, radial, LANES) for i, j in spans],
        [(count, length, LANES), (count, 2, length, LANES)],
        6 * (azimuth + 2) * (radial + 16) * 256 * 256,
        [
            density.reshape(own_bins * azimuth, radial),
            density_next.reshape(own_bins * azimuth, radial),
            sides_den.reshape(own_bins * 4, radial),
            den_sides.reshape(own_bins * 4, radial),
            strip_den,
            gate_wide,
            slope_wide,
            center,
            outward_last,
            inward_next,
            side,
            own_rows,
        ],
    )
    groups = len(spans)
    moved, second = products[:groups], products[groups:]

    own_outs, next_outs, carry = [], [], []
    for g in range(groups):
        first, last = g == 0, g == groups - 1
        low_row = 0 if first else cuts[g] + 2
        high_row = azimuth + 4 if last else cuts[g + 1] + 2
        new = high_row - low_row
        n_out = (azimuth + 2 if last else high_row - 2) - (2 if first else low_row - 2)
        operands = [x.reshape(-1, radial) for x in gathered[g]]
        if first or last:
            operands += sides_by_slot
        operands += [strip_cot[low_row:high_row], gate_wide[max(low_row - 1, 0) : high_row], second[g], moved[g]]
        operands += [center, inward, outward, side, both, own_cols, *carry]
        if not first:
            operands.append(moved[g - 1][-1:])
        outs = [(n_out, RANGE, radial), (n_out, RANGE, radial), (radial, LANES)]
        if not last:
            outs += [(2, 2, length, LANES), (2, length, LANES)]
        own_out, next_out, total, *kept = call(
            functools.partial(adjoint_kernel, azimuth, radial, low_row, high_row),
            outs,
            [(new + 2, 2, length, LANES), (new + 2, length, LANES)],
            6 * new * (radial + 16) * 256 * 768,
            operands,
        )
        carry = [*kept, total]
        own_outs.append(own_out)
        next_outs.append(returning(next_out))
    result = jnp.concatenate(
        [jnp.where(place == 3, there, here) for here, there in zip(own_outs, next_outs)], axis=0
    ).transpose(1, 0, 2)
    speed_gradient = jnp.sum(total, axis=1)
    size = lax.axis_size("mass")
    shares = [
        lax.ppermute(speed_gradient, "mass", [(i, (i + k) % size) for i in range(size)]) for k in range(1, size)
    ]
    shares = jnp.stack([*reversed(shares), speed_gradient] * 2)
    speed_gradient = jnp.sum(lax.dynamic_slice_in_dim(shares, size - 1 - place, size, 0), axis=0)
    step = 1
    while step < phis:
        speed_gradient += lax.ppermute(speed_gradient, "phi", [(i, i ^ step) for i in range(phis)])
        step *= 2
    return (result, speed_gradient)


def solution(mesh):
    in_specs = (
        P("mass", "phi", "row"),
        P("mass", "phi", "row"),
        P("mass", None),
        P("mass", None),
        P("mass"),
        P(),
        P(),
        P(),
        P(),
        P(),
        P(),
        P("phi", "row"),
        P("row"),
        P("phi", "row"),
    )
    out_specs = (P("mass", "phi", "row"), P("row"))
    return jax.shard_map(
        per_device, mesh=mesh, in_specs=in_specs, out_specs=out_specs, check_vma=False
    )
```

```python
import functools

import jax
import jax.numpy as jnp
from jax import lax
from jax.experimental import pallas as pl
from jax.experimental.pallas import tpu as pltpu
from jax.sharding import PartitionSpec as P

RANGE = 64
LANES = 128
EDGE = 16
gate_width = 0.5
BATCH = 4
MICRO = 3 * 10**6
VMEM_LIMIT = 56 * 2**20


def coag_matrix(dest_bins, bott_split, coag_rate):
    number = dest_bins.shape[0]
    row_ids = jnp.arange(number, dtype=jnp.int32)[:, None]
    col_ids = jnp.arange(number, dtype=jnp.int32)[None, :]
    target = dest_bins[None, :]
    lower_part = (row_ids == target).astype(jnp.float32) * (1.0 - bott_split)[None, :]
    upper_part = (row_ids == target + 1).astype(jnp.float32) * bott_split[None, :]
    keeper = (row_ids == col_ids).astype(jnp.float32)
    return (lower_part + upper_part - keeper) * coag_rate[None, :] + keeper


def frag_matrix(frag_pairs, frag_gain, frag_rate):
    number = frag_gain.shape[0]
    blocks = jnp.repeat(jnp.repeat(frag_pairs, RANGE, axis=0), RANGE, axis=1).astype(jnp.float32)
    row_ids = jnp.arange(number, dtype=jnp.int32)[:, None]
    col_ids = jnp.arange(number, dtype=jnp.int32)[None, :]
    below_diag = (row_ids <= col_ids).astype(jnp.float32)
    keeper = (row_ids == col_ids).astype(jnp.float32)
    return frag_gain * blocks * below_diag - keeper * frag_rate[None, :]


def stacked(matrix):
    high = lax.reduce_precision(matrix, 8, 7)
    return jnp.concatenate([high, high, matrix - high], axis=0).astype(jnp.bfloat16)


def split(value):
    high = value.astype(jnp.bfloat16)
    return high, (value - high.astype(jnp.float32)).astype(jnp.bfloat16)


def product(value, table_ref, axis=1):
    high, low = split(value)
    return lax.dot_general(
        jnp.concatenate([high, low, high], axis=axis),
        table_ref[...],
        (((axis,), (0,)), ((), ())),
        preferred_element_type=jnp.float32,
    )


def stencil(slab, index, center, lower, upper, side, start, size):
    rows = pl.ds(start, size)
    return (
        center * slab[(*index(0), rows)]
        + lower * slab[(*index(0), pl.ds(start - 1, size))]
        + upper * slab[(*index(0), pl.ds(start + 1, size))]
        + side * (slab[(*index(-1), rows)] + slab[(*index(1), rows)])
    )


def batches(low, high):
    return [range(i, min(i + BATCH, high)) for i in range(low, high, BATCH)]


def edge_kernel(count, radial, cot_ref, den_ref, first_ref, last_ref):
    @pl.loop(0, count // BATCH)
    def _(b):
        for k in range(BATCH):
            a = b * BATCH + k
            rows = pl.ds(a, RANGE, stride=count)
            wide = jnp.concatenate([cot_ref[rows, :], den_ref[rows, :]], axis=0).T
            first_ref[a] = wide[:2]
            last_ref[a] = wide[radial - 2 :]


def halo_starts(azimuth):
    cot_sides = 4 * (azimuth + 4)
    return cot_sides, cot_sides + 4 * RANGE, cot_sides + 8 * RANGE


def pair(left, right, half):
    lanes = slice(half * RANGE, (half + 1) * RANGE)
    return jnp.concatenate([left[:, lanes], right[:, lanes]], axis=1)


def load_shares(shares, length, center_ref, lower_ref, upper_ref, side_ref):
    for t in range(2):
        left, right = [ref[pl.ds(start, length + 8), :] for ref, start in shares[2 * t : 2 * t + 2]]
        inward = pair(left[:length], right[:length], 0)
        outward = pair(left[:length], right[:length], 1)
        side = pair(left[length:], right[length:], 0)[:1]
        lower_ref[t] = inward
        upper_ref[t] = outward
        side_ref[t : t + 1] = side
        center_ref[t] = 1.0 - inward - outward - 2.0 * side


def forward_kernel(azimuth, radial, cuts, *refs):
    own_ref, next_ref, far_ref, near_ref, share_ref, own_halo, next_halo, gate_ref, slope_ref, table_ref = refs[:10]
    refs = refs[10:]
    groups = len(cuts) - 1
    moved_refs, second_refs = refs[:groups], refs[groups : 2 * groups]
    center_ref, inward_ref, outward_ref, side_ref, slab, mixed = refs[2 * groups :]
    inner = pl.ds(EDGE, radial)
    wide = radial + 16
    outer = pl.ds(8, wide)
    length = radial + 2 * EDGE
    cot_sides, den_sides, halo_end = halo_starts(azimuth)
    first_rows = RANGE * cuts[1]
    shares = [(far_ref, first_rows), (near_ref, first_rows), (share_ref, 0), (next_halo, halo_end)]
    load_shares(shares, length, center_ref, inward_ref, outward_ref, side_ref)

    def place(row, source, other, start, stride):
        bins = jnp.concatenate(
            [source[pl.ds(start, RANGE, stride=stride), :], other[pl.ds(start, RANGE, stride=stride), :]], axis=0
        )
        slab[row, inner, :] = bins.T

    for row, k in ((0, 0), (1, 1), (azimuth + 2, 2), (azimuth + 3, 3)):
        place(row, own_halo, next_halo, den_sides + k, 4)

    @pl.loop(0, azimuth // BATCH)
    def _(b):
        for k in range(BATCH):
            place(b * BATCH + k + 2, own_ref, next_ref, b * BATCH + k, azimuth)

    for row in range(azimuth + 4):
        cells = slice(4 * row, 4 * row + 4)
        strip = pair(own_halo[cells], next_halo[cells], 1)
        slab[row, pl.ds(EDGE - 2, 2), :] = strip[:2]
        slab[row, pl.ds(EDGE + radial, 2), :] = strip[2:]

    def move(rows):
        parts = []
        for a in rows:
            moved = stencil(
                slab,
                lambda d: (a + d,),
                center_ref[1, outer, :],
                outward_ref[1, pl.ds(7, wide), :],
                inward_ref[1, pl.ds(9, wide), :],
                side_ref[1:2, :],
                8,
                wide,
            )
            parts.append(jnp.concatenate([moved, gate_ref[a, outer, :] * moved], axis=1))
        result = product(jnp.concatenate(parts, axis=0), table_ref)
        for k, a in enumerate(rows):
            mixed[a, 0, outer, :] = result[k * wide : (k + 1) * wide, :LANES]
            mixed[a, 1, outer, :] = result[k * wide : (k + 1) * wide, LANES:]
        return [part[8 : 8 + radial, :LANES] for part in parts]

    move([1, azimuth + 2])

    for g, (low, high) in enumerate(zip(cuts, cuts[1:])):

        @pl.loop(0, (high - low) // BATCH)
        def _(b):
            rows = [low + b * BATCH + k for k in range(BATCH)]
            for a, moved in zip(rows, move([a + 2 for a in rows])):
                moved_refs[g][a - low] = slope_ref[a] * moved

    for g, (low, high) in enumerate(zip(cuts, cuts[1:])):

        @pl.loop(low, high)
        def _(a):
            for t in range(2):
                second = stencil(
                    mixed,
                    lambda d: (a + 2 + d, t),
                    center_ref[t, inner, :],
                    outward_ref[t, pl.ds(EDGE - 1, radial), :],
                    inward_ref[t, pl.ds(EDGE + 1, radial), :],
                    side_ref[t : t + 1, :],
                    EDGE,
                    radial,
                )
                second_refs[g][a - low, t] = slope_ref[a] * second


def adjoint_kernel(azimuth, radial, low_row, high_row, offsets, *refs):
    first, last = low_row == 0, high_row == azimuth + 4
    refs = list(refs)

    def take(number):
        taken = refs[:number]
        del refs[:number]
        return taken

    slots = take(4)
    halos = take(4)
    center_ref, lower_ref, upper_ref, side_ref = take(4)
    gate_ref, second_ref, moved_ref = take(3)
    table1_ref, table2_ref = take(2)
    carry_second, carry_first, carry_sum, moved_before = (None, None, None, None) if first else take(4)
    own_out, next_out, sum_out = take(3)
    keep_second, keep_first = (None, None) if last else take(2)
    second, initial = refs

    inner = pl.ds(EDGE, radial)
    wide = radial + 16
    outer = pl.ds(8, wide)
    base = low_row if first else low_row - 2
    first_low, first_high = (1 if first else low_row - 1), high_row - 1
    first_base = first_low if first else first_low - 2
    out_low, out_high = first_base + 1, first_high - 1
    own_low, own_high = max(low_row, 2), min(high_row, azimuth + 2)
    gate_low = max(low_row - 1, 0)

    if not first:
        second[pl.ds(0, 2)] = carry_second[...]
        initial[pl.ds(0, 2)] = carry_first[...]

    cot_sides = halo_starts(azimuth)[0]

    cells = slice(4 * low_row, 4 * high_row)
    edges = [halo[cells] for halo in halos]
    edges = product(jnp.concatenate([pair(*edges[:2], 0), pair(*edges[2:], 0)], axis=1), table1_ref)
    for row in range(low_row, high_row):
        piece = edges[4 * (row - low_row) : 4 * (row - low_row) + 4]
        for start, k in ((EDGE - 2, 0), (EDGE + radial, 2)):
            gate = gate_ref[row - gate_low, pl.ds(start, 2), :]
            for t in range(2):
                second[row - base, t, pl.ds(start, 2), :] = (
                    piece[k : k + 2, t * LANES : (t + 1) * LANES]
                    + gate * piece[k : k + 2, (t + 2) * LANES : (t + 3) * LANES]
                )

    def bins_of(row):
        if row < 2 or row >= azimuth + 2:
            starts = [(halo, cot_sides + (row if row < 2 else row - azimuth), 4) for halo in halos]
        else:
            starts = [(slot, row - 2 - offset, stride) for slot, (offset, stride) in zip(slots, offsets)]
        return jnp.concatenate([ref[pl.ds(start, RANGE, stride=stride), :] for ref, start, stride in starts], axis=0)

    total = jnp.zeros((radial, LANES), jnp.float32) if first else carry_sum[...]
    for group in batches(low_row, high_row):
        result = product(jnp.concatenate([bins_of(row) for row in group], axis=1), table1_ref, 0)
        for k, row in enumerate(group):
            part = result[k * radial : (k + 1) * radial]
            gate = gate_ref[row - gate_low, inner, :]
            for t in range(2):
                frag = part[:, (t + 2) * LANES : (t + 3) * LANES]
                second[row - base, t, inner, :] = part[:, t * LANES : (t + 1) * LANES] + gate * frag
                if own_low <= row < own_high:
                    total += second_ref[row - own_low, t] * frag

    for group in batches(first_low, first_high):
        parts = []
        for row in group:
            halves = [
                stencil(
                    second,
                    lambda d: (row - base + d, t),
                    center_ref[t, outer, :],
                    lower_ref[t, outer, :],
                    upper_ref[t, outer, :],
                    side_ref[t : t + 1, :],
                    8,
                    wide,
                )
                for t in range(2)
            ]
            parts.append(jnp.concatenate(halves, axis=1))
        result = product(jnp.concatenate(parts, axis=0), table2_ref)
        for k, row in enumerate(group):
            part = result[k * wide : (k + 1) * wide]
            frag = part[:, LANES:]
            initial[row - first_base, outer, :] = part[:, :LANES] + gate_ref[row - gate_low, outer, :] * frag
            if own_low <= row < own_high:
                total += moved_ref[row - own_low] * frag[8 : 8 + radial]
            elif 2 <= row < own_low:
                total += moved_before[0] * frag[8 : 8 + radial]
    sum_out[...] = total

    for row in range(out_low, out_high):
        result = stencil(
            initial,
            lambda d: (row - first_base + d,),
            center_ref[1, inner, :],
            lower_ref[1, inner, :],
            upper_ref[1, inner, :],
            side_ref[1:2, :],
            EDGE,
            radial,
        ).T
        own_out[row - out_low] = result[:RANGE]
        next_out[row - out_low] = result[RANGE:]

    if not last:
        keep_second[...] = second[pl.ds(high_row - 2 - base, 2)]
        keep_first[...] = initial[pl.ds(first_high - 2 - first_base, 2)]


def call(kernel, outs, scratch, operands, micros=1):
    vmem = pl.BlockSpec(memory_space=pltpu.VMEM)
    return pl.pallas_call(
        kernel,
        out_shape=[jax.ShapeDtypeStruct(o, jnp.float32) for o in outs],
        in_specs=[vmem] * len(operands),
        out_specs=[vmem] * len(outs),
        scratch_shapes=[pltpu.VMEM(s, jnp.float32) for s in scratch],
        compiler_params=pltpu.CompilerParams(vmem_limit_bytes=VMEM_LIMIT),
        cost_estimate=pl.CostEstimate(flops=0, bytes_accessed=micros * MICRO, transcendentals=0),
    )(*operands)


def per_device(
    density,
    cotangent,
    drift_in,
    drift_out,
    spread,
    dest_bins,
    bott_split,
    coag_rate,
    frag_pairs,
    frag_gain,
    frag_rate,
    collide_speed,
    frag_speed,
    regime,
):
    own_bins, azimuth, radial = density.shape
    place = lax.axis_index("mass")
    row_index = lax.axis_index("row")
    phis, rows = lax.axis_size("phi"), lax.axis_size("row")
    cuts = [0, azimuth // 2, 3 * azimuth // 4, azimuth]
    spans = list(zip(cuts, cuts[1:]))

    def far(x):
        return lax.ppermute(x, "mass", [(0, 2), (2, 1), (1, 0)])

    def near(x):
        return lax.ppermute(x, "mass", [(0, 1), (1, 2)])

    def ending(x):
        return lax.ppermute(x, "mass", [(3, 2)])

    def returning(x):
        return lax.ppermute(x, "mass", [(2, 3)])

    slot_ranges = [
        jnp.where(place == 2, 0, jnp.where(place == 3, 4, place + 1)),
        jnp.where((place == 1) | (place == 2), place - 1, 4),
        place,
        jnp.where(place == 2, 3, 4),
    ]

    count = azimuth + 4
    length = radial + 2 * EDGE

    def flat(x):
        return x.reshape(-1, LANES)

    def window(drift):
        padded = jnp.pad(drift, ((0, 0), (EDGE, EDGE)))
        wide = lax.dynamic_slice_in_dim(padded, row_index * radial, length, 1)
        return wide.T

    spreads = jnp.broadcast_to(jnp.concatenate([spread, spread])[None, :], (8, LANES))
    shares = jnp.concatenate([jnp.concatenate([window(drift_in), window(drift_out)], axis=1), spreads], axis=0)

    density_next = ending(density)
    pieces = [cotangent[:, i:j] for i, j in spans]
    opening = jnp.concatenate([flat(pieces[0]), shares], axis=0)
    far_first, near_first = far(opening), near(opening)

    sigma = jax.nn.sigmoid((collide_speed - frag_speed[None, :]) / gate_width)
    flagged = regime.astype(jnp.float32)
    frag_gate = flagged * sigma
    gate_slope = -flagged * sigma * (1.0 - sigma) / gate_width
    gate_slope = gate_slope * (place < 3).astype(jnp.float32)

    def band(low, high):
        gate_rows = jnp.broadcast_to(frag_gate[None, low:high], (8, high - low, radial))
        return jnp.concatenate([cotangent[:, low:high], density[:, low:high], gate_rows], axis=0)

    upper_band, lower_band = band(azimuth - 2, azimuth), band(0, 2)
    if phis == 2:
        other = lax.ppermute(jnp.concatenate([upper_band, lower_band], axis=1), "phi", [(0, 1), (1, 0)])
    else:
        ring = [(i, (i + 1) % phis) for i in range(phis)]
        other = jnp.concatenate(
            [lax.ppermute(upper_band, "phi", ring), lax.ppermute(lower_band, "phi", [(j, i) for i, j in ring])], axis=1
        )
    sides = other[: 2 * own_bins]
    gates = jnp.concatenate([other[-1, :2], frag_gate, other[-1, 2:]], axis=0)

    def edge_cells(cot, den):
        number = cot.shape[1]
        return call(
            functools.partial(edge_kernel, number, radial),
            [(number, 2, LANES)] * 2,
            [],
            [flat(cot), flat(den)],
        )

    own_edges = edge_cells(cotangent, density)
    side_edges = edge_cells(sides[:own_bins], sides[own_bins:])

    def with_gate(own, side, gate_cols):
        gate_row = jnp.pad(gate_cols.reshape(-1), (0, LANES - 2 * count)).reshape(1, LANES)
        parts = [flat(side[:2]), flat(own), flat(side[2:]), jnp.broadcast_to(gate_row, (8, LANES))]
        return jnp.concatenate(parts, axis=0)

    line = [(i, i + 1) for i in range(rows - 1)]
    left = lax.ppermute(with_gate(own_edges[1], side_edges[1], gates[:, radial - 2 :]), "row", line)
    right = lax.ppermute(
        with_gate(own_edges[0], side_edges[0], gates[:, :2]), "row", [(j, i) for i, j in line]
    )
    left_cols, right_cols = (x[: 2 * count].reshape(count, 2, LANES) for x in (left, right))
    left_gate, right_gate = (x[2 * count, : 2 * count].reshape(count, 2) for x in (left, right))

    gap = jnp.zeros((count, EDGE - 2), jnp.float32)
    gates = jnp.concatenate([gap, left_gate, gates, right_gate, gap], axis=1)
    gate_wide = jnp.broadcast_to(gates[:, :, None], gates.shape + (LANES,))
    slope_wide = jnp.broadcast_to(gate_slope[:, :, None], gate_slope.shape + (LANES,))

    frag_gain, other = lax.optimization_barrier((frag_gain, other))
    edges = flat(jnp.concatenate([left_cols, right_cols], axis=1))
    halos = jnp.concatenate([edges, flat(sides)], axis=0)

    def chosen(matrix, axis):
        return jnp.concatenate(
            [lax.dynamic_slice_in_dim(matrix, r * RANGE, RANGE, axis) for r in slot_ranges], axis=axis
        )

    def related(matrix):
        return chosen(chosen(jnp.pad(matrix, ((0, RANGE), (0, RANGE))), 0), 1)

    coag = related(coag_matrix(dest_bins, bott_split, coag_rate))
    frag = related(frag_matrix(frag_pairs, frag_gain, frag_rate))
    both = stacked(jnp.concatenate([coag, frag], axis=1))
    upper_half = jnp.concatenate([coag[:, 2 * RANGE :], frag[:, 2 * RANGE :]], axis=1)
    own_cols = stacked(upper_half)
    own_rows = stacked(upper_half.T)

    halos_next = ending(jnp.concatenate([halos, shares], axis=0))
    short, pieces[0], far_first, near_first, gate_wide, slope_wide, both, own_cols, own_rows = lax.optimization_barrier(
        (halos[: halo_starts(azimuth)[1]], pieces[0], far_first, near_first, gate_wide, slope_wide, both, own_cols, own_rows)
    )
    gathered = [[far_first, near_first, pieces[0], ending(pieces[0])]]
    halo_refs = [far(short), near(short), halos, halos_next]
    late = cotangent[:, cuts[1] :]
    halos_next, late, *rest = lax.optimization_barrier((halos_next, late, *pieces[1:]))
    halo_refs[3] = halos_next
    late_next = ending(late)
    gathered += [[far(piece), near(piece), piece, late_next] for piece in rest]

    coefs = [(2, length, LANES)] * 3 + [(2, LANES)]
    products = call(
        functools.partial(forward_kernel, azimuth, radial, cuts),
        [(j - i, radial, LANES) for i, j in spans] + [(j - i, 2, radial, LANES) for i, j in spans] + coefs,
        [(count, length, LANES), (count, 2, length, LANES)],
        [
            flat(density),
            flat(density_next),
            far_first,
            near_first,
            shares,
            halos,
            halos_next,
            gate_wide,
            slope_wide,
            own_rows,
        ],
        13,
    )
    groups = len(spans)
    moved, second, coefs = products[:groups], products[groups : 2 * groups], products[2 * groups :]

    own_outs, next_outs, carry = [], [], []
    for g in range(groups):
        first, last = g == 0, g == groups - 1
        low_row = 0 if first else cuts[g] + 2
        high_row = azimuth + 4 if last else cuts[g + 1] + 2
        new = high_row - low_row
        n_out = (azimuth + 2 if last else high_row - 2) - (2 if first else low_row - 2)
        operands = [flat(x) for x in gathered[g]]
        own = (cuts[g], cuts[g + 1] - cuts[g])
        offsets = [own, own, own, own if first else (cuts[1], azimuth - cuts[1])]
        operands += [*halo_refs, *coefs, gate_wide[max(low_row - 1, 0) : high_row], second[g], moved[g]]
        operands += [both, own_cols, *carry]
        if not first:
            operands.append(moved[g - 1][-1:])
        outs = [(n_out, RANGE, radial), (n_out, RANGE, radial), (radial, LANES)]
        if not last:
            outs += [(2, 2, length, LANES), (2, length, LANES)]
        own_out, next_out, total, *kept = call(
            functools.partial(adjoint_kernel, azimuth, radial, low_row, high_row, offsets),
            outs,
            [(new + 2, 2, length, LANES), (new + 2, length, LANES)],
            operands,
            2 + new // 2,
        )
        carry = [*kept, total]
        own_outs.append(own_out)
        next_outs.append(returning(next_out))
    result = jnp.concatenate(
        [jnp.where(place == 3, there, here) for here, there in zip(own_outs, next_outs)], axis=0
    ).transpose(1, 0, 2)
    speed_gradient = jnp.sum(total, axis=1)
    size = lax.axis_size("mass")
    shares = [
        lax.ppermute(speed_gradient, "mass", [(i, (i + k) % size) for i in range(size)]) for k in range(1, size)
    ]
    shares = jnp.stack([*reversed(shares), speed_gradient] * 2)
    speed_gradient = jnp.sum(lax.dynamic_slice_in_dim(shares, size - 1 - place, size, 0), axis=0)
    step = 1
    while step < phis:
        speed_gradient += lax.ppermute(speed_gradient, "phi", [(i, i ^ step) for i in range(phis)])
        step *= 2
    return (result, speed_gradient)


def solution(mesh):
    in_specs = (
        P("mass", "phi", "row"),
        P("mass", "phi", "row"),
        P("mass", None),
        P("mass", None),
        P("mass"),
        P(),
        P(),
        P(),
        P(),
        P(),
        P(),
        P("phi", "row"),
        P("row"),
        P("phi", "row"),
    )
    out_specs = (P("mass", "phi", "row"), P("row"))
    return jax.shard_map(
        per_device, mesh=mesh, in_specs=in_specs, out_specs=out_specs, check_vma=False
    )
```

```python
import functools

import jax
import jax.numpy as jnp
from jax import lax
from jax.experimental import pallas as pl
from jax.experimental.pallas import tpu as pltpu
from jax.sharding import PartitionSpec as P

RANGE = 64
LANES = 128
EDGE = 16
gate_width = 0.5
BATCH = 4
MICRO = 3 * 10**6
VMEM_LIMIT = 56 * 2**20


def coag_matrix(dest_bins, bott_split, coag_rate):
    number = dest_bins.shape[0]
    row_ids = jnp.arange(number, dtype=jnp.int32)[:, None]
    col_ids = jnp.arange(number, dtype=jnp.int32)[None, :]
    target = dest_bins[None, :]
    lower_part = (row_ids == target).astype(jnp.float32) * (1.0 - bott_split)[None, :]
    upper_part = (row_ids == target + 1).astype(jnp.float32) * bott_split[None, :]
    keeper = (row_ids == col_ids).astype(jnp.float32)
    return (lower_part + upper_part - keeper) * coag_rate[None, :] + keeper


def frag_matrix(frag_pairs, frag_gain, frag_rate):
    number = frag_gain.shape[0]
    blocks = jnp.repeat(jnp.repeat(frag_pairs, RANGE, axis=0), RANGE, axis=1).astype(jnp.float32)
    row_ids = jnp.arange(number, dtype=jnp.int32)[:, None]
    col_ids = jnp.arange(number, dtype=jnp.int32)[None, :]
    below_diag = (row_ids <= col_ids).astype(jnp.float32)
    keeper = (row_ids == col_ids).astype(jnp.float32)
    return frag_gain * blocks * below_diag - keeper * frag_rate[None, :]


def stacked(matrix):
    high = lax.reduce_precision(matrix, 8, 7)
    return jnp.concatenate([high, high, matrix - high], axis=0).astype(jnp.bfloat16)


def split(value):
    high = value.astype(jnp.bfloat16)
    return high, (value - high.astype(jnp.float32)).astype(jnp.bfloat16)


def product(value, table_ref, axis=1):
    high, low = split(value)
    return lax.dot_general(
        jnp.concatenate([high, low, high], axis=axis),
        table_ref[...],
        (((axis,), (0,)), ((), ())),
        preferred_element_type=jnp.float32,
    )


def stencil(slab, index, center, lower, upper, side, start, size):
    rows = pl.ds(start, size)
    return (
        center * slab[(*index(0), rows)]
        + lower * slab[(*index(0), pl.ds(start - 1, size))]
        + upper * slab[(*index(0), pl.ds(start + 1, size))]
        + side * (slab[(*index(-1), rows)] + slab[(*index(1), rows)])
    )


def batches(low, high):
    return [range(i, min(i + BATCH, high)) for i in range(low, high, BATCH)]


def side_kernel(azimuth, cot_ref, den_ref, collide_ref, speed_ref, regime_ref, sides_ref, gate_ref, slope_ref):
    sigma = jax.nn.sigmoid((collide_ref[...] - speed_ref[...]) / gate_width)
    flagged = regime_ref[...].astype(jnp.float32)
    gate = flagged * sigma
    gate_ref[...] = gate
    ahead = (lax.axis_index("mass") < 3).astype(jnp.float32)
    slope = -flagged * sigma * (1.0 - sigma) / gate_width * ahead
    slope_ref[:, :azimuth] = slope.T
    for k, row in enumerate((azimuth - 2, azimuth - 1, 0, 1)):
        source, target = pl.ds(row, RANGE, stride=azimuth), pl.ds(k, RANGE, stride=4)
        sides_ref[target, :] = cot_ref[source, :]
        sides_ref[pl.ds(4 * RANGE + k, RANGE, stride=4), :] = den_ref[source, :]
        sides_ref[8 * RANGE + k : 8 * RANGE + k + 1, :] = gate[row : row + 1]
    sides_ref[8 * RANGE + 4 :, :] = jnp.zeros((4, sides_ref.shape[1]), jnp.float32)


def opening_kernel(azimuth, radial, first_rows, *refs):
    cot_ref, den_ref, in_ref, out_ref, spread_ref, opening_ref, shares_ref, first_ref, last_ref = refs

    block, blocks = lax.axis_index("row"), lax.axis_size("row")

    def window(number):
        lanes = pl.ds(pl.multiple_of(number * radial, radial), radial)
        return jnp.concatenate([in_ref[:, lanes], out_ref[:, lanes]], axis=0).T

    before = window(jnp.maximum(block - 1, 0))[radial - EDGE :] * (block > 0).astype(jnp.float32)
    after = window(jnp.minimum(block + 1, blocks - 1))[:EDGE] * (block < blocks - 1).astype(jnp.float32)
    spread = jnp.concatenate([spread_ref[...], spread_ref[...]], axis=1)
    spread = jnp.broadcast_to(spread, (8, LANES))
    shares = jnp.concatenate([before, window(block), after, spread], axis=0)
    shares_ref[...] = shares
    opening_ref[RANGE * first_rows :, :] = shares
    for b in range(RANGE):
        opening_ref[b * first_rows : (b + 1) * first_rows, :] = cot_ref[b * azimuth : b * azimuth + first_rows, :]

    @pl.loop(0, azimuth // BATCH)
    def _(b):
        for k in range(BATCH):
            a = b * BATCH + k
            rows = pl.ds(a, RANGE, stride=azimuth)
            wide = jnp.concatenate([cot_ref[rows, :], den_ref[rows, :]], axis=0).T
            first_ref[a] = wide[:2]
            last_ref[a] = wide[radial - 2 :]


def radial_kernel(azimuth, radial, sides_ref, first_ref, last_ref, gate_ref, left_ref, right_ref, table_ref):
    count = azimuth + 4
    gates = jnp.concatenate(
        [
            sides_ref[8 * RANGE : 8 * RANGE + 2, :],
            gate_ref[...],
            sides_ref[8 * RANGE + 2 : 8 * RANGE + 4, :],
            jnp.zeros((LANES - count, radial), jnp.float32),
        ],
        axis=0,
    ).T
    table_ref[...] = gates
    for out_ref, own_ref, start in ((left_ref, last_ref, radial - 2), (right_ref, first_ref, 0)):
        for k, row in ((0, 0), (1, 1), (2, azimuth + 2), (3, azimuth + 3)):
            wide = sides_ref[pl.ds(k, 2 * RANGE, stride=4), :].T
            out_ref[2 * row : 2 * row + 2, :] = wide[start : start + 2]
        out_ref[4 : 4 + 2 * azimuth, :] = own_ref[...]
        out_ref[2 * count : 2 * count + 2, :] = gates[start : start + 2]
        out_ref[2 * count + 2 :, :] = jnp.zeros((6, LANES), jnp.float32)


def halo_kernel(azimuth, radial, left_ref, right_ref, sides_ref, shares_ref, gates_ref, *refs):
    long_ref, short_ref, table_ref = refs
    count = azimuth + 4
    for k in range(2):
        for source, start in ((left_ref, k), (right_ref, 2 + k)):
            cells = source[pl.ds(k, count, stride=2), :]
            long_ref[pl.ds(start, count, stride=4), :] = cells
            short_ref[pl.ds(start, count, stride=4), :] = cells
    cot_sides, den_sides, end = halo_starts(azimuth)
    long_ref[cot_sides:end, :] = sides_ref[: end - cot_sides, :]
    short_ref[cot_sides:den_sides, :] = sides_ref[: den_sides - cot_sides, :]
    long_ref[end:, :] = shares_ref[...]
    table_ref[...] = jnp.zeros(table_ref.shape, jnp.float32)
    table_ref[EDGE - 2 : EDGE, :] = left_ref[2 * count : 2 * count + 2, :]
    table_ref[EDGE : EDGE + radial, :] = gates_ref[...]
    table_ref[EDGE + radial : EDGE + radial + 2, :] = right_ref[2 * count : 2 * count + 2, :]


def halo_starts(azimuth):
    cot_sides = 4 * (azimuth + 4)
    return cot_sides, cot_sides + 4 * RANGE, cot_sides + 8 * RANGE


def widened(ref, rows, lane):
    value = ref[rows, lane : lane + 1]
    return jnp.broadcast_to(value, (value.shape[0], LANES))


def pair(left, right, half):
    lanes = slice(half * RANGE, (half + 1) * RANGE)
    return jnp.concatenate([left[:, lanes], right[:, lanes]], axis=1)


def load_shares(shares, length, center_ref, lower_ref, upper_ref, side_ref):
    for t in range(2):
        left, right = [ref[pl.ds(start, length + 8), :] for ref, start in shares[2 * t : 2 * t + 2]]
        inward = pair(left[:length], right[:length], 0)
        outward = pair(left[:length], right[:length], 1)
        side = pair(left[length:], right[length:], 0)[:1]
        lower_ref[t] = inward
        upper_ref[t] = outward
        side_ref[t : t + 1] = side
        center_ref[t] = 1.0 - inward - outward - 2.0 * side


def forward_kernel(azimuth, radial, cuts, *refs):
    own_ref, next_ref, far_ref, near_ref, share_ref, own_halo, next_halo, gate_ref, slope_ref, table_ref = refs[:10]
    refs = refs[10:]
    groups = len(cuts) - 1
    moved_refs, second_refs = refs[:groups], refs[groups : 2 * groups]
    center_ref, inward_ref, outward_ref, side_ref, slab, mixed = refs[2 * groups :]
    inner = pl.ds(EDGE, radial)
    wide = radial + 16
    outer = pl.ds(8, wide)
    length = radial + 2 * EDGE
    cot_sides, den_sides, halo_end = halo_starts(azimuth)
    first_rows = RANGE * cuts[1]
    shares = [(far_ref, first_rows), (near_ref, first_rows), (share_ref, 0), (next_halo, halo_end)]
    load_shares(shares, length, center_ref, inward_ref, outward_ref, side_ref)

    def place(row, source, other, start, stride):
        bins = jnp.concatenate(
            [source[pl.ds(start, RANGE, stride=stride), :], other[pl.ds(start, RANGE, stride=stride), :]], axis=0
        )
        slab[row, inner, :] = bins.T

    for row, k in ((0, 0), (1, 1), (azimuth + 2, 2), (azimuth + 3, 3)):
        place(row, own_halo, next_halo, den_sides + k, 4)

    @pl.loop(0, azimuth // BATCH)
    def _(b):
        for k in range(BATCH):
            place(b * BATCH + k + 2, own_ref, next_ref, b * BATCH + k, azimuth)

    for row in range(azimuth + 4):
        cells = slice(4 * row, 4 * row + 4)
        strip = pair(own_halo[cells], next_halo[cells], 1)
        slab[row, pl.ds(EDGE - 2, 2), :] = strip[:2]
        slab[row, pl.ds(EDGE + radial, 2), :] = strip[2:]

    def move(rows):
        parts = []
        for a in rows:
            moved = stencil(
                slab,
                lambda d: (a + d,),
                center_ref[1, outer, :],
                outward_ref[1, pl.ds(7, wide), :],
                inward_ref[1, pl.ds(9, wide), :],
                side_ref[1:2, :],
                8,
                wide,
            )
            parts.append(jnp.concatenate([moved, widened(gate_ref, outer, a) * moved], axis=1))
        result = product(jnp.concatenate(parts, axis=0), table_ref)
        for k, a in enumerate(rows):
            mixed[a, 0, outer, :] = result[k * wide : (k + 1) * wide, :LANES]
            mixed[a, 1, outer, :] = result[k * wide : (k + 1) * wide, LANES:]
        return [part[8 : 8 + radial, :LANES] for part in parts]

    move([1, azimuth + 2])

    for g, (low, high) in enumerate(zip(cuts, cuts[1:])):
        for rows in batches(low, high):
            for a, moved in zip(rows, move([a + 2 for a in rows])):
                moved_refs[g][a - low] = widened(slope_ref, slice(None), a) * moved

    for g, (low, high) in enumerate(zip(cuts, cuts[1:])):
        for a in range(low, high):
            slope = widened(slope_ref, slice(None), a)
            for t in range(2):
                second = stencil(
                    mixed,
                    lambda d: (a + 2 + d, t),
                    center_ref[t, inner, :],
                    outward_ref[t, pl.ds(EDGE - 1, radial), :],
                    inward_ref[t, pl.ds(EDGE + 1, radial), :],
                    side_ref[t : t + 1, :],
                    EDGE,
                    radial,
                )
                second_refs[g][a - low, t] = slope * second


def adjoint_kernel(azimuth, radial, low_row, high_row, offsets, *refs):
    first, last = low_row == 0, high_row == azimuth + 4
    refs = list(refs)

    def take(number):
        taken = refs[:number]
        del refs[:number]
        return taken

    slots = take(4)
    halos = take(4)
    center_ref, lower_ref, upper_ref, side_ref = take(4)
    gate_ref, second_ref, moved_ref = take(3)
    table1_ref, table2_ref = take(2)
    carry_second, carry_first, carry_sum, moved_before = (None, None, None, None) if first else take(4)
    own_out, next_out, sum_out = take(3)
    keep_second, keep_first = (None, None) if last else take(2)
    second, initial = refs

    inner = pl.ds(EDGE, radial)
    wide = radial + 16
    outer = pl.ds(8, wide)
    base = low_row if first else low_row - 2
    first_low, first_high = (1 if first else low_row - 1), high_row - 1
    first_base = first_low if first else first_low - 2
    out_low, out_high = first_base + 1, first_high - 1
    own_low, own_high = max(low_row, 2), min(high_row, azimuth + 2)

    if not first:
        second[pl.ds(0, 2)] = carry_second[...]
        initial[pl.ds(0, 2)] = carry_first[...]

    cot_sides = halo_starts(azimuth)[0]

    cells = slice(4 * low_row, 4 * high_row)
    edges = [halo[cells] for halo in halos]
    edges = product(jnp.concatenate([pair(*edges[:2], 0), pair(*edges[2:], 0)], axis=1), table1_ref)
    for row in range(low_row, high_row):
        piece = edges[4 * (row - low_row) : 4 * (row - low_row) + 4]
        for start, k in ((EDGE - 2, 0), (EDGE + radial, 2)):
            gate = widened(gate_ref, pl.ds(start, 2), row)
            for t in range(2):
                second[row - base, t, pl.ds(start, 2), :] = (
                    piece[k : k + 2, t * LANES : (t + 1) * LANES]
                    + gate * piece[k : k + 2, (t + 2) * LANES : (t + 3) * LANES]
                )

    def bins_of(row):
        if row < 2 or row >= azimuth + 2:
            starts = [(halo, cot_sides + (row if row < 2 else row - azimuth), 4) for halo in halos]
        else:
            starts = [(slot, row - 2 - offset, stride) for slot, (offset, stride) in zip(slots, offsets)]
        return jnp.concatenate([ref[pl.ds(start, RANGE, stride=stride), :] for ref, start, stride in starts], axis=0)

    total = jnp.zeros((radial, LANES), jnp.float32) if first else carry_sum[...]
    for group in batches(low_row, high_row):
        result = product(jnp.concatenate([bins_of(row) for row in group], axis=1), table1_ref, 0)
        for k, row in enumerate(group):
            part = result[k * radial : (k + 1) * radial]
            gate = widened(gate_ref, inner, row)
            for t in range(2):
                frag = part[:, (t + 2) * LANES : (t + 3) * LANES]
                second[row - base, t, inner, :] = part[:, t * LANES : (t + 1) * LANES] + gate * frag
                if own_low <= row < own_high:
                    total += second_ref[row - own_low, t] * frag

    for group in batches(first_low, first_high):
        parts = []
        for row in group:
            halves = [
                stencil(
                    second,
                    lambda d: (row - base + d, t),
                    center_ref[t, outer, :],
                    lower_ref[t, outer, :],
                    upper_ref[t, outer, :],
                    side_ref[t : t + 1, :],
                    8,
                    wide,
                )
                for t in range(2)
            ]
            parts.append(jnp.concatenate(halves, axis=1))
        result = product(jnp.concatenate(parts, axis=0), table2_ref)
        for k, row in enumerate(group):
            part = result[k * wide : (k + 1) * wide]
            frag = part[:, LANES:]
            initial[row - first_base, outer, :] = part[:, :LANES] + widened(gate_ref, outer, row) * frag
            if own_low <= row < own_high:
                total += moved_ref[row - own_low] * frag[8 : 8 + radial]
            elif 2 <= row < own_low:
                total += moved_before[0] * frag[8 : 8 + radial]
    sum_out[...] = total

    for row in range(out_low, out_high):
        result = stencil(
            initial,
            lambda d: (row - first_base + d,),
            center_ref[1, inner, :],
            lower_ref[1, inner, :],
            upper_ref[1, inner, :],
            side_ref[1:2, :],
            EDGE,
            radial,
        ).T
        own_out[row - out_low] = result[:RANGE]
        next_out[row - out_low] = result[RANGE:]

    if not last:
        keep_second[...] = second[pl.ds(high_row - 2 - base, 2)]
        keep_first[...] = initial[pl.ds(first_high - 2 - first_base, 2)]


def call(kernel, outs, scratch, operands, micros=1):
    vmem = pl.BlockSpec(memory_space=pltpu.VMEM)
    return pl.pallas_call(
        kernel,
        out_shape=[jax.ShapeDtypeStruct(o, jnp.float32) for o in outs],
        in_specs=[vmem] * len(operands),
        out_specs=[vmem] * len(outs),
        scratch_shapes=[pltpu.VMEM(s, jnp.float32) for s in scratch],
        compiler_params=pltpu.CompilerParams(vmem_limit_bytes=VMEM_LIMIT),
        cost_estimate=pl.CostEstimate(flops=0, bytes_accessed=micros * MICRO, transcendentals=0),
    )(*operands)


def per_device(
    density,
    cotangent,
    drift_in,
    drift_out,
    spread,
    dest_bins,
    bott_split,
    coag_rate,
    frag_pairs,
    frag_gain,
    frag_rate,
    collide_speed,
    frag_speed,
    regime,
):
    own_bins, azimuth, radial = density.shape
    place = lax.axis_index("mass")
    phis, rows = lax.axis_size("phi"), lax.axis_size("row")
    cuts = [0, azimuth // 2, 3 * azimuth // 4, azimuth]
    spans = list(zip(cuts, cuts[1:]))

    def far(x):
        return lax.ppermute(x, "mass", [(0, 2), (2, 1), (1, 0)])

    def near(x):
        return lax.ppermute(x, "mass", [(0, 1), (1, 2)])

    def ending(x):
        return lax.ppermute(x, "mass", [(3, 2)])

    def returning(x):
        return lax.ppermute(x, "mass", [(2, 3)])

    slot_ranges = [
        jnp.where(place == 2, 0, jnp.where(place == 3, 4, place + 1)),
        jnp.where((place == 1) | (place == 2), place - 1, 4),
        place,
        jnp.where(place == 2, 3, 4),
    ]

    count = azimuth + 4
    length = radial + 2 * EDGE
    share_rows, (cot_sides, den_sides, halo_rows) = length + 8, halo_starts(azimuth)

    def flat(x):
        return x.reshape(-1, LANES)

    sides, gate, slope = call(
        functools.partial(side_kernel, azimuth),
        [(8 * own_bins + 8, LANES), (azimuth, radial), (radial, LANES)],
        [],
        [flat(cotangent), flat(density), collide_speed, frag_speed[None, :], regime],
        2,
    )
    ring = [(i, (i + 1) % phis) for i in range(phis)]
    other = lax.ppermute(sides, "phi", ring)
    if phis > 2:
        after = lax.ppermute(sides, "phi", [(j, i) for i, j in ring])
        from_last = lax.broadcasted_iota(jnp.int32, other.shape, 0) % 4 < 2
        other = jnp.where(from_last, other, after)

    spread_row, gate = lax.optimization_barrier((spread[None, :], gate))
    opening, shares, first_cells, last_cells = call(
        functools.partial(opening_kernel, azimuth, radial, cuts[1]),
        [
            (cuts[1] * own_bins + share_rows, LANES),
            (share_rows, LANES),
            (azimuth, 2, LANES),
            (azimuth, 2, LANES),
        ],
        [],
        [flat(cotangent), flat(density), drift_in, drift_out, spread_row],
        5,
    )
    pieces = [cotangent[:, i:j] for i, j in spans]

    density_next = ending(density)
    far_first, near_first = far(opening), near(opening)
    left_cells, right_cells, gates = call(
        functools.partial(radial_kernel, azimuth, radial),
        [(2 * count + 8, LANES), (2 * count + 8, LANES), (radial, LANES)],
        [],
        [other, flat(first_cells), flat(last_cells), gate],
    )
    line = [(i, i + 1) for i in range(rows - 1)]
    left = lax.ppermute(left_cells, "row", line)
    right = lax.ppermute(right_cells, "row", [(j, i) for i, j in line])
    halos, short, gates = call(
        functools.partial(halo_kernel, azimuth, radial),
        [(halo_rows + share_rows, LANES), (den_sides, LANES), (length, LANES)],
        [],
        [left, right, other, shares, gates],
    )

    frag_gain, halos = lax.optimization_barrier((frag_gain, halos))

    def chosen(matrix, axis):
        return jnp.concatenate(
            [lax.dynamic_slice_in_dim(matrix, r * RANGE, RANGE, axis) for r in slot_ranges], axis=axis
        )

    def related(matrix):
        return chosen(chosen(jnp.pad(matrix, ((0, RANGE), (0, RANGE))), 0), 1)

    coag = related(coag_matrix(dest_bins, bott_split, coag_rate))
    frag = related(frag_matrix(frag_pairs, frag_gain, frag_rate))
    both = stacked(jnp.concatenate([coag, frag], axis=1))
    upper_half = jnp.concatenate([coag[:, 2 * RANGE :], frag[:, 2 * RANGE :]], axis=1)
    own_cols = stacked(upper_half)
    own_rows = stacked(upper_half.T)

    halos_next = ending(halos)
    halo_refs = [far(short), near(short), halos, halos_next]
    halos_next, late, pieces[0], pieces[1] = lax.optimization_barrier(
        (halos_next, cotangent[:, cuts[1] :], pieces[0], pieces[1])
    )
    halo_refs[3] = halos_next
    late_next = ending(late)
    gathered = [
        [far_first, near_first, pieces[0], ending(pieces[0])],
        [far(pieces[1]), near(pieces[1]), pieces[1], late_next],
    ]

    coefs = [(2, length, LANES)] * 3 + [(2, LANES)]
    products = list(call(
        functools.partial(forward_kernel, azimuth, radial, cuts),
        [(j - i, radial, LANES) for i, j in spans] + [(j - i, 2, radial, LANES) for i, j in spans] + coefs,
        [(count, length, LANES), (count, 2, length, LANES)],
        [
            flat(density),
            flat(density_next),
            far_first,
            near_first,
            shares,
            halos,
            halos_next,
            gates,
            slope,
            own_rows,
        ],
        13,
    ))
    groups = len(spans)
    products[0], pieces[2] = lax.optimization_barrier((products[0], pieces[2]))
    gathered.append([far(pieces[2]), near(pieces[2]), pieces[2], late_next])
    moved, second, coefs = products[:groups], products[groups : 2 * groups], products[2 * groups :]

    own_outs, next_outs, carry = [], [], []
    for g in range(groups):
        first, last = g == 0, g == groups - 1
        low_row = 0 if first else cuts[g] + 2
        high_row = azimuth + 4 if last else cuts[g + 1] + 2
        new = high_row - low_row
        n_out = (azimuth + 2 if last else high_row - 2) - (2 if first else low_row - 2)
        operands = [flat(x) for x in gathered[g]]
        own = (cuts[g], cuts[g + 1] - cuts[g])
        offsets = [own, own, own, own if first else (cuts[1], azimuth - cuts[1])]
        operands += [*halo_refs, *coefs, gates, second[g], moved[g]]
        operands += [both, own_cols, *carry]
        if not first:
            operands.append(moved[g - 1][-1:])
        outs = [(n_out, RANGE, radial), (n_out, RANGE, radial), (radial, LANES)]
        if not last:
            outs += [(2, 2, length, LANES), (2, length, LANES)]
        own_out, next_out, total, *kept = call(
            functools.partial(adjoint_kernel, azimuth, radial, low_row, high_row, offsets),
            outs,
            [(new + 2, 2, length, LANES), (new + 2, length, LANES)],
            operands,
            2 + new // 2,
        )
        carry = [*kept, total]
        own_outs.append(own_out)
        next_outs.append(returning(next_out))
    speed_gradient = jnp.sum(total, axis=1)
    size = lax.axis_size("mass")
    shares = [
        lax.ppermute(speed_gradient, "mass", [(i, (i + k) % size) for i in range(size)]) for k in range(1, size)
    ]
    shares = jnp.stack([*reversed(shares), speed_gradient] * 2)
    speed_gradient = jnp.sum(lax.dynamic_slice_in_dim(shares, size - 1 - place, size, 0), axis=0)
    step = 1
    while step < phis:
        speed_gradient += lax.ppermute(speed_gradient, "phi", [(i, i ^ step) for i in range(phis)])
        step *= 2
    next_outs = lax.optimization_barrier(next_outs)
    result = jnp.concatenate(
        [jnp.where(place == 3, there, here) for here, there in zip(own_outs, next_outs)], axis=0
    ).transpose(1, 0, 2)
    return (result, speed_gradient)


def solution(mesh):
    in_specs = (
        P("mass", "phi", "row"),
        P("mass", "phi", "row"),
        P("mass", None),
        P("mass", None),
        P("mass"),
        P(),
        P(),
        P(),
        P(),
        P(),
        P(),
        P("phi", "row"),
        P("row"),
        P("phi", "row"),
    )
    out_specs = (P("mass", "phi", "row"), P("row"))
    return jax.shard_map(
        per_device, mesh=mesh, in_specs=in_specs, out_specs=out_specs, check_vma=False
    )
```

```python
import functools

import jax
import jax.numpy as jnp
from jax import lax
from jax.experimental import pallas as pl
from jax.experimental.pallas import tpu as pltpu
from jax.sharding import PartitionSpec as P

RANGE = 64
LANES = 128
EDGE = 16
gate_width = 0.5
BATCH = 4
MICRO = 3 * 10**6
VMEM_LIMIT = 56 * 2**20


def split(value):
    high = value.astype(jnp.bfloat16)
    return high, (value - high.astype(jnp.float32)).astype(jnp.bfloat16)


def product(value, table_ref, axis=1):
    high, low = split(value)
    return lax.dot_general(
        jnp.concatenate([high, low, high], axis=axis),
        table_ref[...],
        (((axis,), (0,)), ((), ())),
        preferred_element_type=jnp.float32,
    )


def stencil(slab, index, center, lower, upper, side, start, size):
    rows = pl.ds(start, size)
    return (
        center * slab[(*index(0), rows)]
        + lower * slab[(*index(0), pl.ds(start - 1, size))]
        + upper * slab[(*index(0), pl.ds(start + 1, size))]
        + side * (slab[(*index(-1), rows)] + slab[(*index(1), rows)])
    )


def batches(low, high):
    return [range(i, min(i + BATCH, high)) for i in range(low, high, BATCH)]


def side_kernel(azimuth, cot_ref, den_ref, collide_ref, speed_ref, regime_ref, sides_ref, gate_ref, slope_ref):
    sigma = jax.nn.sigmoid((collide_ref[...] - speed_ref[...]) / gate_width)
    flagged = regime_ref[...].astype(jnp.float32)
    gate = flagged * sigma
    gate_ref[...] = gate
    ahead = (lax.axis_index("mass") < 3).astype(jnp.float32)
    slope = -flagged * sigma * (1.0 - sigma) / gate_width * ahead
    slope_ref[:, :azimuth] = slope.T
    for k, row in enumerate((azimuth - 2, azimuth - 1, 0, 1)):
        source, target = pl.ds(row, RANGE, stride=azimuth), pl.ds(k, RANGE, stride=4)
        sides_ref[target, :] = cot_ref[source, :]
        sides_ref[pl.ds(4 * RANGE + k, RANGE, stride=4), :] = den_ref[source, :]
        sides_ref[8 * RANGE + k : 8 * RANGE + k + 1, :] = gate[row : row + 1]
    sides_ref[8 * RANGE + 4 :, :] = jnp.zeros((4, sides_ref.shape[1]), jnp.float32)


def opening_kernel(azimuth, radial, first_rows, *refs):
    cot_ref, den_ref, in_ref, out_ref, spread_ref, opening_ref, shares_ref, first_ref, last_ref, late_ref = refs

    block, blocks = lax.axis_index("row"), lax.axis_size("row")

    def window(number):
        lanes = pl.ds(pl.multiple_of(number * radial, radial), radial)
        return jnp.concatenate([in_ref[:, lanes], out_ref[:, lanes]], axis=0).T

    before = window(jnp.maximum(block - 1, 0))[radial - EDGE :] * (block > 0).astype(jnp.float32)
    after = window(jnp.minimum(block + 1, blocks - 1))[:EDGE] * (block < blocks - 1).astype(jnp.float32)
    spread = jnp.concatenate([spread_ref[...], spread_ref[...]], axis=1)
    spread = jnp.broadcast_to(spread, (8, LANES))
    shares = jnp.concatenate([before, window(block), after, spread], axis=0)
    shares_ref[...] = shares
    opening_ref[RANGE * first_rows :, :] = shares
    for b in range(RANGE):
        opening_ref[b * first_rows : (b + 1) * first_rows, :] = cot_ref[b * azimuth : b * azimuth + first_rows, :]
        low, high = b * (azimuth - first_rows), (b + 1) * (azimuth - first_rows)
        late_ref[low:high, :] = cot_ref[b * azimuth + first_rows : (b + 1) * azimuth, :]

    @pl.loop(0, azimuth // BATCH)
    def _(b):
        for k in range(BATCH):
            a = b * BATCH + k
            rows = pl.ds(a, RANGE, stride=azimuth)
            wide = jnp.concatenate([cot_ref[rows, :], den_ref[rows, :]], axis=0).T
            first_ref[a] = wide[:2]
            last_ref[a] = wide[radial - 2 :]


def radial_kernel(azimuth, radial, sides_ref, first_ref, last_ref, gate_ref, left_ref, right_ref, table_ref):
    count = azimuth + 4
    gates = jnp.concatenate(
        [
            sides_ref[8 * RANGE : 8 * RANGE + 2, :],
            gate_ref[...],
            sides_ref[8 * RANGE + 2 : 8 * RANGE + 4, :],
            jnp.zeros((LANES - count, radial), jnp.float32),
        ],
        axis=0,
    ).T
    table_ref[...] = gates
    for out_ref, own_ref, start in ((left_ref, last_ref, radial - 2), (right_ref, first_ref, 0)):
        for k, row in ((0, 0), (1, 1), (2, azimuth + 2), (3, azimuth + 3)):
            wide = sides_ref[pl.ds(k, 2 * RANGE, stride=4), :].T
            out_ref[2 * row : 2 * row + 2, :] = wide[start : start + 2]
        out_ref[4 : 4 + 2 * azimuth, :] = own_ref[...]
        out_ref[2 * count : 2 * count + 2, :] = gates[start : start + 2]
        out_ref[2 * count + 2 :, :] = jnp.zeros((6, LANES), jnp.float32)


def halo_kernel(azimuth, radial, left_ref, right_ref, sides_ref, shares_ref, gates_ref, *refs):
    long_ref, short_ref, table_ref = refs
    count = azimuth + 4
    for k in range(2):
        for source, start in ((left_ref, k), (right_ref, 2 + k)):
            cells = source[pl.ds(k, count, stride=2), :]
            long_ref[pl.ds(start, count, stride=4), :] = cells
            short_ref[pl.ds(start, count, stride=4), :] = cells
    strips = 4 * count
    short_ref[strips:, :] = sides_ref[: 4 * RANGE, :]
    long_ref[strips : strips + 4 * RANGE, :] = sides_ref[4 * RANGE : 8 * RANGE, :]
    long_ref[strips + 4 * RANGE :, :] = shares_ref[...]
    table_ref[...] = jnp.zeros(table_ref.shape, jnp.float32)
    table_ref[EDGE - 2 : EDGE, :] = left_ref[2 * count : 2 * count + 2, :]
    table_ref[EDGE : EDGE + radial, :] = gates_ref[...]
    table_ref[EDGE + radial : EDGE + radial + 2, :] = right_ref[2 * count : 2 * count + 2, :]


def slot_ranges():
    place = lax.axis_index("mass")
    return [
        jnp.where(place == 2, 0, jnp.where(place == 3, 4, place + 1)),
        jnp.where((place == 1) | (place == 2), place - 1, 4),
        place,
        jnp.where(place == 2, 3, 4),
    ]


def table_kernel(gain_ref, dest_ref, split_ref, coag_ref, frag_ref, pairs_ref, both_ref, cols_ref, rows_ref):
    ranges = slot_ranges()
    size = 4 * RANGE

    def ordered(value, scales=(1, 1, 1, 1)):
        parts = []
        for r, scale in zip(ranges, scales):
            part = jnp.zeros((value.shape[0], RANGE), value.dtype)
            for q in range(4):
                part = jnp.where(r == q, value[:, q * RANGE : (q + 1) * RANGE], part)
            parts.append(part * scale)
        return jnp.concatenate(parts, axis=1)

    def bin_ids(axis):
        ids = lax.broadcasted_iota(jnp.int32, (size, size), axis)
        shift = jnp.zeros((size, size), jnp.int32)
        for k, r in enumerate(ranges):
            shift = jnp.where((ids >= k * RANGE) & (ids < (k + 1) * RANGE), (r - k) * RANGE, shift)
        return ids + shift

    gains = []
    for r in ranges:
        held = jnp.minimum(r, 3)
        block = gain_ref[pl.ds(pl.multiple_of(held * RANGE, RANGE), RANGE), :]
        scales = [
            jnp.where((r < 4) & (c < 4), pairs_ref[held, jnp.minimum(c, 3)], 0).astype(jnp.float32) for c in ranges
        ]
        gains.append(ordered(block, scales))
    row_ids, col_ids = bin_ids(0), bin_ids(1)
    target = ordered(dest_ref[...])
    upper = ordered(split_ref[...])
    keeper = (row_ids == col_ids).astype(jnp.float32)
    moved = jnp.where(row_ids == target, 1.0 - upper, 0.0) + jnp.where(row_ids == target + 1, upper, 0.0)
    coag = (moved - keeper) * ordered(coag_ref[...]) + keeper
    frag = jnp.where(row_ids <= col_ids, jnp.concatenate(gains, axis=0), 0.0) - keeper * ordered(frag_ref[...])
    own = jnp.concatenate([coag[:, 2 * RANGE :], frag[:, 2 * RANGE :]], axis=1)
    for ref, table in ((both_ref, jnp.concatenate([coag, frag], axis=1)), (cols_ref, own), (rows_ref, own.T)):
        high, low = split(table)
        ref[:size] = high
        ref[size : 2 * size] = high
        ref[2 * size :] = low


def widened(ref, rows, lane):
    value = ref[rows, lane : lane + 1]
    return jnp.broadcast_to(value, (value.shape[0], LANES))


def pair(left, right, half):
    lanes = slice(half * RANGE, (half + 1) * RANGE)
    return jnp.concatenate([left[:, lanes], right[:, lanes]], axis=1)


def load_shares(shares, length, center_ref, lower_ref, upper_ref, side_ref):
    for t in range(2):
        left, right = [ref[pl.ds(start, length + 8), :] for ref, start in shares[2 * t : 2 * t + 2]]
        inward = pair(left[:length], right[:length], 0)
        outward = pair(left[:length], right[:length], 1)
        side = pair(left[length:], right[length:], 0)[:1]
        lower_ref[t] = inward
        upper_ref[t] = outward
        side_ref[t : t + 1] = side
        center_ref[t] = 1.0 - inward - outward - 2.0 * side


def forward_kernel(azimuth, radial, cuts, *refs):
    own_ref, next_ref, far_ref, near_ref, share_ref, own_halo, next_halo, gate_ref, slope_ref, table_ref = refs[:10]
    refs = refs[10:]
    groups = len(cuts) - 1
    moved_refs, second_refs = refs[:groups], refs[groups : 2 * groups]
    center_ref, inward_ref, outward_ref, side_ref, slab, mixed = refs[2 * groups :]
    inner = pl.ds(EDGE, radial)
    wide = radial + 16
    outer = pl.ds(8, wide)
    length = radial + 2 * EDGE
    strips = 4 * (azimuth + 4)
    first_rows = RANGE * cuts[1]
    shares = [(far_ref, first_rows), (near_ref, first_rows), (share_ref, 0), (next_halo, strips + 4 * RANGE)]
    load_shares(shares, length, center_ref, inward_ref, outward_ref, side_ref)

    def place(row, source, other, start, stride):
        bins = jnp.concatenate(
            [source[pl.ds(start, RANGE, stride=stride), :], other[pl.ds(start, RANGE, stride=stride), :]], axis=0
        )
        slab[row, inner, :] = bins.T

    for row, k in ((0, 0), (1, 1), (azimuth + 2, 2), (azimuth + 3, 3)):
        place(row, own_halo, next_halo, strips + k, 4)

    @pl.loop(0, azimuth // BATCH)
    def _(b):
        for k in range(BATCH):
            place(b * BATCH + k + 2, own_ref, next_ref, b * BATCH + k, azimuth)

    for row in range(azimuth + 4):
        cells = slice(4 * row, 4 * row + 4)
        strip = pair(own_halo[cells], next_halo[cells], 1)
        slab[row, pl.ds(EDGE - 2, 2), :] = strip[:2]
        slab[row, pl.ds(EDGE + radial, 2), :] = strip[2:]

    def move(rows):
        parts = []
        for a in rows:
            moved = stencil(
                slab,
                lambda d: (a + d,),
                center_ref[1, outer, :],
                outward_ref[1, pl.ds(7, wide), :],
                inward_ref[1, pl.ds(9, wide), :],
                side_ref[1:2, :],
                8,
                wide,
            )
            parts.append(jnp.concatenate([moved, widened(gate_ref, outer, a) * moved], axis=1))
        result = product(jnp.concatenate(parts, axis=0), table_ref)
        for k, a in enumerate(rows):
            mixed[a, 0, outer, :] = result[k * wide : (k + 1) * wide, :LANES]
            mixed[a, 1, outer, :] = result[k * wide : (k + 1) * wide, LANES:]
        return [part[8 : 8 + radial, :LANES] for part in parts]

    move([1, azimuth + 2])

    for g, (low, high) in enumerate(zip(cuts, cuts[1:])):
        for rows in batches(low, high):
            for a, moved in zip(rows, move([a + 2 for a in rows])):
                moved_refs[g][a - low] = widened(slope_ref, slice(None), a) * moved

    for g, (low, high) in enumerate(zip(cuts, cuts[1:])):
        for a in range(low, high):
            slope = widened(slope_ref, slice(None), a)
            for t in range(2):
                second = stencil(
                    mixed,
                    lambda d: (a + 2 + d, t),
                    center_ref[t, inner, :],
                    outward_ref[t, pl.ds(EDGE - 1, radial), :],
                    inward_ref[t, pl.ds(EDGE + 1, radial), :],
                    side_ref[t : t + 1, :],
                    EDGE,
                    radial,
                )
                second_refs[g][a - low, t] = slope * second


def adjoint_kernel(azimuth, radial, low_row, high_row, offsets, *refs):
    first, last = low_row == 0, high_row == azimuth + 4
    refs = list(refs)

    def take(number):
        taken = refs[:number]
        del refs[:number]
        return taken

    slots = take(4)
    halos = take(4)
    next_sides = take(1) if first or last else None
    center_ref, lower_ref, upper_ref, side_ref = take(4)
    gate_ref, second_ref, moved_ref = take(3)
    table1_ref, table2_ref = take(2)
    carry_second, carry_first, carry_sum, moved_before = (None, None, None, None) if first else take(4)
    own_out, next_out, sum_out = take(3)
    keep_second, keep_first = (None, None) if last else take(2)
    second, initial = refs

    inner = pl.ds(EDGE, radial)
    wide = radial + 16
    outer = pl.ds(8, wide)
    base = low_row if first else low_row - 2
    first_low, first_high = (1 if first else low_row - 1), high_row - 1
    first_base = first_low if first else first_low - 2
    out_low, out_high = first_base + 1, first_high - 1
    own_low, own_high = max(low_row, 2), min(high_row, azimuth + 2)

    if not first:
        second[pl.ds(0, 2)] = carry_second[...]
        initial[pl.ds(0, 2)] = carry_first[...]

    cells = slice(4 * low_row, 4 * high_row)
    edges = [halo[cells] for halo in halos]
    edges = product(jnp.concatenate([pair(*edges[:2], 0), pair(*edges[2:], 0)], axis=1), table1_ref)
    for row in range(low_row, high_row):
        piece = edges[4 * (row - low_row) : 4 * (row - low_row) + 4]
        for start, k in ((EDGE - 2, 0), (EDGE + radial, 2)):
            gate = widened(gate_ref, pl.ds(start, 2), row)
            for t in range(2):
                second[row - base, t, pl.ds(start, 2), :] = (
                    piece[k : k + 2, t * LANES : (t + 1) * LANES]
                    + gate * piece[k : k + 2, (t + 2) * LANES : (t + 3) * LANES]
                )

    def bins_of(row):
        if row < 2 or row >= azimuth + 2:
            k = row if row < 2 else row - azimuth
            starts = [(halo, 4 * (azimuth + 4) + k, 4) for halo in halos[:3]]
            starts.append((next_sides[0], next_sides[0].shape[0] - 4 * RANGE + k, 4))
        else:
            starts = [(slot, row - 2 - offset, stride) for slot, (offset, stride) in zip(slots, offsets)]
        return jnp.concatenate([ref[pl.ds(start, RANGE, stride=stride), :] for ref, start, stride in starts], axis=0)

    total = jnp.zeros((radial, LANES), jnp.float32) if first else carry_sum[...]
    for group in batches(low_row, high_row):
        result = product(jnp.concatenate([bins_of(row) for row in group], axis=1), table1_ref, 0)
        for k, row in enumerate(group):
            part = result[k * radial : (k + 1) * radial]
            gate = widened(gate_ref, inner, row)
            for t in range(2):
                frag = part[:, (t + 2) * LANES : (t + 3) * LANES]
                second[row - base, t, inner, :] = part[:, t * LANES : (t + 1) * LANES] + gate * frag
                if own_low <= row < own_high:
                    total += second_ref[row - own_low, t] * frag

    for group in batches(first_low, first_high):
        parts = []
        for row in group:
            halves = [
                stencil(
                    second,
                    lambda d: (row - base + d, t),
                    center_ref[t, outer, :],
                    lower_ref[t, outer, :],
                    upper_ref[t, outer, :],
                    side_ref[t : t + 1, :],
                    8,
                    wide,
                )
                for t in range(2)
            ]
            parts.append(jnp.concatenate(halves, axis=1))
        result = product(jnp.concatenate(parts, axis=0), table2_ref)
        for k, row in enumerate(group):
            part = result[k * wide : (k + 1) * wide]
            frag = part[:, LANES:]
            initial[row - first_base, outer, :] = part[:, :LANES] + widened(gate_ref, outer, row) * frag
            if own_low <= row < own_high:
                total += moved_ref[row - own_low] * frag[8 : 8 + radial]
            elif 2 <= row < own_low:
                total += moved_before[0] * frag[8 : 8 + radial]
    sum_out[...] = total

    for row in range(out_low, out_high):
        result = stencil(
            initial,
            lambda d: (row - first_base + d,),
            center_ref[1, inner, :],
            lower_ref[1, inner, :],
            upper_ref[1, inner, :],
            side_ref[1:2, :],
            EDGE,
            radial,
        ).T
        own_out[row - out_low] = result[:RANGE]
        next_out[row - out_low] = result[RANGE:]

    if not last:
        keep_second[...] = second[pl.ds(high_row - 2 - base, 2)]
        keep_first[...] = initial[pl.ds(first_high - 2 - first_base, 2)]


def call(kernel, outs, scratch, operands, micros=1):
    vmem = pl.BlockSpec(memory_space=pltpu.VMEM)
    return pl.pallas_call(
        kernel,
        out_shape=[jax.ShapeDtypeStruct(o, jnp.float32) for o in outs],
        in_specs=[vmem] * len(operands),
        out_specs=[vmem] * len(outs),
        scratch_shapes=[pltpu.VMEM(s, jnp.float32) for s in scratch],
        compiler_params=pltpu.CompilerParams(vmem_limit_bytes=VMEM_LIMIT),
        cost_estimate=pl.CostEstimate(flops=0, bytes_accessed=micros * MICRO, transcendentals=0),
    )(*operands)


def per_device(
    density,
    cotangent,
    drift_in,
    drift_out,
    spread,
    dest_bins,
    bott_split,
    coag_rate,
    frag_pairs,
    frag_gain,
    frag_rate,
    collide_speed,
    frag_speed,
    regime,
):
    own_bins, azimuth, radial = density.shape
    place = lax.axis_index("mass")
    phis, rows = lax.axis_size("phi"), lax.axis_size("row")
    cuts = [0, azimuth // 2, 3 * azimuth // 4, azimuth]
    spans = list(zip(cuts, cuts[1:]))

    def far(x):
        return lax.ppermute(x, "mass", [(0, 2), (2, 1), (1, 0)])

    def near(x):
        return lax.ppermute(x, "mass", [(0, 1), (1, 2)])

    def ending(x):
        return lax.ppermute(x, "mass", [(3, 2)])

    def returning(x):
        return lax.ppermute(x, "mass", [(2, 3)])

    count = azimuth + 4
    length = radial + 2 * EDGE
    share_rows, strip_rows = length + 8, 4 * count

    def flat(x):
        return x.reshape(-1, LANES)

    sides, gate, slope = call(
        functools.partial(side_kernel, azimuth),
        [(8 * own_bins + 8, LANES), (azimuth, radial), (radial, LANES)],
        [],
        [flat(cotangent), flat(density), collide_speed, frag_speed[None, :], regime],
        2,
    )
    ring = [(i, (i + 1) % phis) for i in range(phis)]
    other = lax.ppermute(sides, "phi", ring)
    if phis > 2:
        after = lax.ppermute(sides, "phi", [(j, i) for i, j in ring])
        from_last = lax.broadcasted_iota(jnp.int32, other.shape, 0) % 4 < 2
        other = jnp.where(from_last, other, after)

    spread_row, gate = lax.optimization_barrier((spread[None, :], gate))
    opening, shares, first_cells, last_cells, late = call(
        functools.partial(opening_kernel, azimuth, radial, cuts[1]),
        [
            (cuts[1] * own_bins + share_rows, LANES),
            (share_rows, LANES),
            (azimuth, 2, LANES),
            (azimuth, 2, LANES),
            (own_bins * (azimuth - cuts[1]), radial),
        ],
        [],
        [flat(cotangent), flat(density), drift_in, drift_out, spread_row],
        5,
    )

    density_next = ending(density)
    far_first, near_first = far(opening), near(opening)
    left_cells, right_cells, gates = call(
        functools.partial(radial_kernel, azimuth, radial),
        [(2 * count + 8, LANES), (2 * count + 8, LANES), (radial, LANES)],
        [],
        [other, flat(first_cells), flat(last_cells), gate],
    )
    line = [(i, i + 1) for i in range(rows - 1)]
    left = lax.ppermute(left_cells, "row", line)
    right = lax.ppermute(right_cells, "row", [(j, i) for i, j in line])
    gates, density_next = lax.optimization_barrier((gates, density_next))
    long, short, gates = call(
        functools.partial(halo_kernel, azimuth, radial),
        [(strip_rows + 4 * own_bins + share_rows, LANES), (strip_rows + 4 * own_bins, LANES), (length, LANES)],
        [],
        [left, right, other, shares, gates],
    )

    frag_gain, long = lax.optimization_barrier((frag_gain, long))
    vmem = pl.BlockSpec(memory_space=pltpu.VMEM)
    total_bins = frag_gain.shape[0]
    both, own_cols, own_rows = pl.pallas_call(
        table_kernel,
        out_shape=[jax.ShapeDtypeStruct((3 * total_bins, n * total_bins), jnp.bfloat16) for n in (2, 1, 1)],
        in_specs=[vmem] * 5 + [pl.BlockSpec(memory_space=pltpu.SMEM)],
        out_specs=[vmem] * 3,
        compiler_params=pltpu.CompilerParams(vmem_limit_bytes=VMEM_LIMIT),
        cost_estimate=pl.CostEstimate(flops=0, bytes_accessed=3 * MICRO, transcendentals=0),
    )(
        frag_gain,
        dest_bins[None, :],
        bott_split[None, :],
        coag_rate[None, :],
        frag_rate[None, :],
        frag_pairs,
    )

    long_next = ending(long)
    first_next = jnp.concatenate([opening[: own_bins * cuts[1]], other[: 4 * own_bins]], axis=0)
    short, first_next, late, far_first, near_first, both = lax.optimization_barrier(
        (short, first_next, late, far_first, near_first, both)
    )
    halo_refs = [far(short), near(short), short, long_next]
    first_next = ending(first_next)
    far_late, near_late = far(late), near(late)

    coefs = [(2, length, LANES)] * 3 + [(2, LANES)]
    products = list(call(
        functools.partial(forward_kernel, azimuth, radial, cuts),
        [(j - i, radial, LANES) for i, j in spans] + [(j - i, 2, radial, LANES) for i, j in spans] + coefs,
        [(count, length, LANES), (count, 2, length, LANES)],
        [
            flat(density),
            flat(density_next),
            far_first,
            near_first,
            shares,
            long,
            long_next,
            gates,
            slope,
            own_rows,
        ],
        13,
    ))
    groups = len(spans)
    products[0], halo_refs[0], halo_refs[1], late = lax.optimization_barrier(
        (products[0], halo_refs[0], halo_refs[1], late)
    )
    gathered = [[far_first, near_first, opening, first_next], [far_late, near_late, late, ending(late)]]
    moved, second, coefs = products[:groups], products[groups : 2 * groups], products[2 * groups :]

    own_outs, next_outs, carry = [], [], []
    for g in range(groups):
        first, last = g == 0, g == groups - 1
        low_row = 0 if first else cuts[g] + 2
        high_row = azimuth + 4 if last else cuts[g + 1] + 2
        new = high_row - low_row
        n_out = (azimuth + 2 if last else high_row - 2) - (2 if first else low_row - 2)
        operands = [*gathered[min(g, 1)]]
        offsets = [(cuts[0], cuts[1]) if first else (cuts[1], azimuth - cuts[1])] * 4
        operands += halo_refs + ([first_next] if first or last else [])
        operands += [*coefs, gates, second[g], moved[g]]
        operands += [both, own_cols, *carry]
        if not first:
            operands.append(moved[g - 1][-1:])
        outs = [(n_out, RANGE, radial), (n_out, RANGE, radial), (radial, LANES)]
        if not last:
            outs += [(2, 2, length, LANES), (2, length, LANES)]
        own_out, next_out, total, *kept = call(
            functools.partial(adjoint_kernel, azimuth, radial, low_row, high_row, offsets),
            outs,
            [(new + 2, 2, length, LANES), (new + 2, length, LANES)],
            operands,
            2 + new // 2,
        )
        carry = [*kept, total]
        own_outs.append(own_out)
        next_outs.append(returning(next_out))
    speed_gradient = jnp.sum(total, axis=1)
    size = lax.axis_size("mass")
    shares = [
        lax.ppermute(speed_gradient, "mass", [(i, (i + k) % size) for i in range(size)]) for k in range(1, size)
    ]
    shares = jnp.stack([*reversed(shares), speed_gradient] * 2)
    speed_gradient = jnp.sum(lax.dynamic_slice_in_dim(shares, size - 1 - place, size, 0), axis=0)
    step = 1
    while step < phis:
        speed_gradient += lax.ppermute(speed_gradient, "phi", [(i, i ^ step) for i in range(phis)])
        step *= 2
    next_outs = lax.optimization_barrier(next_outs)
    result = jnp.concatenate(
        [jnp.where(place == 3, there, here) for here, there in zip(own_outs, next_outs)], axis=0
    ).transpose(1, 0, 2)
    return (result, speed_gradient)


def solution(mesh):
    in_specs = (
        P("mass", "phi", "row"),
        P("mass", "phi", "row"),
        P("mass", None),
        P("mass", None),
        P("mass"),
        P(),
        P(),
        P(),
        P(),
        P(),
        P(),
        P("phi", "row"),
        P("row"),
        P("phi", "row"),
    )
    out_specs = (P("mass", "phi", "row"), P("row"))
    return jax.shard_map(
        per_device, mesh=mesh, in_specs=in_specs, out_specs=out_specs, check_vma=False
    )
```

```python
import functools

import jax
import jax.numpy as jnp
from jax import lax
from jax.experimental import pallas as pl
from jax.experimental.pallas import tpu as pltpu
from jax.sharding import PartitionSpec as P

RANGE = 64
LANES = 128
EDGE = 16
gate_width = 0.5
BATCH = 4
MICRO = 3 * 10**6
VMEM_LIMIT = 56 * 2**20


def split(value):
    high = value.astype(jnp.bfloat16)
    return high, (value - high.astype(jnp.float32)).astype(jnp.bfloat16)


def product(value, table_ref, axis=1):
    high, low = split(value)
    return lax.dot_general(
        jnp.concatenate([high, low, high], axis=axis),
        table_ref[...],
        (((axis,), (0,)), ((), ())),
        preferred_element_type=jnp.float32,
    )


def stencil(slab, index, center, lower, upper, side, start, size):
    rows = pl.ds(start, size)
    return (
        center * slab[(*index(0), rows)]
        + lower * slab[(*index(0), pl.ds(start - 1, size))]
        + upper * slab[(*index(0), pl.ds(start + 1, size))]
        + side * (slab[(*index(-1), rows)] + slab[(*index(1), rows)])
    )


def batches(low, high):
    return [range(i, min(i + BATCH, high)) for i in range(low, high, BATCH)]


def opening_kernel(azimuth, radial, first_rows, *refs):
    cot_ref, den_ref, in_ref, out_ref, spread_ref, collide_ref, speed_ref, regime_ref = refs[:8]
    sides_ref, gate_ref, slope_ref, opening_ref, shares_ref, first_ref, last_ref, late_ref = refs[8:]
    sigma = jax.nn.sigmoid((collide_ref[...] - speed_ref[...]) / gate_width)
    flagged = regime_ref[...].astype(jnp.float32)
    gate = flagged * sigma
    gate_ref[...] = gate
    ahead = (lax.axis_index("mass") < 3).astype(jnp.float32)
    slope = -flagged * sigma * (1.0 - sigma) / gate_width * ahead
    slope_ref[:, :azimuth] = slope.T
    for k, row in enumerate((azimuth - 2, azimuth - 1, 0, 1)):
        source, target = pl.ds(row, RANGE, stride=azimuth), pl.ds(k, RANGE, stride=4)
        sides_ref[target, :] = cot_ref[source, :]
        sides_ref[pl.ds(4 * RANGE + k, RANGE, stride=4), :] = den_ref[source, :]
        sides_ref[8 * RANGE + k : 8 * RANGE + k + 1, :] = gate[row : row + 1]
    sides_ref[8 * RANGE + 4 :, :] = jnp.zeros((4, radial), jnp.float32)

    block, blocks = lax.axis_index("row"), lax.axis_size("row")

    def window(number):
        lanes = pl.ds(pl.multiple_of(number * radial, radial), radial)
        return jnp.concatenate([in_ref[:, lanes], out_ref[:, lanes]], axis=0).T

    before = window(jnp.maximum(block - 1, 0))[radial - EDGE :] * (block > 0).astype(jnp.float32)
    after = window(jnp.minimum(block + 1, blocks - 1))[:EDGE] * (block < blocks - 1).astype(jnp.float32)
    spread = jnp.concatenate([spread_ref[...], spread_ref[...]], axis=1)
    spread = jnp.broadcast_to(spread, (8, LANES))
    shares = jnp.concatenate([before, window(block), after, spread], axis=0)
    shares_ref[...] = shares
    opening_ref[RANGE * first_rows :, :] = shares
    for b in range(RANGE):
        opening_ref[b * first_rows : (b + 1) * first_rows, :] = cot_ref[b * azimuth : b * azimuth + first_rows, :]
        low, high = b * (azimuth - first_rows), (b + 1) * (azimuth - first_rows)
        late_ref[low:high, :] = cot_ref[b * azimuth + first_rows : (b + 1) * azimuth, :]

    @pl.loop(0, azimuth // BATCH)
    def _(b):
        for k in range(BATCH):
            a = b * BATCH + k
            rows = pl.ds(a, RANGE, stride=azimuth)
            wide = jnp.concatenate([cot_ref[rows, :], den_ref[rows, :]], axis=0).T
            first_ref[a] = wide[:2]
            last_ref[a] = wide[radial - 2 :]


def radial_kernel(azimuth, radial, sides_ref, first_ref, last_ref, gate_ref, left_ref, right_ref, table_ref):
    count = azimuth + 4
    gates = jnp.concatenate(
        [
            sides_ref[8 * RANGE : 8 * RANGE + 2, :],
            gate_ref[...],
            sides_ref[8 * RANGE + 2 : 8 * RANGE + 4, :],
            jnp.zeros((LANES - count, radial), jnp.float32),
        ],
        axis=0,
    ).T
    table_ref[...] = gates
    for out_ref, own_ref, start in ((left_ref, last_ref, radial - 2), (right_ref, first_ref, 0)):
        for k, row in ((0, 0), (1, 1), (2, azimuth + 2), (3, azimuth + 3)):
            wide = sides_ref[pl.ds(k, 2 * RANGE, stride=4), :].T
            out_ref[2 * row : 2 * row + 2, :] = wide[start : start + 2]
        out_ref[4 : 4 + 2 * azimuth, :] = own_ref[...]
        out_ref[2 * count : 2 * count + 2, :] = gates[start : start + 2]
        out_ref[2 * count + 2 :, :] = jnp.zeros((6, LANES), jnp.float32)


def halo_kernel(azimuth, radial, left_ref, right_ref, sides_ref, shares_ref, gates_ref, *refs):
    long_ref, short_ref, table_ref = refs
    count = azimuth + 4
    for k in range(2):
        for source, start in ((left_ref, k), (right_ref, 2 + k)):
            cells = source[pl.ds(k, count, stride=2), :]
            long_ref[pl.ds(start, count, stride=4), :] = cells
            short_ref[pl.ds(start, count, stride=4), :] = cells
    strips = 4 * count
    short_ref[strips:, :] = sides_ref[: 4 * RANGE, :]
    long_ref[strips : strips + 4 * RANGE, :] = sides_ref[4 * RANGE : 8 * RANGE, :]
    long_ref[strips + 4 * RANGE :, :] = shares_ref[...]
    table_ref[...] = jnp.zeros(table_ref.shape, jnp.float32)
    table_ref[EDGE - 2 : EDGE, :] = left_ref[2 * count : 2 * count + 2, :]
    table_ref[EDGE : EDGE + radial, :] = gates_ref[...]
    table_ref[EDGE + radial : EDGE + radial + 2, :] = right_ref[2 * count : 2 * count + 2, :]


def slot_ranges():
    place = lax.axis_index("mass")
    return [
        jnp.where(place == 2, 0, jnp.where(place == 3, 4, place + 1)),
        jnp.where((place == 1) | (place == 2), place - 1, 4),
        place,
        jnp.where(place == 2, 3, 4),
    ]


def table_kernel(gain_ref, dest_ref, split_ref, coag_ref, frag_ref, pairs_ref, both_ref, cols_ref, rows_ref):
    ranges = slot_ranges()
    size = 4 * RANGE

    def ordered(value, scales=(1, 1, 1, 1)):
        parts = []
        for r, scale in zip(ranges, scales):
            part = jnp.zeros((value.shape[0], RANGE), value.dtype)
            for q in range(4):
                part = jnp.where(r == q, value[:, q * RANGE : (q + 1) * RANGE], part)
            parts.append(part * scale)
        return jnp.concatenate(parts, axis=1)

    def bin_ids(axis):
        ids = lax.broadcasted_iota(jnp.int32, (size, size), axis)
        shift = jnp.zeros((size, size), jnp.int32)
        for k, r in enumerate(ranges):
            shift = jnp.where((ids >= k * RANGE) & (ids < (k + 1) * RANGE), (r - k) * RANGE, shift)
        return ids + shift

    gains = []
    for r in ranges:
        held = jnp.minimum(r, 3)
        block = gain_ref[pl.ds(pl.multiple_of(held * RANGE, RANGE), RANGE), :]
        scales = [
            jnp.where((r < 4) & (c < 4), pairs_ref[held, jnp.minimum(c, 3)], 0).astype(jnp.float32) for c in ranges
        ]
        gains.append(ordered(block, scales))
    row_ids, col_ids = bin_ids(0), bin_ids(1)
    target = ordered(dest_ref[...])
    upper = ordered(split_ref[...])
    keeper = (row_ids == col_ids).astype(jnp.float32)
    moved = jnp.where(row_ids == target, 1.0 - upper, 0.0) + jnp.where(row_ids == target + 1, upper, 0.0)
    coag = (moved - keeper) * ordered(coag_ref[...]) + keeper
    frag = jnp.where(row_ids <= col_ids, jnp.concatenate(gains, axis=0), 0.0) - keeper * ordered(frag_ref[...])
    own = jnp.concatenate([coag[:, 2 * RANGE :], frag[:, 2 * RANGE :]], axis=1)
    for ref, table in ((both_ref, jnp.concatenate([coag, frag], axis=1)), (cols_ref, own), (rows_ref, own.T)):
        high, low = split(table)
        ref[:size] = high
        ref[size : 2 * size] = high
        ref[2 * size :] = low


def widened(ref, rows, lane):
    value = ref[rows, lane : lane + 1]
    return jnp.broadcast_to(value, (value.shape[0], LANES))


def pair(left, right, half):
    lanes = slice(half * RANGE, (half + 1) * RANGE)
    return jnp.concatenate([left[:, lanes], right[:, lanes]], axis=1)


def load_shares(shares, length, center_ref, lower_ref, upper_ref, side_ref):
    for t in range(2):
        left, right = [ref[pl.ds(start, length + 8), :] for ref, start in shares[2 * t : 2 * t + 2]]
        inward = pair(left[:length], right[:length], 0)
        outward = pair(left[:length], right[:length], 1)
        side = pair(left[length:], right[length:], 0)[:1]
        lower_ref[t] = inward
        upper_ref[t] = outward
        side_ref[t : t + 1] = side
        center_ref[t] = 1.0 - inward - outward - 2.0 * side


def forward_kernel(azimuth, radial, cuts, *refs):
    own_ref, next_ref, far_ref, near_ref, share_ref, own_halo, next_halo, gate_ref, slope_ref, table_ref = refs[:10]
    refs = refs[10:]
    groups = len(cuts) - 1
    moved_refs, second_refs = refs[:groups], refs[groups : 2 * groups]
    center_ref, inward_ref, outward_ref, side_ref, slab, mixed = refs[2 * groups :]
    inner = pl.ds(EDGE, radial)
    wide = radial + 16
    outer = pl.ds(8, wide)
    length = radial + 2 * EDGE
    strips = 4 * (azimuth + 4)
    first_rows = RANGE * cuts[1]
    shares = [(far_ref, first_rows), (near_ref, first_rows), (share_ref, 0), (next_halo, strips + 4 * RANGE)]
    load_shares(shares, length, center_ref, inward_ref, outward_ref, side_ref)

    def place(row, source, other, start, stride):
        bins = jnp.concatenate(
            [source[pl.ds(start, RANGE, stride=stride), :], other[pl.ds(start, RANGE, stride=stride), :]], axis=0
        )
        slab[row, inner, :] = bins.T

    for row, k in ((0, 0), (1, 1), (azimuth + 2, 2), (azimuth + 3, 3)):
        place(row, own_halo, next_halo, strips + k, 4)

    @pl.loop(0, azimuth // BATCH)
    def _(b):
        for k in range(BATCH):
            place(b * BATCH + k + 2, own_ref, next_ref, b * BATCH + k, azimuth)

    for row in range(azimuth + 4):
        cells = slice(4 * row, 4 * row + 4)
        strip = pair(own_halo[cells], next_halo[cells], 1)
        slab[row, pl.ds(EDGE - 2, 2), :] = strip[:2]
        slab[row, pl.ds(EDGE + radial, 2), :] = strip[2:]

    def move(rows):
        parts = []
        for a in rows:
            moved = stencil(
                slab,
                lambda d: (a + d,),
                center_ref[1, outer, :],
                outward_ref[1, pl.ds(7, wide), :],
                inward_ref[1, pl.ds(9, wide), :],
                side_ref[1:2, :],
                8,
                wide,
            )
            parts.append(jnp.concatenate([moved, widened(gate_ref, outer, a) * moved], axis=1))
        result = product(jnp.concatenate(parts, axis=0), table_ref)
        for k, a in enumerate(rows):
            mixed[a, 0, outer, :] = result[k * wide : (k + 1) * wide, :LANES]
            mixed[a, 1, outer, :] = result[k * wide : (k + 1) * wide, LANES:]
        return [part[8 : 8 + radial, :LANES] for part in parts]

    move([1, azimuth + 2])

    for g, (low, high) in enumerate(zip(cuts, cuts[1:])):
        for rows in batches(low, high):
            for a, moved in zip(rows, move([a + 2 for a in rows])):
                h, start = (g, max(low - 1, 0)) if a < high - 1 or high == azimuth else (g + 1, high - 1)
                moved_refs[h][a - start] = widened(slope_ref, slice(None), a) * moved

    for g, (low, high) in enumerate(zip(cuts, cuts[1:])):
        for a in range(low, high):
            slope = widened(slope_ref, slice(None), a)
            for t in range(2):
                second = stencil(
                    mixed,
                    lambda d: (a + 2 + d, t),
                    center_ref[t, inner, :],
                    outward_ref[t, pl.ds(EDGE - 1, radial), :],
                    inward_ref[t, pl.ds(EDGE + 1, radial), :],
                    side_ref[t : t + 1, :],
                    EDGE,
                    radial,
                )
                second_refs[g][a - low, t] = slope * second


def adjoint_kernel(azimuth, radial, low_row, high_row, offsets, *refs):
    first, last = low_row == 0, high_row == azimuth + 4
    refs = list(refs)

    def take(number):
        taken = refs[:number]
        del refs[:number]
        return taken

    slots = take(4)
    halos = take(4)
    next_sides = take(1) if first or last else None
    center_ref, lower_ref, upper_ref, side_ref = take(4)
    gate_ref, second_ref, moved_ref = take(3)
    table1_ref, table2_ref = take(2)
    carry_second, carry_first, carry_sum = (None, None, None) if first else take(3)
    own_out, next_out, sum_out = take(3)
    keep_second, keep_first = (None, None) if last else take(2)
    second, initial = refs

    inner = pl.ds(EDGE, radial)
    wide = radial + 16
    outer = pl.ds(8, wide)
    base = low_row if first else low_row - 2
    first_low, first_high = (1 if first else low_row - 1), high_row - 1
    first_base = first_low if first else first_low - 2
    out_low, out_high = first_base + 1, first_high - 1
    own_low, own_high = max(low_row, 2), min(high_row, azimuth + 2)

    if not first:
        second[pl.ds(0, 2)] = carry_second[...]
        initial[pl.ds(0, 2)] = carry_first[...]

    cells = slice(4 * low_row, 4 * high_row)
    edges = [halo[cells] for halo in halos]
    edges = product(jnp.concatenate([pair(*edges[:2], 0), pair(*edges[2:], 0)], axis=1), table1_ref)
    for row in range(low_row, high_row):
        piece = edges[4 * (row - low_row) : 4 * (row - low_row) + 4]
        for start, k in ((EDGE - 2, 0), (EDGE + radial, 2)):
            gate = widened(gate_ref, pl.ds(start, 2), row)
            for t in range(2):
                second[row - base, t, pl.ds(start, 2), :] = (
                    piece[k : k + 2, t * LANES : (t + 1) * LANES]
                    + gate * piece[k : k + 2, (t + 2) * LANES : (t + 3) * LANES]
                )

    def bins_of(row):
        if row < 2 or row >= azimuth + 2:
            k = row if row < 2 else row - azimuth
            starts = [(halo, 4 * (azimuth + 4) + k, 4) for halo in halos[:3]]
            starts.append((next_sides[0], next_sides[0].shape[0] - 4 * RANGE + k, 4))
        else:
            starts = [(slot, row - 2 - offset, stride) for slot, (offset, stride) in zip(slots, offsets)]
        return jnp.concatenate([ref[pl.ds(start, RANGE, stride=stride), :] for ref, start, stride in starts], axis=0)

    total = jnp.zeros((radial, LANES), jnp.float32) if first else carry_sum[...]
    for group in batches(low_row, high_row):
        result = product(jnp.concatenate([bins_of(row) for row in group], axis=1), table1_ref, 0)
        for k, row in enumerate(group):
            part = result[k * radial : (k + 1) * radial]
            gate = widened(gate_ref, inner, row)
            for t in range(2):
                frag = part[:, (t + 2) * LANES : (t + 3) * LANES]
                second[row - base, t, inner, :] = part[:, t * LANES : (t + 1) * LANES] + gate * frag
                if own_low <= row < own_high:
                    total += second_ref[row - own_low, t] * frag

    for group in batches(first_low, first_high):
        parts = []
        for row in group:
            halves = [
                stencil(
                    second,
                    lambda d: (row - base + d, t),
                    center_ref[t, outer, :],
                    lower_ref[t, outer, :],
                    upper_ref[t, outer, :],
                    side_ref[t : t + 1, :],
                    8,
                    wide,
                )
                for t in range(2)
            ]
            parts.append(jnp.concatenate(halves, axis=1))
        result = product(jnp.concatenate(parts, axis=0), table2_ref)
        for k, row in enumerate(group):
            part = result[k * wide : (k + 1) * wide]
            frag = part[:, LANES:]
            initial[row - first_base, outer, :] = part[:, :LANES] + widened(gate_ref, outer, row) * frag
            if 2 <= row < azimuth + 2:
                total += moved_ref[row - max(first_low, 2)] * frag[8 : 8 + radial]
    if last:
        sum_out[...] = jnp.broadcast_to(jnp.sum(total.T, axis=0, keepdims=True), sum_out.shape)
    else:
        sum_out[...] = total

    for row in range(out_low, out_high):
        result = stencil(
            initial,
            lambda d: (row - first_base + d,),
            center_ref[1, inner, :],
            lower_ref[1, inner, :],
            upper_ref[1, inner, :],
            side_ref[1:2, :],
            EDGE,
            radial,
        ).T
        own_out[row - out_low] = result[:RANGE]
        next_out[row - out_low] = result[RANGE:]

    if not last:
        keep_second[...] = second[pl.ds(high_row - 2 - base, 2)]
        keep_first[...] = initial[pl.ds(first_high - 2 - first_base, 2)]


def call(kernel, outs, scratch, operands, micros=1):
    vmem = pl.BlockSpec(memory_space=pltpu.VMEM)
    return pl.pallas_call(
        kernel,
        out_shape=[jax.ShapeDtypeStruct(o, jnp.float32) for o in outs],
        in_specs=[vmem] * len(operands),
        out_specs=[vmem] * len(outs),
        scratch_shapes=[pltpu.VMEM(s, jnp.float32) for s in scratch],
        compiler_params=pltpu.CompilerParams(vmem_limit_bytes=VMEM_LIMIT),
        cost_estimate=pl.CostEstimate(flops=0, bytes_accessed=micros * MICRO, transcendentals=0),
    )(*operands)


def per_device(
    density,
    cotangent,
    drift_in,
    drift_out,
    spread,
    dest_bins,
    bott_split,
    coag_rate,
    frag_pairs,
    frag_gain,
    frag_rate,
    collide_speed,
    frag_speed,
    regime,
):
    own_bins, azimuth, radial = density.shape
    place = lax.axis_index("mass")
    phis, rows = lax.axis_size("phi"), lax.axis_size("row")
    cuts = [0, 5 * azimuth // 8, azimuth]
    spans = list(zip(cuts, cuts[1:]))

    def far(x):
        return lax.ppermute(x, "mass", [(0, 2), (2, 1), (1, 0)])

    def near(x):
        return lax.ppermute(x, "mass", [(0, 1), (1, 2)])

    def ending(x):
        return lax.ppermute(x, "mass", [(3, 2)])

    def returning(x):
        return lax.ppermute(x, "mass", [(2, 3)])

    count = azimuth + 4
    length = radial + 2 * EDGE
    share_rows, strip_rows = length + 8, 4 * count

    def flat(x):
        return x.reshape(-1, LANES)

    sides, gate, slope, opening, shares, first_cells, last_cells, late = call(
        functools.partial(opening_kernel, azimuth, radial, cuts[1]),
        [
            (8 * own_bins + 8, LANES),
            (azimuth, radial),
            (radial, LANES),
            (cuts[1] * own_bins + share_rows, LANES),
            (share_rows, LANES),
            (azimuth, 2, LANES),
            (azimuth, 2, LANES),
            (own_bins * (azimuth - cuts[1]), radial),
        ],
        [],
        [
            flat(cotangent),
            flat(density),
            drift_in,
            drift_out,
            spread[None, :],
            collide_speed,
            frag_speed[None, :],
            regime,
        ],
    )
    ring = [(i, (i + 1) % phis) for i in range(phis)]
    other = lax.ppermute(sides, "phi", ring)
    if phis > 2:
        after = lax.ppermute(sides, "phi", [(j, i) for i, j in ring])
        from_last = lax.broadcasted_iota(jnp.int32, other.shape, 0) % 4 < 2
        other = jnp.where(from_last, other, after)

    density_next = ending(density)
    far_first, near_first = far(opening), near(opening)
    left_cells, right_cells, gates = call(
        functools.partial(radial_kernel, azimuth, radial),
        [(2 * count + 8, LANES), (2 * count + 8, LANES), (radial, LANES)],
        [],
        [other, flat(first_cells), flat(last_cells), gate],
    )
    line = [(i, i + 1) for i in range(rows - 1)]
    left = lax.ppermute(left_cells, "row", line)
    right = lax.ppermute(right_cells, "row", [(j, i) for i, j in line])
    gates, density_next = lax.optimization_barrier((gates, density_next))
    long, short, gates = call(
        functools.partial(halo_kernel, azimuth, radial),
        [(strip_rows + 4 * own_bins + share_rows, LANES), (strip_rows + 4 * own_bins, LANES), (length, LANES)],
        [],
        [left, right, other, shares, gates],
    )

    frag_gain, long = lax.optimization_barrier((frag_gain, long))
    vmem = pl.BlockSpec(memory_space=pltpu.VMEM)
    total_bins = frag_gain.shape[0]
    both, own_cols, own_rows = pl.pallas_call(
        table_kernel,
        out_shape=[jax.ShapeDtypeStruct((3 * total_bins, n * total_bins), jnp.bfloat16) for n in (2, 1, 1)],
        in_specs=[vmem] * 5 + [pl.BlockSpec(memory_space=pltpu.SMEM)],
        out_specs=[vmem] * 3,
        compiler_params=pltpu.CompilerParams(vmem_limit_bytes=VMEM_LIMIT),
        cost_estimate=pl.CostEstimate(flops=0, bytes_accessed=3 * MICRO, transcendentals=0),
    )(
        frag_gain,
        dest_bins[None, :],
        bott_split[None, :],
        coag_rate[None, :],
        frag_rate[None, :],
        frag_pairs,
    )

    long_next = ending(long)
    first_next = jnp.concatenate([opening[: own_bins * cuts[1]], other[: 4 * own_bins]], axis=0)
    halo_refs = [far(short), near(short), short, long_next]
    first_next, late, far_first, near_first, both = lax.optimization_barrier(
        (first_next, late, far_first, near_first, both)
    )
    first_next = ending(first_next)
    far_late, near_late = far(late), near(late)

    coefs = [(2, length, LANES)] * 3 + [(2, LANES)]
    products = list(call(
        functools.partial(forward_kernel, azimuth, radial, cuts),
        [(j - (j < azimuth) - max(i - 1, 0), radial, LANES) for i, j in spans]
        + [(j - i, 2, radial, LANES) for i, j in spans]
        + coefs,
        [(count, length, LANES), (count, 2, length, LANES)],
        [
            flat(density),
            flat(density_next),
            far_first,
            near_first,
            shares,
            long,
            long_next,
            gates,
            slope,
            own_rows,
        ],
        13,
    ))
    groups = len(spans)
    products[0], halo_refs[0], halo_refs[1], late = lax.optimization_barrier(
        (products[0], halo_refs[0], halo_refs[1], late)
    )
    gathered = [[far_first, near_first, opening, first_next], [far_late, near_late, late, ending(late)]]
    moved, second, coefs = products[:groups], products[groups : 2 * groups], products[2 * groups :]

    own_outs, next_outs, carry = [], [], []
    for g in range(groups):
        first, last = g == 0, g == groups - 1
        low_row = 0 if first else cuts[g] + 2
        high_row = azimuth + 4 if last else cuts[g + 1] + 2
        new = high_row - low_row
        n_out = (azimuth + 2 if last else high_row - 2) - (2 if first else low_row - 2)
        operands = [*gathered[min(g, 1)]]
        offsets = [(cuts[0], cuts[1]) if first else (cuts[1], azimuth - cuts[1])] * 4
        operands += halo_refs + ([first_next] if first or last else [])
        operands += [*coefs, gates, second[g], moved[g]]
        operands += [both, own_cols, *carry]
        outs = [(n_out, RANGE, radial), (n_out, RANGE, radial), (8, radial) if last else (radial, LANES)]
        if not last:
            outs += [(2, 2, length, LANES), (2, length, LANES)]
        own_out, next_out, total, *kept = call(
            functools.partial(adjoint_kernel, azimuth, radial, low_row, high_row, offsets),
            outs,
            [(new + 2, 2, length, LANES), (new + 2, length, LANES)],
            operands,
            2 + new // 2,
        )
        carry = [*kept, total]
        own_outs.append(own_out)
        next_outs.append(returning(next_out))
    speed_gradient = total[0]
    size = lax.axis_size("mass")
    shares = [
        lax.ppermute(speed_gradient, "mass", [(i, (i + k) % size) for i in range(size)]) for k in range(1, size)
    ]
    shares = jnp.stack([*reversed(shares), speed_gradient] * 2)
    speed_gradient = jnp.sum(lax.dynamic_slice_in_dim(shares, size - 1 - place, size, 0), axis=0)
    step = 1
    while step < phis:
        speed_gradient += lax.ppermute(speed_gradient, "phi", [(i, i ^ step) for i in range(phis)])
        step *= 2
    next_outs = lax.optimization_barrier(next_outs)
    result = jnp.concatenate(
        [jnp.where(place == 3, there, here) for here, there in zip(own_outs, next_outs)], axis=0
    ).transpose(1, 0, 2)
    return (result, speed_gradient)


def solution(mesh):
    in_specs = (
        P("mass", "phi", "row"),
        P("mass", "phi", "row"),
        P("mass", None),
        P("mass", None),
        P("mass"),
        P(),
        P(),
        P(),
        P(),
        P(),
        P(),
        P("phi", "row"),
        P("row"),
        P("phi", "row"),
    )
    out_specs = (P("mass", "phi", "row"), P("row"))
    return jax.shard_map(
        per_device, mesh=mesh, in_specs=in_specs, out_specs=out_specs, check_vma=False
    )
```

```python
import functools

import jax
import jax.numpy as jnp
from jax import lax
from jax.experimental import pallas as pl
from jax.experimental.pallas import tpu as pltpu
from jax.sharding import PartitionSpec as P

RANGE = 64
LANES = 128
EDGE = 16
gate_width = 0.5
BATCH = 4
MICRO = 3 * 10**6
VMEM_LIMIT = 56 * 2**20


def split(value):
    high = value.astype(jnp.bfloat16)
    return high, (value - high.astype(jnp.float32)).astype(jnp.bfloat16)


def product(value, table_ref, axis=1):
    high, low = split(value)
    return lax.dot_general(
        jnp.concatenate([high, low, high], axis=axis),
        table_ref[...],
        (((axis,), (0,)), ((), ())),
        preferred_element_type=jnp.float32,
    )


def stencil(slab, index, center, lower, upper, side, start, size):
    rows = pl.ds(start, size)
    return (
        center * slab[(*index(0), rows)]
        + lower * slab[(*index(0), pl.ds(start - 1, size))]
        + upper * slab[(*index(0), pl.ds(start + 1, size))]
        + side * (slab[(*index(-1), rows)] + slab[(*index(1), rows)])
    )


def batches(low, high):
    return [range(i, min(i + BATCH, high)) for i in range(low, high, BATCH)]


def opening_kernel(azimuth, radial, first_rows, *refs):
    cot_ref, den_ref, in_ref, out_ref, spread_ref, collide_ref, speed_ref, regime_ref = refs[:8]
    sides_ref, gate_ref, slope_ref, opening_ref, shares_ref, first_ref, last_ref, late_ref = refs[8:]
    sigma = jax.nn.sigmoid((collide_ref[...] - speed_ref[...]) / gate_width)
    flagged = regime_ref[...].astype(jnp.float32)
    gate = flagged * sigma
    gate_ref[...] = gate
    ahead = (lax.axis_index("mass") < 3).astype(jnp.float32)
    slope = -flagged * sigma * (1.0 - sigma) / gate_width * ahead
    slope_ref[:, :azimuth] = slope.T
    for k, row in enumerate((azimuth - 2, azimuth - 1, 0, 1)):
        source, target = pl.ds(row, RANGE, stride=azimuth), pl.ds(k, RANGE, stride=4)
        sides_ref[target, :] = cot_ref[source, :]
        sides_ref[pl.ds(4 * RANGE + k, RANGE, stride=4), :] = den_ref[source, :]
        sides_ref[8 * RANGE + k : 8 * RANGE + k + 1, :] = gate[row : row + 1]
    sides_ref[8 * RANGE + 4 :, :] = jnp.zeros((4, radial), jnp.float32)

    block, blocks = lax.axis_index("row"), lax.axis_size("row")

    def window(number):
        lanes = pl.ds(pl.multiple_of(number * radial, radial), radial)
        return jnp.concatenate([in_ref[:, lanes], out_ref[:, lanes]], axis=0).T

    before = window(jnp.maximum(block - 1, 0))[radial - EDGE :] * (block > 0).astype(jnp.float32)
    after = window(jnp.minimum(block + 1, blocks - 1))[:EDGE] * (block < blocks - 1).astype(jnp.float32)
    spread = jnp.concatenate([spread_ref[...], spread_ref[...]], axis=1)
    spread = jnp.broadcast_to(spread, (8, LANES))
    shares = jnp.concatenate([before, window(block), after, spread], axis=0)
    shares_ref[...] = shares
    opening_ref[RANGE * first_rows :, :] = shares
    for b in range(RANGE):
        opening_ref[b * first_rows : (b + 1) * first_rows, :] = cot_ref[b * azimuth : b * azimuth + first_rows, :]
        low, high = b * (azimuth - first_rows), (b + 1) * (azimuth - first_rows)
        late_ref[low:high, :] = cot_ref[b * azimuth + first_rows : (b + 1) * azimuth, :]

    @pl.loop(0, azimuth // BATCH)
    def _(b):
        for k in range(BATCH):
            a = b * BATCH + k
            rows = pl.ds(a, RANGE, stride=azimuth)
            wide = jnp.concatenate([cot_ref[rows, :], den_ref[rows, :]], axis=0).T
            first_ref[a] = wide[:2]
            last_ref[a] = wide[radial - 2 :]


def radial_kernel(azimuth, radial, sides_ref, first_ref, last_ref, gate_ref, left_ref, right_ref, table_ref):
    count = azimuth + 4
    gates = jnp.concatenate(
        [
            sides_ref[8 * RANGE : 8 * RANGE + 2, :],
            gate_ref[...],
            sides_ref[8 * RANGE + 2 : 8 * RANGE + 4, :],
            jnp.zeros((LANES - count, radial), jnp.float32),
        ],
        axis=0,
    ).T
    table_ref[...] = gates
    for out_ref, own_ref, start in ((left_ref, last_ref, radial - 2), (right_ref, first_ref, 0)):
        for k, row in ((0, 0), (1, 1), (2, azimuth + 2), (3, azimuth + 3)):
            wide = sides_ref[pl.ds(k, 2 * RANGE, stride=4), :].T
            out_ref[2 * row : 2 * row + 2, :] = wide[start : start + 2]
        out_ref[4 : 4 + 2 * azimuth, :] = own_ref[...]
        out_ref[2 * count : 2 * count + 2, :] = gates[start : start + 2]
        out_ref[2 * count + 2 :, :] = jnp.zeros((6, LANES), jnp.float32)


def halo_kernel(azimuth, radial, left_ref, right_ref, sides_ref, shares_ref, gates_ref, *refs):
    long_ref, short_ref, table_ref = refs
    count = azimuth + 4
    for k in range(2):
        for source, start in ((left_ref, k), (right_ref, 2 + k)):
            cells = source[pl.ds(k, count, stride=2), :]
            long_ref[pl.ds(start, count, stride=4), :] = cells
            short_ref[pl.ds(start, count, stride=4), :] = cells
    strips = 4 * count
    short_ref[strips:, :] = sides_ref[: 4 * RANGE, :]
    long_ref[strips : strips + 4 * RANGE, :] = sides_ref[4 * RANGE : 8 * RANGE, :]
    long_ref[strips + 4 * RANGE :, :] = shares_ref[...]
    table_ref[...] = jnp.zeros(table_ref.shape, jnp.float32)
    table_ref[EDGE - 2 : EDGE, :] = left_ref[2 * count : 2 * count + 2, :]
    table_ref[EDGE : EDGE + radial, :] = gates_ref[...]
    table_ref[EDGE + radial : EDGE + radial + 2, :] = right_ref[2 * count : 2 * count + 2, :]


def slot_ranges():
    place = lax.axis_index("mass")
    return [
        jnp.where(place == 2, 0, jnp.where(place == 3, 4, place + 1)),
        jnp.where((place == 1) | (place == 2), place - 1, 4),
        place,
        jnp.where(place == 2, 3, 4),
    ]


def table_kernel(gain_ref, dest_ref, split_ref, coag_ref, frag_ref, pairs_ref, both_ref, cols_ref, rows_ref):
    ranges = slot_ranges()
    size = 4 * RANGE

    def ordered(value, scales=(1, 1, 1, 1)):
        parts = []
        for r, scale in zip(ranges, scales):
            part = jnp.zeros((value.shape[0], RANGE), value.dtype)
            for q in range(4):
                part = jnp.where(r == q, value[:, q * RANGE : (q + 1) * RANGE], part)
            parts.append(part * scale)
        return jnp.concatenate(parts, axis=1)

    def bin_ids(axis):
        ids = lax.broadcasted_iota(jnp.int32, (size, size), axis)
        shift = jnp.zeros((size, size), jnp.int32)
        for k, r in enumerate(ranges):
            shift = jnp.where((ids >= k * RANGE) & (ids < (k + 1) * RANGE), (r - k) * RANGE, shift)
        return ids + shift

    gains = []
    for r in ranges:
        held = jnp.minimum(r, 3)
        block = gain_ref[pl.ds(pl.multiple_of(held * RANGE, RANGE), RANGE), :]
        scales = [
            jnp.where((r < 4) & (c < 4), pairs_ref[held, jnp.minimum(c, 3)], 0).astype(jnp.float32) for c in ranges
        ]
        gains.append(ordered(block, scales))
    row_ids, col_ids = bin_ids(0), bin_ids(1)
    target = ordered(dest_ref[...])
    upper = ordered(split_ref[...])
    keeper = (row_ids == col_ids).astype(jnp.float32)
    moved = jnp.where(row_ids == target, 1.0 - upper, 0.0) + jnp.where(row_ids == target + 1, upper, 0.0)
    coag = (moved - keeper) * ordered(coag_ref[...]) + keeper
    frag = jnp.where(row_ids <= col_ids, jnp.concatenate(gains, axis=0), 0.0) - keeper * ordered(frag_ref[...])
    own = jnp.concatenate([coag[:, 2 * RANGE :], frag[:, 2 * RANGE :]], axis=1)
    for ref, table in ((both_ref, jnp.concatenate([coag, frag], axis=1)), (cols_ref, own), (rows_ref, own.T)):
        high, low = split(table)
        ref[:size] = high
        ref[size : 2 * size] = high
        ref[2 * size :] = low


def widened(ref, rows, lane):
    value = ref[rows, lane : lane + 1]
    return jnp.broadcast_to(value, (value.shape[0], LANES))


def pair(left, right, half):
    lanes = slice(half * RANGE, (half + 1) * RANGE)
    return jnp.concatenate([left[:, lanes], right[:, lanes]], axis=1)


def load_shares(shares, length, center_ref, lower_ref, upper_ref, side_ref):
    for t in range(2):
        left, right = [ref[pl.ds(start, length + 8), :] for ref, start in shares[2 * t : 2 * t + 2]]
        inward = pair(left[:length], right[:length], 0)
        outward = pair(left[:length], right[:length], 1)
        side = pair(left[length:], right[length:], 0)[:1]
        lower_ref[t] = inward
        upper_ref[t] = outward
        side_ref[t : t + 1] = side
        center_ref[t] = 1.0 - inward - outward - 2.0 * side


def forward_kernel(azimuth, radial, cuts, *refs):
    own_ref, next_ref, far_ref, near_ref, share_ref, own_halo, next_halo, gate_ref, slope_ref, table_ref = refs[:10]
    refs = refs[10:]
    groups = len(cuts) - 1
    moved_refs, second_refs = refs[:groups], refs[groups : 2 * groups]
    center_ref, inward_ref, outward_ref, side_ref, slab, mixed = refs[2 * groups :]
    inner = pl.ds(EDGE, radial)
    wide = radial + 16
    outer = pl.ds(8, wide)
    length = radial + 2 * EDGE
    strips = 4 * (azimuth + 4)
    first_rows = RANGE * cuts[1]
    shares = [(far_ref, first_rows), (near_ref, first_rows), (share_ref, 0), (next_halo, strips + 4 * RANGE)]
    load_shares(shares, length, center_ref, inward_ref, outward_ref, side_ref)

    def place(row, source, other, start, stride):
        bins = jnp.concatenate(
            [source[pl.ds(start, RANGE, stride=stride), :], other[pl.ds(start, RANGE, stride=stride), :]], axis=0
        )
        slab[row, inner, :] = bins.T

    for row, k in ((0, 0), (1, 1), (azimuth + 2, 2), (azimuth + 3, 3)):
        place(row, own_halo, next_halo, strips + k, 4)

    @pl.loop(0, azimuth // BATCH)
    def _(b):
        for k in range(BATCH):
            place(b * BATCH + k + 2, own_ref, next_ref, b * BATCH + k, azimuth)

    for row in range(azimuth + 4):
        cells = slice(4 * row, 4 * row + 4)
        strip = pair(own_halo[cells], next_halo[cells], 1)
        slab[row, pl.ds(EDGE - 2, 2), :] = strip[:2]
        slab[row, pl.ds(EDGE + radial, 2), :] = strip[2:]

    def move(rows):
        parts = []
        for a in rows:
            moved = stencil(
                slab,
                lambda d: (a + d,),
                center_ref[1, outer, :],
                outward_ref[1, pl.ds(7, wide), :],
                inward_ref[1, pl.ds(9, wide), :],
                side_ref[1:2, :],
                8,
                wide,
            )
            parts.append(jnp.concatenate([moved, widened(gate_ref, outer, a) * moved], axis=1))
        result = product(jnp.concatenate(parts, axis=0), table_ref)
        for k, a in enumerate(rows):
            mixed[a, 0, outer, :] = result[k * wide : (k + 1) * wide, :LANES]
            mixed[a, 1, outer, :] = result[k * wide : (k + 1) * wide, LANES:]
        return [part[8 : 8 + radial, :LANES] for part in parts]

    move([1, azimuth + 2])

    for g, (low, high) in enumerate(zip(cuts, cuts[1:])):
        for rows in batches(low, high):
            for a, moved in zip(rows, move([a + 2 for a in rows])):
                h, start = (g, max(low - 1, 0)) if a < high - 1 or high == azimuth else (g + 1, high - 1)
                moved_refs[h][a - start] = widened(slope_ref, slice(None), a) * moved

    for g, (low, high) in enumerate(zip(cuts, cuts[1:])):
        for a in range(low, high):
            slope = widened(slope_ref, slice(None), a)
            for t in range(2):
                second = stencil(
                    mixed,
                    lambda d: (a + 2 + d, t),
                    center_ref[t, inner, :],
                    outward_ref[t, pl.ds(EDGE - 1, radial), :],
                    inward_ref[t, pl.ds(EDGE + 1, radial), :],
                    side_ref[t : t + 1, :],
                    EDGE,
                    radial,
                )
                second_refs[g][a - low, t] = slope * second


def adjoint_kernel(azimuth, radial, low_row, high_row, offsets, *refs):
    first, last = low_row == 0, high_row == azimuth + 4
    refs = list(refs)

    def take(number):
        taken = refs[:number]
        del refs[:number]
        return taken

    slots = take(4)
    halos = take(4)
    next_sides = take(1) if first or last else None
    center_ref, lower_ref, upper_ref, side_ref = take(4)
    gate_ref, second_ref, moved_ref = take(3)
    table1_ref, table2_ref = take(2)
    carry_second, carry_first, carry_sum = (None, None, None) if first else take(3)
    own_out, next_out, sum_out = take(3)
    keep_second, keep_first = (None, None) if last else take(2)
    second, initial = refs

    inner = pl.ds(EDGE, radial)
    wide = radial + 16
    outer = pl.ds(8, wide)
    base = low_row if first else low_row - 2
    first_low, first_high = (1 if first else low_row - 1), high_row - 1
    first_base = first_low if first else first_low - 2
    out_low, out_high = first_base + 1, first_high - 1
    own_low, own_high = max(low_row, 2), min(high_row, azimuth + 2)

    if not first:
        second[pl.ds(0, 2)] = carry_second[...]
        initial[pl.ds(0, 2)] = carry_first[...]

    cells = slice(4 * low_row, 4 * high_row)
    edges = [halo[cells] for halo in halos]
    edges = product(jnp.concatenate([pair(*edges[:2], 0), pair(*edges[2:], 0)], axis=1), table1_ref)
    for row in range(low_row, high_row):
        piece = edges[4 * (row - low_row) : 4 * (row - low_row) + 4]
        for start, k in ((EDGE - 2, 0), (EDGE + radial, 2)):
            gate = widened(gate_ref, pl.ds(start, 2), row)
            for t in range(2):
                second[row - base, t, pl.ds(start, 2), :] = (
                    piece[k : k + 2, t * LANES : (t + 1) * LANES]
                    + gate * piece[k : k + 2, (t + 2) * LANES : (t + 3) * LANES]
                )

    def bins_of(row):
        if row < 2 or row >= azimuth + 2:
            k = row if row < 2 else row - azimuth
            starts = [(halo, 4 * (azimuth + 4) + k, 4) for halo in halos[:3]]
            starts.append((next_sides[0], next_sides[0].shape[0] - 4 * RANGE + k, 4))
        else:
            starts = [(slot, row - 2 - offset, stride) for slot, (offset, stride) in zip(slots, offsets)]
        return jnp.concatenate([ref[pl.ds(start, RANGE, stride=stride), :] for ref, start, stride in starts], axis=0)

    total = jnp.zeros((radial, LANES), jnp.float32) if first else carry_sum[...]
    for group in batches(low_row, high_row):
        result = product(jnp.concatenate([bins_of(row) for row in group], axis=1), table1_ref, 0)
        for k, row in enumerate(group):
            part = result[k * radial : (k + 1) * radial]
            gate = widened(gate_ref, inner, row)
            for t in range(2):
                frag = part[:, (t + 2) * LANES : (t + 3) * LANES]
                second[row - base, t, inner, :] = part[:, t * LANES : (t + 1) * LANES] + gate * frag
                if own_low <= row < own_high:
                    total += second_ref[row - own_low, t] * frag

    for group in batches(first_low, first_high):
        parts = []
        for row in group:
            halves = [
                stencil(
                    second,
                    lambda d: (row - base + d, t),
                    center_ref[t, outer, :],
                    lower_ref[t, outer, :],
                    upper_ref[t, outer, :],
                    side_ref[t : t + 1, :],
                    8,
                    wide,
                )
                for t in range(2)
            ]
            parts.append(jnp.concatenate(halves, axis=1))
        result = product(jnp.concatenate(parts, axis=0), table2_ref)
        for k, row in enumerate(group):
            part = result[k * wide : (k + 1) * wide]
            frag = part[:, LANES:]
            initial[row - first_base, outer, :] = part[:, :LANES] + widened(gate_ref, outer, row) * frag
            if 2 <= row < azimuth + 2:
                total += moved_ref[row - max(first_low, 2)] * frag[8 : 8 + radial]
    if last:
        sum_out[...] = jnp.broadcast_to(jnp.sum(total.T, axis=0, keepdims=True), sum_out.shape)
    else:
        sum_out[...] = total

    for row in range(out_low, out_high):
        result = stencil(
            initial,
            lambda d: (row - first_base + d,),
            center_ref[1, inner, :],
            lower_ref[1, inner, :],
            upper_ref[1, inner, :],
            side_ref[1:2, :],
            EDGE,
            radial,
        ).T
        own_out[row - out_low] = result[:RANGE]
        next_out[row - out_low] = result[RANGE:]

    if not last:
        keep_second[...] = second[pl.ds(high_row - 2 - base, 2)]
        keep_first[...] = initial[pl.ds(first_high - 2 - first_base, 2)]


def call(kernel, outs, scratch, operands, micros=1):
    vmem = pl.BlockSpec(memory_space=pltpu.VMEM)
    return pl.pallas_call(
        kernel,
        out_shape=[jax.ShapeDtypeStruct(o, jnp.float32) for o in outs],
        in_specs=[vmem] * len(operands),
        out_specs=[vmem] * len(outs),
        scratch_shapes=[pltpu.VMEM(s, jnp.float32) for s in scratch],
        compiler_params=pltpu.CompilerParams(vmem_limit_bytes=VMEM_LIMIT),
        cost_estimate=pl.CostEstimate(flops=0, bytes_accessed=micros * MICRO, transcendentals=0),
    )(*operands)


def per_device(
    density,
    cotangent,
    drift_in,
    drift_out,
    spread,
    dest_bins,
    bott_split,
    coag_rate,
    frag_pairs,
    frag_gain,
    frag_rate,
    collide_speed,
    frag_speed,
    regime,
):
    own_bins, azimuth, radial = density.shape
    place = lax.axis_index("mass")
    phis, rows = lax.axis_size("phi"), lax.axis_size("row")
    cuts = [0, 5 * azimuth // 8, azimuth]
    spans = list(zip(cuts, cuts[1:]))

    def far(x):
        return lax.ppermute(x, "mass", [(0, 2), (2, 1), (1, 0)])

    def near(x):
        return lax.ppermute(x, "mass", [(0, 1), (1, 2)])

    def ending(x):
        return lax.ppermute(x, "mass", [(3, 2)])

    def returning(x):
        return lax.ppermute(x, "mass", [(2, 3)])

    count = azimuth + 4
    length = radial + 2 * EDGE
    share_rows, strip_rows = length + 8, 4 * count

    def flat(x):
        return x.reshape(-1, LANES)

    sides, gate, slope, opening, shares, first_cells, last_cells, late = call(
        functools.partial(opening_kernel, azimuth, radial, cuts[1]),
        [
            (8 * own_bins + 8, LANES),
            (azimuth, radial),
            (radial, LANES),
            (cuts[1] * own_bins + share_rows, LANES),
            (share_rows, LANES),
            (azimuth, 2, LANES),
            (azimuth, 2, LANES),
            (own_bins * (azimuth - cuts[1]), radial),
        ],
        [],
        [
            flat(cotangent),
            flat(density),
            drift_in,
            drift_out,
            spread[None, :],
            collide_speed,
            frag_speed[None, :],
            regime,
        ],
    )
    ring = [(i, (i + 1) % phis) for i in range(phis)]
    other = lax.ppermute(sides, "phi", ring)
    if phis > 2:
        after = lax.ppermute(sides, "phi", [(j, i) for i, j in ring])
        from_last = lax.broadcasted_iota(jnp.int32, other.shape, 0) % 4 < 2
        other = jnp.where(from_last, other, after)

    density_next = ending(density)
    far_first, near_first = far(opening), near(opening)
    left_cells, right_cells, gates = call(
        functools.partial(radial_kernel, azimuth, radial),
        [(2 * count + 8, LANES), (2 * count + 8, LANES), (radial, LANES)],
        [],
        [other, flat(first_cells), flat(last_cells), gate],
    )
    line = [(i, i + 1) for i in range(rows - 1)]
    left = lax.ppermute(left_cells, "row", line)
    right = lax.ppermute(right_cells, "row", [(j, i) for i, j in line])
    gates, density_next = lax.optimization_barrier((gates, density_next))
    long, short, gates = call(
        functools.partial(halo_kernel, azimuth, radial),
        [(strip_rows + 4 * own_bins + share_rows, LANES), (strip_rows + 4 * own_bins, LANES), (length, LANES)],
        [],
        [left, right, other, shares, gates],
    )

    frag_gain, long = lax.optimization_barrier((frag_gain, long))
    vmem = pl.BlockSpec(memory_space=pltpu.VMEM)
    total_bins = frag_gain.shape[0]
    both, own_cols, own_rows = pl.pallas_call(
        table_kernel,
        out_shape=[jax.ShapeDtypeStruct((3 * total_bins, n * total_bins), jnp.bfloat16) for n in (2, 1, 1)],
        in_specs=[vmem] * 5 + [pl.BlockSpec(memory_space=pltpu.SMEM)],
        out_specs=[vmem] * 3,
        compiler_params=pltpu.CompilerParams(vmem_limit_bytes=VMEM_LIMIT),
        cost_estimate=pl.CostEstimate(flops=0, bytes_accessed=3 * MICRO, transcendentals=0),
    )(
        frag_gain,
        dest_bins[None, :],
        bott_split[None, :],
        coag_rate[None, :],
        frag_rate[None, :],
        frag_pairs,
    )

    long_next = ending(long)
    first_next = jnp.concatenate([opening[: own_bins * cuts[1]], other[: 4 * own_bins]], axis=0)
    short, first_next, late, far_first, near_first, long_next, both = lax.optimization_barrier(
        (short, first_next, late, far_first, near_first, long_next, both)
    )
    halo_refs = [far(short), near(short), short, long_next]
    first_next = ending(first_next)
    far_late, near_late = far(late), near(late)

    coefs = [(2, length, LANES)] * 3 + [(2, LANES)]
    products = list(call(
        functools.partial(forward_kernel, azimuth, radial, cuts),
        [(j - (j < azimuth) - max(i - 1, 0), radial, LANES) for i, j in spans]
        + [(j - i, 2, radial, LANES) for i, j in spans]
        + coefs,
        [(count, length, LANES), (count, 2, length, LANES)],
        [
            flat(density),
            flat(density_next),
            far_first,
            near_first,
            shares,
            long,
            long_next,
            gates,
            slope,
            own_rows,
        ],
        13,
    ))
    groups = len(spans)
    products[0], halo_refs[0], halo_refs[1], late = lax.optimization_barrier(
        (products[0], halo_refs[0], halo_refs[1], late)
    )
    gathered = [[far_first, near_first, opening, first_next], [far_late, near_late, late, ending(late)]]
    moved, second, coefs = products[:groups], products[groups : 2 * groups], products[2 * groups :]

    own_outs, next_outs, carry = [], [], []
    for g in range(groups):
        first, last = g == 0, g == groups - 1
        low_row = 0 if first else cuts[g] + 2
        high_row = azimuth + 4 if last else cuts[g + 1] + 2
        new = high_row - low_row
        n_out = (azimuth + 2 if last else high_row - 2) - (2 if first else low_row - 2)
        operands = [*gathered[min(g, 1)]]
        offsets = [(cuts[0], cuts[1]) if first else (cuts[1], azimuth - cuts[1])] * 4
        operands += halo_refs + ([first_next] if first or last else [])
        operands += [*coefs, gates, second[g], moved[g]]
        operands += [both, own_cols, *carry]
        outs = [(n_out, RANGE, radial), (n_out, RANGE, radial), (8, radial) if last else (radial, LANES)]
        if not last:
            outs += [(2, 2, length, LANES), (2, length, LANES)]
        own_out, next_out, total, *kept = call(
            functools.partial(adjoint_kernel, azimuth, radial, low_row, high_row, offsets),
            outs,
            [(new + 2, 2, length, LANES), (new + 2, length, LANES)],
            operands,
            2 + new // 2,
        )
        carry = [*kept, total]
        own_outs.append(own_out)
        next_outs.append(returning(next_out))
    speed_gradient = total[0]
    size = lax.axis_size("mass")
    shares = [
        lax.ppermute(speed_gradient, "mass", [(i, (i + k) % size) for i in range(size)]) for k in range(1, size)
    ]
    shares = jnp.stack([*reversed(shares), speed_gradient] * 2)
    speed_gradient = jnp.sum(lax.dynamic_slice_in_dim(shares, size - 1 - place, size, 0), axis=0)
    step = 1
    while step < phis:
        speed_gradient += lax.ppermute(speed_gradient, "phi", [(i, i ^ step) for i in range(phis)])
        step *= 2
    next_outs = lax.optimization_barrier(next_outs)
    result = jnp.concatenate(
        [jnp.where(place == 3, there, here) for here, there in zip(own_outs, next_outs)], axis=0
    ).transpose(1, 0, 2)
    return (result, speed_gradient)


def solution(mesh):
    in_specs = (
        P("mass", "phi", "row"),
        P("mass", "phi", "row"),
        P("mass", None),
        P("mass", None),
        P("mass"),
        P(),
        P(),
        P(),
        P(),
        P(),
        P(),
        P("phi", "row"),
        P("row"),
        P("phi", "row"),
    )
    out_specs = (P("mass", "phi", "row"), P("row"))
    return jax.shard_map(
        per_device, mesh=mesh, in_specs=in_specs, out_specs=out_specs, check_vma=False
    )
```

```python
import functools

import jax
import jax.numpy as jnp
from jax import lax
from jax.experimental import pallas as pl
from jax.experimental.pallas import tpu as pltpu
from jax.sharding import PartitionSpec as P

RANGE = 64
LANES = 128
EDGE = 16
gate_width = 0.5
BATCH = 8
MICRO = 3 * 10**6
VMEM_LIMIT = 56 * 2**20


def split(value):
    high = value.astype(jnp.bfloat16)
    return high, (value - high.astype(jnp.float32)).astype(jnp.bfloat16)


def product(value, table_ref, axis=1):
    high, low = split(value)
    return lax.dot_general(
        jnp.concatenate([high, low, high], axis=axis),
        table_ref[...],
        (((axis,), (0,)), ((), ())),
        preferred_element_type=jnp.float32,
    )


def stencil(slab, index, center, lower, upper, side, start, size):
    rows = pl.ds(start, size)
    return (
        center * slab[(*index(0), rows)]
        + lower * slab[(*index(0), pl.ds(start - 1, size))]
        + upper * slab[(*index(0), pl.ds(start + 1, size))]
        + side * (slab[(*index(-1), rows)] + slab[(*index(1), rows)])
    )


def batches(low, high):
    return [range(i, min(i + BATCH, high)) for i in range(low, high, BATCH)]


def opening_kernel(azimuth, radial, first_rows, *refs):
    cot_ref, den_ref, in_ref, out_ref, spread_ref, collide_ref, speed_ref, regime_ref = refs[:8]
    sides_ref, gate_ref, slope_ref, opening_ref, shares_ref, first_ref, last_ref, late_ref = refs[8:]
    sigma = jax.nn.sigmoid((collide_ref[...] - speed_ref[...]) / gate_width)
    flagged = regime_ref[...].astype(jnp.float32)
    gate = flagged * sigma
    gate_ref[...] = gate
    ahead = (lax.axis_index("mass") < 3).astype(jnp.float32)
    slope = -flagged * sigma * (1.0 - sigma) / gate_width * ahead
    slope_ref[:, :azimuth] = slope.T
    for k, row in enumerate((azimuth - 2, azimuth - 1, 0, 1)):
        source, target = pl.ds(row, RANGE, stride=azimuth), pl.ds(k, RANGE, stride=4)
        sides_ref[target, :] = cot_ref[source, :]
        sides_ref[pl.ds(4 * RANGE + k, RANGE, stride=4), :] = den_ref[source, :]
        sides_ref[8 * RANGE + k : 8 * RANGE + k + 1, :] = gate[row : row + 1]
    sides_ref[8 * RANGE + 4 :, :] = jnp.zeros((4, radial), jnp.float32)

    block, blocks = lax.axis_index("row"), lax.axis_size("row")

    def window(number):
        lanes = pl.ds(pl.multiple_of(number * radial, radial), radial)
        return jnp.concatenate([in_ref[:, lanes], out_ref[:, lanes]], axis=0).T

    before = window(jnp.maximum(block - 1, 0))[radial - EDGE :] * (block > 0).astype(jnp.float32)
    after = window(jnp.minimum(block + 1, blocks - 1))[:EDGE] * (block < blocks - 1).astype(jnp.float32)
    spread = jnp.concatenate([spread_ref[...], spread_ref[...]], axis=1)
    spread = jnp.broadcast_to(spread, (8, LANES))
    shares = jnp.concatenate([before, window(block), after, spread], axis=0)
    shares_ref[...] = shares
    opening_ref[RANGE * first_rows :, :] = shares
    for b in range(RANGE):
        opening_ref[b * first_rows : (b + 1) * first_rows, :] = cot_ref[b * azimuth : b * azimuth + first_rows, :]
        low, high = b * (azimuth - first_rows), (b + 1) * (azimuth - first_rows)
        late_ref[low:high, :] = cot_ref[b * azimuth + first_rows : (b + 1) * azimuth, :]

    @pl.loop(0, azimuth // BATCH)
    def _(b):
        for k in range(BATCH):
            a = b * BATCH + k
            rows = pl.ds(a, RANGE, stride=azimuth)
            wide = jnp.concatenate([cot_ref[rows, :], den_ref[rows, :]], axis=0).T
            first_ref[a] = wide[:2]
            last_ref[a] = wide[radial - 2 :]


def radial_kernel(azimuth, radial, sides_ref, first_ref, last_ref, gate_ref, left_ref, right_ref, table_ref):
    count = azimuth + 4
    gates = jnp.concatenate(
        [
            sides_ref[8 * RANGE : 8 * RANGE + 2, :],
            gate_ref[...],
            sides_ref[8 * RANGE + 2 : 8 * RANGE + 4, :],
            jnp.zeros((LANES - count, radial), jnp.float32),
        ],
        axis=0,
    ).T
    table_ref[...] = gates
    for out_ref, own_ref, start in ((left_ref, last_ref, radial - 2), (right_ref, first_ref, 0)):
        for k, row in ((0, 0), (1, 1), (2, azimuth + 2), (3, azimuth + 3)):
            wide = sides_ref[pl.ds(k, 2 * RANGE, stride=4), :].T
            out_ref[2 * row : 2 * row + 2, :] = wide[start : start + 2]
        out_ref[4 : 4 + 2 * azimuth, :] = own_ref[...]
        out_ref[2 * count : 2 * count + 2, :] = gates[start : start + 2]
        out_ref[2 * count + 2 :, :] = jnp.zeros((6, LANES), jnp.float32)


def halo_kernel(azimuth, radial, left_ref, right_ref, sides_ref, shares_ref, gates_ref, *refs):
    long_ref, short_ref, table_ref = refs
    count = azimuth + 4
    for k in range(2):
        for source, start in ((left_ref, k), (right_ref, 2 + k)):
            cells = source[pl.ds(k, count, stride=2), :]
            long_ref[pl.ds(start, count, stride=4), :] = cells
            short_ref[pl.ds(start, count, stride=4), :] = cells
    strips = 4 * count
    short_ref[strips:, :] = sides_ref[: 4 * RANGE, :]
    long_ref[strips : strips + 4 * RANGE, :] = sides_ref[4 * RANGE : 8 * RANGE, :]
    long_ref[strips + 4 * RANGE :, :] = shares_ref[...]
    table_ref[...] = jnp.zeros(table_ref.shape, jnp.float32)
    table_ref[EDGE - 2 : EDGE, :] = left_ref[2 * count : 2 * count + 2, :]
    table_ref[EDGE : EDGE + radial, :] = gates_ref[...]
    table_ref[EDGE + radial : EDGE + radial + 2, :] = right_ref[2 * count : 2 * count + 2, :]


def slot_ranges():
    place = lax.axis_index("mass")
    return [
        jnp.where(place == 2, 0, jnp.where(place == 3, 4, place + 1)),
        jnp.where((place == 1) | (place == 2), place - 1, 4),
        place,
        jnp.where(place == 2, 3, 4),
    ]


def table_kernel(gain_ref, dest_ref, split_ref, coag_ref, frag_ref, pairs_ref, both_ref, cols_ref, rows_ref):
    ranges = slot_ranges()
    size = 4 * RANGE

    def ordered(value, scales=(1, 1, 1, 1)):
        parts = []
        for r, scale in zip(ranges, scales):
            part = jnp.zeros((value.shape[0], RANGE), value.dtype)
            for q in range(4):
                part = jnp.where(r == q, value[:, q * RANGE : (q + 1) * RANGE], part)
            parts.append(part * scale)
        return jnp.concatenate(parts, axis=1)

    def bin_ids(axis):
        ids = lax.broadcasted_iota(jnp.int32, (size, size), axis)
        shift = jnp.zeros((size, size), jnp.int32)
        for k, r in enumerate(ranges):
            shift = jnp.where((ids >= k * RANGE) & (ids < (k + 1) * RANGE), (r - k) * RANGE, shift)
        return ids + shift

    gains = []
    for r in ranges:
        held = jnp.minimum(r, 3)
        block = gain_ref[pl.ds(pl.multiple_of(held * RANGE, RANGE), RANGE), :]
        scales = [
            jnp.where((r < 4) & (c < 4), pairs_ref[held, jnp.minimum(c, 3)], 0).astype(jnp.float32) for c in ranges
        ]
        gains.append(ordered(block, scales))
    row_ids, col_ids = bin_ids(0), bin_ids(1)
    target = ordered(dest_ref[...])
    upper = ordered(split_ref[...])
    keeper = (row_ids == col_ids).astype(jnp.float32)
    moved = jnp.where(row_ids == target, 1.0 - upper, 0.0) + jnp.where(row_ids == target + 1, upper, 0.0)
    coag = (moved - keeper) * ordered(coag_ref[...]) + keeper
    frag = jnp.where(row_ids <= col_ids, jnp.concatenate(gains, axis=0), 0.0) - keeper * ordered(frag_ref[...])
    own = jnp.concatenate([coag[:, 2 * RANGE :], frag[:, 2 * RANGE :]], axis=1)
    for ref, table in ((both_ref, jnp.concatenate([coag, frag], axis=1)), (cols_ref, own), (rows_ref, own.T)):
        high, low = split(table)
        ref[:size] = high
        ref[size : 2 * size] = high
        ref[2 * size :] = low


def widened(ref, rows, lane):
    value = ref[rows, lane : lane + 1]
    return jnp.broadcast_to(value, (value.shape[0], LANES))


def pair(left, right, half):
    lanes = slice(half * RANGE, (half + 1) * RANGE)
    return jnp.concatenate([left[:, lanes], right[:, lanes]], axis=1)


def load_shares(shares, length, center_ref, lower_ref, upper_ref, side_ref):
    for t in range(2):
        left, right = [ref[pl.ds(start, length + 8), :] for ref, start in shares[2 * t : 2 * t + 2]]
        inward = pair(left[:length], right[:length], 0)
        outward = pair(left[:length], right[:length], 1)
        side = pair(left[length:], right[length:], 0)[:1]
        lower_ref[t] = inward
        upper_ref[t] = outward
        side_ref[t : t + 1] = side
        center_ref[t] = 1.0 - inward - outward - 2.0 * side


def forward_kernel(azimuth, radial, cuts, *refs):
    own_ref, next_ref, far_ref, near_ref, share_ref, own_halo, next_halo, gate_ref, slope_ref, table_ref = refs[:10]
    refs = refs[10:]
    groups = len(cuts) - 1
    moved_refs, second_refs = refs[:groups], refs[groups : 2 * groups]
    center_ref, inward_ref, outward_ref, side_ref, slab, mixed = refs[2 * groups :]
    inner = pl.ds(EDGE, radial)
    wide = radial + 16
    outer = pl.ds(8, wide)
    length = radial + 2 * EDGE
    strips = 4 * (azimuth + 4)
    first_rows = RANGE * cuts[1]
    shares = [(far_ref, first_rows), (near_ref, first_rows), (share_ref, 0), (next_halo, strips + 4 * RANGE)]
    load_shares(shares, length, center_ref, inward_ref, outward_ref, side_ref)

    def place(row, source, other, start, stride):
        bins = jnp.concatenate(
            [source[pl.ds(start, RANGE, stride=stride), :], other[pl.ds(start, RANGE, stride=stride), :]], axis=0
        )
        slab[row, inner, :] = bins.T

    for row, k in ((0, 0), (1, 1), (azimuth + 2, 2), (azimuth + 3, 3)):
        place(row, own_halo, next_halo, strips + k, 4)

    @pl.loop(0, azimuth // BATCH)
    def _(b):
        for k in range(BATCH):
            place(b * BATCH + k + 2, own_ref, next_ref, b * BATCH + k, azimuth)

    for row in range(azimuth + 4):
        cells = slice(4 * row, 4 * row + 4)
        strip = pair(own_halo[cells], next_halo[cells], 1)
        slab[row, pl.ds(EDGE - 2, 2), :] = strip[:2]
        slab[row, pl.ds(EDGE + radial, 2), :] = strip[2:]

    def move(rows):
        parts = []
        for a in rows:
            moved = stencil(
                slab,
                lambda d: (a + d,),
                center_ref[1, outer, :],
                outward_ref[1, pl.ds(7, wide), :],
                inward_ref[1, pl.ds(9, wide), :],
                side_ref[1:2, :],
                8,
                wide,
            )
            parts.append(jnp.concatenate([moved, widened(gate_ref, outer, a) * moved], axis=1))
        result = product(jnp.concatenate(parts, axis=0), table_ref)
        for k, a in enumerate(rows):
            mixed[a, 0, outer, :] = result[k * wide : (k + 1) * wide, :LANES]
            mixed[a, 1, outer, :] = result[k * wide : (k + 1) * wide, LANES:]
        return [part[8 : 8 + radial, :LANES] for part in parts]

    move([1, azimuth + 2])

    for g, (low, high) in enumerate(zip(cuts, cuts[1:])):
        for rows in batches(low, high):
            for a, moved in zip(rows, move([a + 2 for a in rows])):
                h, start = (g, max(low - 1, 0)) if a < high - 1 or high == azimuth else (g + 1, high - 1)
                moved_refs[h][a - start] = widened(slope_ref, slice(None), a) * moved

    for g, (low, high) in enumerate(zip(cuts, cuts[1:])):
        for a in range(low, high):
            slope = widened(slope_ref, slice(None), a)
            for t in range(2):
                second = stencil(
                    mixed,
                    lambda d: (a + 2 + d, t),
                    center_ref[t, inner, :],
                    outward_ref[t, pl.ds(EDGE - 1, radial), :],
                    inward_ref[t, pl.ds(EDGE + 1, radial), :],
                    side_ref[t : t + 1, :],
                    EDGE,
                    radial,
                )
                second_refs[g][a - low, t] = slope * second


def adjoint_kernel(azimuth, radial, low_row, high_row, offsets, *refs):
    first, last = low_row == 0, high_row == azimuth + 4
    refs = list(refs)

    def take(number):
        taken = refs[:number]
        del refs[:number]
        return taken

    slots = take(4)
    halos = take(4)
    next_sides = take(1) if first or last else None
    center_ref, lower_ref, upper_ref, side_ref = take(4)
    gate_ref, second_ref, moved_ref = take(3)
    table1_ref, table2_ref = take(2)
    carry_second, carry_first, carry_sum = (None, None, None) if first else take(3)
    own_out, next_out, sum_out = take(3)
    keep_second, keep_first = (None, None) if last else take(2)
    second, initial = refs

    inner = pl.ds(EDGE, radial)
    wide = radial + 16
    outer = pl.ds(8, wide)
    base = low_row if first else low_row - 2
    first_low, first_high = (1 if first else low_row - 1), high_row - 1
    first_base = first_low if first else first_low - 2
    out_low, out_high = first_base + 1, first_high - 1
    own_low, own_high = max(low_row, 2), min(high_row, azimuth + 2)

    if not first:
        second[pl.ds(0, 2)] = carry_second[...]
        initial[pl.ds(0, 2)] = carry_first[...]

    cells = slice(4 * low_row, 4 * high_row)
    edges = [halo[cells] for halo in halos]
    edges = product(jnp.concatenate([pair(*edges[:2], 0), pair(*edges[2:], 0)], axis=1), table1_ref)
    for row in range(low_row, high_row):
        piece = edges[4 * (row - low_row) : 4 * (row - low_row) + 4]
        for start, k in ((EDGE - 2, 0), (EDGE + radial, 2)):
            gate = widened(gate_ref, pl.ds(start, 2), row)
            for t in range(2):
                second[row - base, t, pl.ds(start, 2), :] = (
                    piece[k : k + 2, t * LANES : (t + 1) * LANES]
                    + gate * piece[k : k + 2, (t + 2) * LANES : (t + 3) * LANES]
                )

    def bins_of(row):
        if row < 2 or row >= azimuth + 2:
            k = row if row < 2 else row - azimuth
            starts = [(halo, 4 * (azimuth + 4) + k, 4) for halo in halos[:3]]
            starts.append((next_sides[0], next_sides[0].shape[0] - 4 * RANGE + k, 4))
        else:
            starts = [(slot, row - 2 - offset, stride) for slot, (offset, stride) in zip(slots, offsets)]
        return jnp.concatenate([ref[pl.ds(start, RANGE, stride=stride), :] for ref, start, stride in starts], axis=0)

    total = jnp.zeros((radial, LANES), jnp.float32) if first else carry_sum[...]
    for group in batches(low_row, high_row):
        result = product(jnp.concatenate([bins_of(row) for row in group], axis=1), table1_ref, 0)
        for k, row in enumerate(group):
            part = result[k * radial : (k + 1) * radial]
            gate = widened(gate_ref, inner, row)
            for t in range(2):
                frag = part[:, (t + 2) * LANES : (t + 3) * LANES]
                second[row - base, t, inner, :] = part[:, t * LANES : (t + 1) * LANES] + gate * frag
                if own_low <= row < own_high:
                    total += second_ref[row - own_low, t] * frag

    for group in batches(first_low, first_high):
        parts = []
        for row in group:
            halves = [
                stencil(
                    second,
                    lambda d: (row - base + d, t),
                    center_ref[t, outer, :],
                    lower_ref[t, outer, :],
                    upper_ref[t, outer, :],
                    side_ref[t : t + 1, :],
                    8,
                    wide,
                )
                for t in range(2)
            ]
            parts.append(jnp.concatenate(halves, axis=1))
        result = product(jnp.concatenate(parts, axis=0), table2_ref)
        for k, row in enumerate(group):
            part = result[k * wide : (k + 1) * wide]
            frag = part[:, LANES:]
            initial[row - first_base, outer, :] = part[:, :LANES] + widened(gate_ref, outer, row) * frag
            if 2 <= row < azimuth + 2:
                total += moved_ref[row - max(first_low, 2)] * frag[8 : 8 + radial]
    if last:
        sum_out[...] = jnp.broadcast_to(jnp.sum(total.T, axis=0, keepdims=True), sum_out.shape)
    else:
        sum_out[...] = total

    for row in range(out_low, out_high):
        result = stencil(
            initial,
            lambda d: (row - first_base + d,),
            center_ref[1, inner, :],
            lower_ref[1, inner, :],
            upper_ref[1, inner, :],
            side_ref[1:2, :],
            EDGE,
            radial,
        ).T
        rows = pl.ds(row - out_low, RANGE, stride=out_high - out_low)
        own_out[rows, :] = result[:RANGE]
        next_out[rows, :] = result[RANGE:]

    if not last:
        keep_second[...] = second[pl.ds(high_row - 2 - base, 2)]
        keep_first[...] = initial[pl.ds(first_high - 2 - first_base, 2)]


def call(kernel, outs, scratch, operands, micros=1):
    vmem = pl.BlockSpec(memory_space=pltpu.VMEM)
    return pl.pallas_call(
        kernel,
        out_shape=[jax.ShapeDtypeStruct(o, jnp.float32) for o in outs],
        in_specs=[vmem] * len(operands),
        out_specs=[vmem] * len(outs),
        scratch_shapes=[pltpu.VMEM(s, jnp.float32) for s in scratch],
        compiler_params=pltpu.CompilerParams(vmem_limit_bytes=VMEM_LIMIT),
        cost_estimate=pl.CostEstimate(flops=0, bytes_accessed=micros * MICRO, transcendentals=0),
    )(*operands)


def per_device(
    density,
    cotangent,
    drift_in,
    drift_out,
    spread,
    dest_bins,
    bott_split,
    coag_rate,
    frag_pairs,
    frag_gain,
    frag_rate,
    collide_speed,
    frag_speed,
    regime,
):
    own_bins, azimuth, radial = density.shape
    place = lax.axis_index("mass")
    phis, rows = lax.axis_size("phi"), lax.axis_size("row")
    cuts = [0, azimuth // 2 + 2, azimuth]
    spans = list(zip(cuts, cuts[1:]))

    def far(x):
        return lax.ppermute(x, "mass", [(0, 2), (2, 1), (1, 0)])

    def near(x):
        return lax.ppermute(x, "mass", [(0, 1), (1, 2)])

    def ending(x):
        return lax.ppermute(x, "mass", [(3, 2)])

    def returning(x):
        return lax.ppermute(x, "mass", [(2, 3)])

    count = azimuth + 4
    length = radial + 2 * EDGE
    share_rows, strip_rows = length + 8, 4 * count

    def flat(x):
        return x.reshape(-1, LANES)

    sides, gate, slope, opening, shares, first_cells, last_cells, late = call(
        functools.partial(opening_kernel, azimuth, radial, cuts[1]),
        [
            (8 * own_bins + 8, LANES),
            (azimuth, radial),
            (radial, LANES),
            (cuts[1] * own_bins + share_rows, LANES),
            (share_rows, LANES),
            (azimuth, 2, LANES),
            (azimuth, 2, LANES),
            (own_bins * (azimuth - cuts[1]), radial),
        ],
        [],
        [
            flat(cotangent),
            flat(density),
            drift_in,
            drift_out,
            spread[None, :],
            collide_speed,
            frag_speed[None, :],
            regime,
        ],
    )
    ring = [(i, (i + 1) % phis) for i in range(phis)]
    other = lax.ppermute(sides, "phi", ring)
    if phis > 2:
        after = lax.ppermute(sides, "phi", [(j, i) for i, j in ring])
        from_last = lax.broadcasted_iota(jnp.int32, other.shape, 0) % 4 < 2
        other = jnp.where(from_last, other, after)

    density_next = ending(density)
    far_first, near_first = far(opening), near(opening)
    left_cells, right_cells, gates = call(
        functools.partial(radial_kernel, azimuth, radial),
        [(2 * count + 8, LANES), (2 * count + 8, LANES), (radial, LANES)],
        [],
        [other, flat(first_cells), flat(last_cells), gate],
    )
    line = [(i, i + 1) for i in range(rows - 1)]
    left = lax.ppermute(left_cells, "row", line)
    right = lax.ppermute(right_cells, "row", [(j, i) for i, j in line])
    gates, density_next = lax.optimization_barrier((gates, density_next))
    long, short, gates = call(
        functools.partial(halo_kernel, azimuth, radial),
        [(strip_rows + 4 * own_bins + share_rows, LANES), (strip_rows + 4 * own_bins, LANES), (length, LANES)],
        [],
        [left, right, other, shares, gates],
    )

    frag_gain, long = lax.optimization_barrier((frag_gain, long))
    vmem = pl.BlockSpec(memory_space=pltpu.VMEM)
    total_bins = frag_gain.shape[0]
    both, own_cols, own_rows = pl.pallas_call(
        table_kernel,
        out_shape=[jax.ShapeDtypeStruct((3 * total_bins, n * total_bins), jnp.bfloat16) for n in (2, 1, 1)],
        in_specs=[vmem] * 5 + [pl.BlockSpec(memory_space=pltpu.SMEM)],
        out_specs=[vmem] * 3,
        compiler_params=pltpu.CompilerParams(vmem_limit_bytes=VMEM_LIMIT),
        cost_estimate=pl.CostEstimate(flops=0, bytes_accessed=3 * MICRO, transcendentals=0),
    )(
        frag_gain,
        dest_bins[None, :],
        bott_split[None, :],
        coag_rate[None, :],
        frag_rate[None, :],
        frag_pairs,
    )

    long_next = ending(long)
    first_next = jnp.concatenate([opening[: own_bins * cuts[1]], other[: 4 * own_bins]], axis=0)
    short, first_next, late, far_first, near_first, long_next, both = lax.optimization_barrier(
        (short, first_next, late, far_first, near_first, long_next, both)
    )
    halo_refs = [far(short), near(short), short, long_next]
    first_next = ending(first_next)
    far_late, near_late = far(late), near(late)

    coefs = [(2, length, LANES)] * 3 + [(2, LANES)]
    products = list(call(
        functools.partial(forward_kernel, azimuth, radial, cuts),
        [(j - (j < azimuth) - max(i - 1, 0), radial, LANES) for i, j in spans]
        + [(j - i, 2, radial, LANES) for i, j in spans]
        + coefs,
        [(count, length, LANES), (count, 2, length, LANES)],
        [
            flat(density),
            flat(density_next),
            far_first,
            near_first,
            shares,
            long,
            long_next,
            gates,
            slope,
            own_rows,
        ],
        13,
    ))
    groups = len(spans)
    products[0], halo_refs[0], halo_refs[1], late = lax.optimization_barrier(
        (products[0], halo_refs[0], halo_refs[1], late)
    )
    gathered = [[far_first, near_first, opening, first_next], [far_late, near_late, late, ending(late)]]
    moved, second, coefs = products[:groups], products[groups : 2 * groups], products[2 * groups :]

    own_outs, next_outs, carry = [], [], []
    for g in range(groups):
        first, last = g == 0, g == groups - 1
        low_row = 0 if first else cuts[g] + 2
        high_row = azimuth + 4 if last else cuts[g + 1] + 2
        new = high_row - low_row
        n_out = (azimuth + 2 if last else high_row - 2) - (2 if first else low_row - 2)
        operands = [*gathered[min(g, 1)]]
        offsets = [(cuts[0], cuts[1]) if first else (cuts[1], azimuth - cuts[1])] * 4
        operands += halo_refs + ([first_next] if first or last else [])
        operands += [*coefs, gates, second[g], moved[g]]
        operands += [both, own_cols, *carry]
        outs = [(RANGE * n_out, radial), (RANGE * n_out + 8 * first, radial), (8, radial) if last else (radial, LANES)]
        if not last:
            outs += [(2, 2, length, LANES), (2, length, LANES)]
        own_out, next_out, total, *kept = call(
            functools.partial(adjoint_kernel, azimuth, radial, low_row, high_row, offsets),
            outs,
            [(new + 2, 2, length, LANES), (new + 2, length, LANES)],
            operands,
            2 + new // 2,
        )
        carry = [*kept, total]
        own_outs.append(own_out)
        next_outs.append(returning(next_out))
    speed_gradient = total[0]
    step = 1
    while step < phis:
        speed_gradient += lax.ppermute(speed_gradient, "phi", [(i, i ^ step) for i in range(phis)])
        step *= 2
    size = lax.axis_size("mass")
    shares = [
        lax.ppermute(speed_gradient, "mass", [(i, (i + k) % size) for i in range(size)]) for k in range(1, size)
    ]
    shares = jnp.stack([*reversed(shares), speed_gradient] * 2)
    speed_gradient = jnp.sum(lax.dynamic_slice_in_dim(shares, size - 1 - place, size, 0), axis=0)
    next_outs = lax.optimization_barrier(next_outs)
    result = jnp.concatenate(
        [
            jnp.where(place == 3, there[: here.shape[0]], here).reshape(own_bins, -1, radial)
            for here, there in zip(own_outs, next_outs)
        ],
        axis=1,
    )
    return (result, speed_gradient)


def solution(mesh):
    in_specs = (
        P("mass", "phi", "row"),
        P("mass", "phi", "row"),
        P("mass", None),
        P("mass", None),
        P("mass"),
        P(),
        P(),
        P(),
        P(),
        P(),
        P(),
        P("phi", "row"),
        P("row"),
        P("phi", "row"),
    )
    out_specs = (P("mass", "phi", "row"), P("row"))
    return jax.shard_map(
        per_device, mesh=mesh, in_specs=in_specs, out_specs=out_specs, check_vma=False
    )
```

```python
import functools

import jax
import jax.numpy as jnp
from jax import lax
from jax.experimental import pallas as pl
from jax.experimental.pallas import tpu as pltpu
from jax.sharding import PartitionSpec as P

RANGE = 64
LANES = 128
EDGE = 16
gate_width = 0.5
BATCH = 8
MICRO = 3 * 10**6
VMEM_LIMIT = 56 * 2**20


def split(value):
    high = value.astype(jnp.bfloat16)
    return high, (value - high.astype(jnp.float32)).astype(jnp.bfloat16)


def product(value, table_ref, axis=1):
    high, low = split(value)
    return lax.dot_general(
        jnp.concatenate([high, low, high], axis=axis),
        table_ref[...],
        (((axis,), (0,)), ((), ())),
        preferred_element_type=jnp.float32,
    )


def stencil(slab, index, center, lower, upper, side, start, size):
    rows = pl.ds(start, size)
    return (
        center * slab[(*index(0), rows)]
        + lower * slab[(*index(0), pl.ds(start - 1, size))]
        + upper * slab[(*index(0), pl.ds(start + 1, size))]
        + side * (slab[(*index(-1), rows)] + slab[(*index(1), rows)])
    )


def batches(low, high):
    return [range(i, min(i + BATCH, high)) for i in range(low, high, BATCH)]


def opening_kernel(azimuth, radial, first_rows, *refs):
    cot_ref, den_ref, in_ref, out_ref, spread_ref, collide_ref, speed_ref, regime_ref = refs[:8]
    sides_ref, gate_ref, slope_ref, opening_ref, shares_ref, first_ref, last_ref, late_ref = refs[8:]
    sigma = jax.nn.sigmoid((collide_ref[...] - speed_ref[...]) / gate_width)
    flagged = regime_ref[...].astype(jnp.float32)
    gate = flagged * sigma
    gate_ref[...] = gate
    ahead = (lax.axis_index("mass") < 3).astype(jnp.float32)
    slope = -flagged * sigma * (1.0 - sigma) / gate_width * ahead
    slope_ref[:, :azimuth] = slope.T
    for k, row in enumerate((azimuth - 2, azimuth - 1, 0, 1)):
        source, target = pl.ds(row, RANGE, stride=azimuth), pl.ds(k, RANGE, stride=4)
        sides_ref[target, :] = cot_ref[source, :]
        sides_ref[pl.ds(4 * RANGE + k, RANGE, stride=4), :] = den_ref[source, :]
        sides_ref[8 * RANGE + k : 8 * RANGE + k + 1, :] = gate[row : row + 1]
    sides_ref[8 * RANGE + 4 :, :] = jnp.zeros((4, radial), jnp.float32)

    block, blocks = lax.axis_index("row"), lax.axis_size("row")

    def window(number):
        lanes = pl.ds(pl.multiple_of(number * radial, radial), radial)
        return jnp.concatenate([in_ref[:, lanes], out_ref[:, lanes]], axis=0).T

    before = window(jnp.maximum(block - 1, 0))[radial - EDGE :] * (block > 0).astype(jnp.float32)
    after = window(jnp.minimum(block + 1, blocks - 1))[:EDGE] * (block < blocks - 1).astype(jnp.float32)
    spread = jnp.concatenate([spread_ref[...], spread_ref[...]], axis=1)
    spread = jnp.broadcast_to(spread, (8, LANES))
    shares = jnp.concatenate([before, window(block), after, spread], axis=0)
    shares_ref[...] = shares
    opening_ref[RANGE * first_rows :, :] = shares
    for b in range(RANGE):
        opening_ref[b * first_rows : (b + 1) * first_rows, :] = cot_ref[b * azimuth : b * azimuth + first_rows, :]
        low, high = b * (azimuth - first_rows), (b + 1) * (azimuth - first_rows)
        late_ref[low:high, :] = cot_ref[b * azimuth + first_rows : (b + 1) * azimuth, :]

    @pl.loop(0, azimuth // BATCH)
    def _(b):
        for k in range(BATCH):
            a = b * BATCH + k
            rows = pl.ds(a, RANGE, stride=azimuth)
            wide = jnp.concatenate([cot_ref[rows, :], den_ref[rows, :]], axis=0).T
            first_ref[a] = wide[:2]
            last_ref[a] = wide[radial - 2 :]


def radial_kernel(azimuth, radial, sides_ref, first_ref, last_ref, gate_ref, left_ref, right_ref, table_ref):
    count = azimuth + 4
    gates = jnp.concatenate(
        [
            sides_ref[8 * RANGE : 8 * RANGE + 2, :],
            gate_ref[...],
            sides_ref[8 * RANGE + 2 : 8 * RANGE + 4, :],
            jnp.zeros((LANES - count, radial), jnp.float32),
        ],
        axis=0,
    ).T
    table_ref[...] = gates
    for out_ref, own_ref, start in ((left_ref, last_ref, radial - 2), (right_ref, first_ref, 0)):
        for k, row in ((0, 0), (1, 1), (2, azimuth + 2), (3, azimuth + 3)):
            wide = sides_ref[pl.ds(k, 2 * RANGE, stride=4), :].T
            out_ref[2 * row : 2 * row + 2, :] = wide[start : start + 2]
        out_ref[4 : 4 + 2 * azimuth, :] = own_ref[...]
        out_ref[2 * count : 2 * count + 2, :] = gates[start : start + 2]
        out_ref[2 * count + 2 :, :] = jnp.zeros((6, LANES), jnp.float32)


def halo_kernel(azimuth, radial, left_ref, right_ref, sides_ref, shares_ref, gates_ref, *refs):
    long_ref, short_ref, table_ref = refs
    count = azimuth + 4
    for k in range(2):
        for source, start in ((left_ref, k), (right_ref, 2 + k)):
            cells = source[pl.ds(k, count, stride=2), :]
            long_ref[pl.ds(start, count, stride=4), :] = cells
            short_ref[pl.ds(start, count, stride=4), :] = cells
    strips = 4 * count
    short_ref[strips:, :] = sides_ref[: 4 * RANGE, :]
    long_ref[strips : strips + 4 * RANGE, :] = sides_ref[4 * RANGE : 8 * RANGE, :]
    long_ref[strips + 4 * RANGE :, :] = shares_ref[...]
    table_ref[...] = jnp.zeros(table_ref.shape, jnp.float32)
    table_ref[EDGE - 2 : EDGE, :] = left_ref[2 * count : 2 * count + 2, :]
    table_ref[EDGE : EDGE + radial, :] = gates_ref[...]
    table_ref[EDGE + radial : EDGE + radial + 2, :] = right_ref[2 * count : 2 * count + 2, :]


def slot_ranges():
    place = lax.axis_index("mass")
    return [
        jnp.where(place == 2, 0, jnp.where(place == 3, 4, place + 1)),
        jnp.where((place == 1) | (place == 2), place - 1, 4),
        place,
        jnp.where(place == 2, 3, 4),
    ]


def table_kernel(gain_ref, dest_ref, split_ref, coag_ref, frag_ref, pairs_ref, both_ref, cols_ref, rows_ref):
    ranges = slot_ranges()
    size = 4 * RANGE

    def ordered(value, scales=(1, 1, 1, 1)):
        parts = []
        for r, scale in zip(ranges, scales):
            part = jnp.zeros((value.shape[0], RANGE), value.dtype)
            for q in range(4):
                part = jnp.where(r == q, value[:, q * RANGE : (q + 1) * RANGE], part)
            parts.append(part * scale)
        return jnp.concatenate(parts, axis=1)

    def bin_ids(axis):
        ids = lax.broadcasted_iota(jnp.int32, (size, size), axis)
        shift = jnp.zeros((size, size), jnp.int32)
        for k, r in enumerate(ranges):
            shift = jnp.where((ids >= k * RANGE) & (ids < (k + 1) * RANGE), (r - k) * RANGE, shift)
        return ids + shift

    gains = []
    for r in ranges:
        held = jnp.minimum(r, 3)
        block = gain_ref[pl.ds(pl.multiple_of(held * RANGE, RANGE), RANGE), :]
        scales = [
            jnp.where((r < 4) & (c < 4), pairs_ref[held, jnp.minimum(c, 3)], 0).astype(jnp.float32) for c in ranges
        ]
        gains.append(ordered(block, scales))
    row_ids, col_ids = bin_ids(0), bin_ids(1)
    target = ordered(dest_ref[...])
    upper = ordered(split_ref[...])
    keeper = (row_ids == col_ids).astype(jnp.float32)
    moved = jnp.where(row_ids == target, 1.0 - upper, 0.0) + jnp.where(row_ids == target + 1, upper, 0.0)
    coag = (moved - keeper) * ordered(coag_ref[...]) + keeper
    frag = jnp.where(row_ids <= col_ids, jnp.concatenate(gains, axis=0), 0.0) - keeper * ordered(frag_ref[...])
    own = jnp.concatenate([coag[:, 2 * RANGE :], frag[:, 2 * RANGE :]], axis=1)
    for ref, table in ((both_ref, jnp.concatenate([coag, frag], axis=1)), (cols_ref, own), (rows_ref, own.T)):
        high, low = split(table)
        ref[:size] = high
        ref[size : 2 * size] = high
        ref[2 * size :] = low


def widened(ref, rows, lane):
    value = ref[rows, lane : lane + 1]
    return jnp.broadcast_to(value, (value.shape[0], LANES))


def pair(left, right, half):
    lanes = slice(half * RANGE, (half + 1) * RANGE)
    return jnp.concatenate([left[:, lanes], right[:, lanes]], axis=1)


def load_shares(shares, length, center_ref, lower_ref, upper_ref, side_ref):
    for t in range(2):
        left, right = [ref[pl.ds(start, length + 8), :] for ref, start in shares[2 * t : 2 * t + 2]]
        inward = pair(left[:length], right[:length], 0)
        outward = pair(left[:length], right[:length], 1)
        side = pair(left[length:], right[length:], 0)[:1]
        lower_ref[t] = inward
        upper_ref[t] = outward
        side_ref[t : t + 1] = side
        center_ref[t] = 1.0 - inward - outward - 2.0 * side


def forward_kernel(azimuth, radial, cuts, *refs):
    own_ref, next_ref, far_ref, near_ref, share_ref, own_halo, next_halo, gate_ref, slope_ref, table_ref = refs[:10]
    refs = refs[10:]
    groups = len(cuts) - 1
    moved_refs, second_refs = refs[:groups], refs[groups : 2 * groups]
    center_ref, inward_ref, outward_ref, side_ref, slab, mixed = refs[2 * groups :]
    inner = pl.ds(EDGE, radial)
    wide = radial + 16
    outer = pl.ds(8, wide)
    length = radial + 2 * EDGE
    strips = 4 * (azimuth + 4)
    first_rows = RANGE * cuts[1]
    shares = [(far_ref, first_rows), (near_ref, first_rows), (share_ref, 0), (next_halo, strips + 4 * RANGE)]
    load_shares(shares, length, center_ref, inward_ref, outward_ref, side_ref)

    def place(row, source, other, start, stride):
        bins = jnp.concatenate(
            [source[pl.ds(start, RANGE, stride=stride), :], other[pl.ds(start, RANGE, stride=stride), :]], axis=0
        )
        slab[row, inner, :] = bins.T

    for row, k in ((0, 0), (1, 1), (azimuth + 2, 2), (azimuth + 3, 3)):
        place(row, own_halo, next_halo, strips + k, 4)

    @pl.loop(0, azimuth // BATCH)
    def _(b):
        for k in range(BATCH):
            place(b * BATCH + k + 2, own_ref, next_ref, b * BATCH + k, azimuth)

    for row in range(azimuth + 4):
        cells = slice(4 * row, 4 * row + 4)
        strip = pair(own_halo[cells], next_halo[cells], 1)
        slab[row, pl.ds(EDGE - 2, 2), :] = strip[:2]
        slab[row, pl.ds(EDGE + radial, 2), :] = strip[2:]

    def move(rows):
        parts = []
        for a in rows:
            moved = stencil(
                slab,
                lambda d: (a + d,),
                center_ref[1, outer, :],
                outward_ref[1, pl.ds(7, wide), :],
                inward_ref[1, pl.ds(9, wide), :],
                side_ref[1:2, :],
                8,
                wide,
            )
            parts.append(jnp.concatenate([moved, widened(gate_ref, outer, a) * moved], axis=1))
        result = product(jnp.concatenate(parts, axis=0), table_ref)
        for k, a in enumerate(rows):
            mixed[a, 0, outer, :] = result[k * wide : (k + 1) * wide, :LANES]
            mixed[a, 1, outer, :] = result[k * wide : (k + 1) * wide, LANES:]
        return [part[8 : 8 + radial, :LANES] for part in parts]

    move([1, azimuth + 2])

    for g, (low, high) in enumerate(zip(cuts, cuts[1:])):
        for rows in batches(low, high):
            for a, moved in zip(rows, move([a + 2 for a in rows])):
                h, start = (g, max(low - 1, 0)) if a < high - 1 or high == azimuth else (g + 1, high - 1)
                moved_refs[h][a - start] = widened(slope_ref, slice(None), a) * moved

    for g, (low, high) in enumerate(zip(cuts, cuts[1:])):
        for a in range(low, high):
            slope = widened(slope_ref, slice(None), a)
            for t in range(2):
                second = stencil(
                    mixed,
                    lambda d: (a + 2 + d, t),
                    center_ref[t, inner, :],
                    outward_ref[t, pl.ds(EDGE - 1, radial), :],
                    inward_ref[t, pl.ds(EDGE + 1, radial), :],
                    side_ref[t : t + 1, :],
                    EDGE,
                    radial,
                )
                second_refs[g][a - low, t] = slope * second


def adjoint_kernel(azimuth, radial, low_row, high_row, offsets, *refs):
    first, last = low_row == 0, high_row == azimuth + 4
    refs = list(refs)

    def take(number):
        taken = refs[:number]
        del refs[:number]
        return taken

    slots = take(4)
    halos = take(4)
    next_sides = take(1) if first or last else None
    center_ref, lower_ref, upper_ref, side_ref = take(4)
    gate_ref, second_ref, moved_ref = take(3)
    table1_ref, table2_ref = take(2)
    carry_second, carry_first, carry_sum = (None, None, None) if first else take(3)
    own_out, next_out, sum_out = take(3)
    keep_second, keep_first = (None, None) if last else take(2)
    second, initial = refs

    inner = pl.ds(EDGE, radial)
    wide = radial + 16
    outer = pl.ds(8, wide)
    base = low_row if first else low_row - 2
    first_low, first_high = (1 if first else low_row - 1), high_row - 1
    first_base = first_low if first else first_low - 2
    out_low, out_high = first_base + 1, first_high - 1
    own_low, own_high = max(low_row, 2), min(high_row, azimuth + 2)

    if not first:
        second[pl.ds(0, 2)] = carry_second[...]
        initial[pl.ds(0, 2)] = carry_first[...]

    cells = slice(4 * low_row, 4 * high_row)
    edges = [halo[cells] for halo in halos]
    edges = product(jnp.concatenate([pair(*edges[:2], 0), pair(*edges[2:], 0)], axis=1), table1_ref)
    for row in range(low_row, high_row):
        piece = edges[4 * (row - low_row) : 4 * (row - low_row) + 4]
        for start, k in ((EDGE - 2, 0), (EDGE + radial, 2)):
            gate = widened(gate_ref, pl.ds(start, 2), row)
            for t in range(2):
                second[row - base, t, pl.ds(start, 2), :] = (
                    piece[k : k + 2, t * LANES : (t + 1) * LANES]
                    + gate * piece[k : k + 2, (t + 2) * LANES : (t + 3) * LANES]
                )

    def bins_of(row):
        if row < 2 or row >= azimuth + 2:
            k = row if row < 2 else row - azimuth
            starts = [(halo, 4 * (azimuth + 4) + k, 4) for halo in halos[:3]]
            starts.append((next_sides[0], next_sides[0].shape[0] - 4 * RANGE + k, 4))
        else:
            starts = [(slot, row - 2 - offset, stride) for slot, (offset, stride) in zip(slots, offsets)]
        return jnp.concatenate([ref[pl.ds(start, RANGE, stride=stride), :] for ref, start, stride in starts], axis=0)

    total = jnp.zeros((radial, LANES), jnp.float32) if first else carry_sum[...]
    for group in batches(low_row, high_row):
        result = product(jnp.concatenate([bins_of(row) for row in group], axis=1), table1_ref, 0)
        for k, row in enumerate(group):
            part = result[k * radial : (k + 1) * radial]
            gate = widened(gate_ref, inner, row)
            for t in range(2):
                frag = part[:, (t + 2) * LANES : (t + 3) * LANES]
                second[row - base, t, inner, :] = part[:, t * LANES : (t + 1) * LANES] + gate * frag
                if own_low <= row < own_high:
                    total += second_ref[row - own_low, t] * frag

    for group in batches(first_low, first_high):
        parts = []
        for row in group:
            halves = [
                stencil(
                    second,
                    lambda d: (row - base + d, t),
                    center_ref[t, outer, :],
                    lower_ref[t, outer, :],
                    upper_ref[t, outer, :],
                    side_ref[t : t + 1, :],
                    8,
                    wide,
                )
                for t in range(2)
            ]
            parts.append(jnp.concatenate(halves, axis=1))
        result = product(jnp.concatenate(parts, axis=0), table2_ref)
        for k, row in enumerate(group):
            part = result[k * wide : (k + 1) * wide]
            frag = part[:, LANES:]
            initial[row - first_base, outer, :] = part[:, :LANES] + widened(gate_ref, outer, row) * frag
            if 2 <= row < azimuth + 2:
                total += moved_ref[row - max(first_low, 2)] * frag[8 : 8 + radial]
    if last:
        sum_out[...] = jnp.broadcast_to(jnp.sum(total.T, axis=0, keepdims=True), sum_out.shape)
    else:
        sum_out[...] = total

    for row in range(out_low, out_high):
        result = stencil(
            initial,
            lambda d: (row - first_base + d,),
            center_ref[1, inner, :],
            lower_ref[1, inner, :],
            upper_ref[1, inner, :],
            side_ref[1:2, :],
            EDGE,
            radial,
        ).T
        rows = pl.ds(row - out_low, RANGE, stride=out_high - out_low)
        own_out[rows, :] = result[:RANGE]
        next_out[rows, :] = result[RANGE:]

    if not last:
        keep_second[...] = second[pl.ds(high_row - 2 - base, 2)]
        keep_first[...] = initial[pl.ds(first_high - 2 - first_base, 2)]


def call(kernel, outs, scratch, operands, micros=1):
    vmem = pl.BlockSpec(memory_space=pltpu.VMEM)
    return pl.pallas_call(
        kernel,
        out_shape=[jax.ShapeDtypeStruct(o, jnp.float32) for o in outs],
        in_specs=[vmem] * len(operands),
        out_specs=[vmem] * len(outs),
        scratch_shapes=[pltpu.VMEM(s, jnp.float32) for s in scratch],
        compiler_params=pltpu.CompilerParams(vmem_limit_bytes=VMEM_LIMIT),
        cost_estimate=pl.CostEstimate(flops=0, bytes_accessed=micros * MICRO, transcendentals=0),
    )(*operands)


def per_device(
    density,
    cotangent,
    drift_in,
    drift_out,
    spread,
    dest_bins,
    bott_split,
    coag_rate,
    frag_pairs,
    frag_gain,
    frag_rate,
    collide_speed,
    frag_speed,
    regime,
):
    own_bins, azimuth, radial = density.shape
    place = lax.axis_index("mass")
    phis, rows = lax.axis_size("phi"), lax.axis_size("row")
    cuts = [0, azimuth // 2 + 2, azimuth]
    spans = list(zip(cuts, cuts[1:]))

    def far(x):
        return lax.ppermute(x, "mass", [(0, 2), (2, 1), (1, 0)])

    def near(x):
        return lax.ppermute(x, "mass", [(0, 1), (1, 2)])

    def ending(x):
        return lax.ppermute(x, "mass", [(3, 2)])

    def returning(x):
        return lax.ppermute(x, "mass", [(2, 3)])

    count = azimuth + 4
    length = radial + 2 * EDGE
    share_rows, strip_rows = length + 8, 4 * count

    def flat(x):
        return x.reshape(-1, LANES)

    sides, gate, slope, opening, shares, first_cells, last_cells, late = call(
        functools.partial(opening_kernel, azimuth, radial, cuts[1]),
        [
            (8 * own_bins + 8, LANES),
            (azimuth, radial),
            (radial, LANES),
            (cuts[1] * own_bins + share_rows, LANES),
            (share_rows, LANES),
            (azimuth, 2, LANES),
            (azimuth, 2, LANES),
            (own_bins * (azimuth - cuts[1]), radial),
        ],
        [],
        [
            flat(cotangent),
            flat(density),
            drift_in,
            drift_out,
            spread[None, :],
            collide_speed,
            frag_speed[None, :],
            regime,
        ],
    )
    ring = [(i, (i + 1) % phis) for i in range(phis)]
    other = lax.ppermute(sides, "phi", ring)
    if phis > 2:
        after = lax.ppermute(sides, "phi", [(j, i) for i, j in ring])
        from_last = lax.broadcasted_iota(jnp.int32, other.shape, 0) % 4 < 2
        other = jnp.where(from_last, other, after)

    density_next = ending(density)
    far_first, near_first = far(opening), near(opening)
    left_cells, right_cells, gates = call(
        functools.partial(radial_kernel, azimuth, radial),
        [(2 * count + 8, LANES), (2 * count + 8, LANES), (radial, LANES)],
        [],
        [other, flat(first_cells), flat(last_cells), gate],
    )
    line = [(i, i + 1) for i in range(rows - 1)]
    left = lax.ppermute(left_cells, "row", line)
    right = lax.ppermute(right_cells, "row", [(j, i) for i, j in line])
    gates, density_next = lax.optimization_barrier((gates, density_next))
    long, short, gates = call(
        functools.partial(halo_kernel, azimuth, radial),
        [(strip_rows + 4 * own_bins + share_rows, LANES), (strip_rows + 4 * own_bins, LANES), (length, LANES)],
        [],
        [left, right, other, shares, gates],
    )

    frag_gain, long = lax.optimization_barrier((frag_gain, long))
    vmem = pl.BlockSpec(memory_space=pltpu.VMEM)
    total_bins = frag_gain.shape[0]
    both, own_cols, own_rows = pl.pallas_call(
        table_kernel,
        out_shape=[jax.ShapeDtypeStruct((3 * total_bins, n * total_bins), jnp.bfloat16) for n in (2, 1, 1)],
        in_specs=[vmem] * 5 + [pl.BlockSpec(memory_space=pltpu.SMEM)],
        out_specs=[vmem] * 3,
        compiler_params=pltpu.CompilerParams(vmem_limit_bytes=VMEM_LIMIT),
        cost_estimate=pl.CostEstimate(flops=0, bytes_accessed=3 * MICRO, transcendentals=0),
    )(
        frag_gain,
        dest_bins[None, :],
        bott_split[None, :],
        coag_rate[None, :],
        frag_rate[None, :],
        frag_pairs,
    )

    long_next = ending(long)
    first_next = jnp.concatenate([opening[: own_bins * cuts[1]], other[: 4 * own_bins]], axis=0)
    halo_refs = [far(short), near(short), short, long_next]
    first_next = ending(first_next)
    far_late, near_late = far(late), near(late)

    coefs = [(2, length, LANES)] * 3 + [(2, LANES)]
    products = list(call(
        functools.partial(forward_kernel, azimuth, radial, cuts),
        [(j - (j < azimuth) - max(i - 1, 0), radial, LANES) for i, j in spans]
        + [(j - i, 2, radial, LANES) for i, j in spans]
        + coefs,
        [(count, length, LANES), (count, 2, length, LANES)],
        [
            flat(density),
            flat(density_next),
            far_first,
            near_first,
            shares,
            long,
            long_next,
            gates,
            slope,
            own_rows,
        ],
        13,
    ))
    groups = len(spans)
    products[0], halo_refs[0], halo_refs[1], late = lax.optimization_barrier(
        (products[0], halo_refs[0], halo_refs[1], late)
    )
    gathered = [[far_first, near_first, opening, first_next], [far_late, near_late, late, ending(late)]]
    moved, second, coefs = products[:groups], products[groups : 2 * groups], products[2 * groups :]

    own_outs, next_outs, carry = [], [], []
    for g in range(groups):
        first, last = g == 0, g == groups - 1
        low_row = 0 if first else cuts[g] + 2
        high_row = azimuth + 4 if last else cuts[g + 1] + 2
        new = high_row - low_row
        n_out = (azimuth + 2 if last else high_row - 2) - (2 if first else low_row - 2)
        operands = [*gathered[min(g, 1)]]
        offsets = [(cuts[0], cuts[1]) if first else (cuts[1], azimuth - cuts[1])] * 4
        operands += halo_refs + ([first_next] if first or last else [])
        operands += [*coefs, gates, second[g], moved[g]]
        operands += [both, own_cols, *carry]
        outs = [(RANGE * n_out, radial), (RANGE * n_out + 8 * first, radial), (8, radial) if last else (radial, LANES)]
        if not last:
            outs += [(2, 2, length, LANES), (2, length, LANES)]
        own_out, next_out, total, *kept = call(
            functools.partial(adjoint_kernel, azimuth, radial, low_row, high_row, offsets),
            outs,
            [(new + 2, 2, length, LANES), (new + 2, length, LANES)],
            operands,
            2 + new // 2,
        )
        carry = [*kept, total]
        own_outs.append(own_out)
        next_outs.append(returning(next_out))
    speed_gradient = total[0]
    step = 1
    while step < phis:
        speed_gradient += lax.ppermute(speed_gradient, "phi", [(i, i ^ step) for i in range(phis)])
        step *= 2
    size = lax.axis_size("mass")
    shares = [
        lax.ppermute(speed_gradient, "mass", [(i, (i + k) % size) for i in range(size)]) for k in range(1, size)
    ]
    shares = jnp.stack([*reversed(shares), speed_gradient] * 2)
    speed_gradient = jnp.sum(lax.dynamic_slice_in_dim(shares, size - 1 - place, size, 0), axis=0)
    next_outs = lax.optimization_barrier(next_outs)
    result = jnp.concatenate(
        [
            jnp.where(place == 3, there[: here.shape[0]], here).reshape(own_bins, -1, radial)
            for here, there in zip(own_outs, next_outs)
        ],
        axis=1,
    )
    return (result, speed_gradient)


def solution(mesh):
    in_specs = (
        P("mass", "phi", "row"),
        P("mass", "phi", "row"),
        P("mass", None),
        P("mass", None),
        P("mass"),
        P(),
        P(),
        P(),
        P(),
        P(),
        P(),
        P("phi", "row"),
        P("row"),
        P("phi", "row"),
    )
    out_specs = (P("mass", "phi", "row"), P("row"))
    return jax.shard_map(
        per_device, mesh=mesh, in_specs=in_specs, out_specs=out_specs, check_vma=False
    )
```

```python
import functools

import jax
import jax.numpy as jnp
from jax import lax
from jax.experimental import pallas as pl
from jax.experimental.pallas import tpu as pltpu
from jax.sharding import PartitionSpec as P

RANGE = 64
LANES = 128
EDGE = 16
gate_width = 0.5
BATCH = 8
EDGE = 16
gate_width = 0.5
BATCH = 8
VMEM_LIMIT = 56 * 2**20


def split(value):
    high = value.astype(jnp.bfloat16)
    return high, (value - high.astype(jnp.float32)).astype(jnp.bfloat16)


def product(value, table_ref, axis=1):
    high, low = split(value)
    return lax.dot_general(
        jnp.concatenate([high, low, high], axis=axis),
        table_ref[...],
        (((axis,), (0,)), ((), ())),
        preferred_element_type=jnp.float32,
    )


def stencil(slab, index, center, lower, upper, side, start, size):
    rows = pl.ds(start, size)
    return (
        center * slab[(*index(0), rows)]
        + lower * slab[(*index(0), pl.ds(start - 1, size))]
        + upper * slab[(*index(0), pl.ds(start + 1, size))]
        + side * (slab[(*index(-1), rows)] + slab[(*index(1), rows)])
    )


def batches(low, high):
    return [range(i, min(i + BATCH, high)) for i in range(low, high, BATCH)]


def opening_kernel(azimuth, radial, first_rows, *refs):
    cot_ref, den_ref, in_ref, out_ref, spread_ref, collide_ref, speed_ref, regime_ref = refs[:8]
    sides_ref, gate_ref, slope_ref, opening_ref, shares_ref, first_ref, last_ref, late_ref = refs[8:]
    sigma = jax.nn.sigmoid((collide_ref[...] - speed_ref[...]) / gate_width)
    flagged = regime_ref[...].astype(jnp.float32)
    gate = flagged * sigma
    gate_ref[...] = gate
    ahead = (lax.axis_index("mass") < 3).astype(jnp.float32)
    slope = -flagged * sigma * (1.0 - sigma) / gate_width * ahead
    slope_ref[:, :azimuth] = slope.T
    for k, row in enumerate((azimuth - 2, azimuth - 1, 0, 1)):
        source, target = pl.ds(row, RANGE, stride=azimuth), pl.ds(k, RANGE, stride=4)
        sides_ref[target, :] = cot_ref[source, :]
        sides_ref[pl.ds(4 * RANGE + k, RANGE, stride=4), :] = den_ref[source, :]
        sides_ref[8 * RANGE + k : 8 * RANGE + k + 1, :] = gate[row : row + 1]
    sides_ref[8 * RANGE + 4 :, :] = jnp.zeros((4, radial), jnp.float32)

    block, blocks = lax.axis_index("row"), lax.axis_size("row")

    def window(number):
        lanes = pl.ds(pl.multiple_of(number * radial, radial), radial)
        return jnp.concatenate([in_ref[:, lanes], out_ref[:, lanes]], axis=0).T

    before = window(jnp.maximum(block - 1, 0))[radial - EDGE :] * (block > 0).astype(jnp.float32)
    after = window(jnp.minimum(block + 1, blocks - 1))[:EDGE] * (block < blocks - 1).astype(jnp.float32)
    spread = jnp.concatenate([spread_ref[...], spread_ref[...]], axis=1)
    spread = jnp.broadcast_to(spread, (8, LANES))
    shares = jnp.concatenate([before, window(block), after, spread], axis=0)
    shares_ref[...] = shares
    opening_ref[RANGE * first_rows :, :] = shares
    for b in range(RANGE):
        opening_ref[b * first_rows : (b + 1) * first_rows, :] = cot_ref[b * azimuth : b * azimuth + first_rows, :]
        low, high = b * (azimuth - first_rows), (b + 1) * (azimuth - first_rows)
        late_ref[low:high, :] = cot_ref[b * azimuth + first_rows : (b + 1) * azimuth, :]

    @pl.loop(0, azimuth // BATCH)
    def _(b):
        for k in range(BATCH):
            a = b * BATCH + k
            rows = pl.ds(a, RANGE, stride=azimuth)
            wide = jnp.concatenate([cot_ref[rows, :], den_ref[rows, :]], axis=0).T
            first_ref[a] = wide[:2]
            last_ref[a] = wide[radial - 2 :]


def radial_kernel(azimuth, radial, sides_ref, first_ref, last_ref, gate_ref, left_ref, right_ref, table_ref):
    count = azimuth + 4
    gates = jnp.concatenate(
        [
            sides_ref[8 * RANGE : 8 * RANGE + 2, :],
            gate_ref[...],
            sides_ref[8 * RANGE + 2 : 8 * RANGE + 4, :],
            jnp.zeros((LANES - count, radial), jnp.float32),
        ],
        axis=0,
    ).T
    table_ref[...] = gates
    for out_ref, own_ref, start in ((left_ref, last_ref, radial - 2), (right_ref, first_ref, 0)):
        for k, row in ((0, 0), (1, 1), (2, azimuth + 2), (3, azimuth + 3)):
            wide = sides_ref[pl.ds(k, 2 * RANGE, stride=4), :].T
            out_ref[2 * row : 2 * row + 2, :] = wide[start : start + 2]
        out_ref[4 : 4 + 2 * azimuth, :] = own_ref[...]
        out_ref[2 * count : 2 * count + 2, :] = gates[start : start + 2]
        out_ref[2 * count + 2 :, :] = jnp.zeros((6, LANES), jnp.float32)


def halo_kernel(azimuth, radial, left_ref, right_ref, sides_ref, shares_ref, gates_ref, *refs):
    long_ref, short_ref, table_ref = refs
    count = azimuth + 4
    for k in range(2):
        for source, start in ((left_ref, k), (right_ref, 2 + k)):
            cells = source[pl.ds(k, count, stride=2), :]
            long_ref[pl.ds(start, count, stride=4), :] = cells
            short_ref[pl.ds(start, count, stride=4), :] = cells
    strips = 4 * count
    short_ref[strips:, :] = sides_ref[: 4 * RANGE, :]
    long_ref[strips : strips + 4 * RANGE, :] = sides_ref[4 * RANGE : 8 * RANGE, :]
    long_ref[strips + 4 * RANGE :, :] = shares_ref[...]
    table_ref[...] = jnp.zeros(table_ref.shape, jnp.float32)
    table_ref[EDGE - 2 : EDGE, :] = left_ref[2 * count : 2 * count + 2, :]
    table_ref[EDGE : EDGE + radial, :] = gates_ref[...]
    table_ref[EDGE + radial : EDGE + radial + 2, :] = right_ref[2 * count : 2 * count + 2, :]


def slot_ranges():
    place = lax.axis_index("mass")
    return [
        jnp.where(place == 2, 0, jnp.where(place == 3, 4, place + 1)),
        jnp.where((place == 1) | (place == 2), place - 1, 4),
        place,
        jnp.where(place == 2, 3, 4),
    ]


def table_kernel(gain_ref, dest_ref, split_ref, coag_ref, frag_ref, pairs_ref, both_ref, cols_ref, rows_ref):
    ranges = slot_ranges()
    size = 4 * RANGE

    def ordered(value, scales=(1, 1, 1, 1)):
        parts = []
        for r, scale in zip(ranges, scales):
            part = jnp.zeros((value.shape[0], RANGE), value.dtype)
            for q in range(4):
                part = jnp.where(r == q, value[:, q * RANGE : (q + 1) * RANGE], part)
            parts.append(part * scale)
        return jnp.concatenate(parts, axis=1)

    def bin_ids(axis):
        ids = lax.broadcasted_iota(jnp.int32, (size, size), axis)
        shift = jnp.zeros((size, size), jnp.int32)
        for k, r in enumerate(ranges):
            shift = jnp.where((ids >= k * RANGE) & (ids < (k + 1) * RANGE), (r - k) * RANGE, shift)
        return ids + shift

    gains = []
    for r in ranges:
        held = jnp.minimum(r, 3)
        block = gain_ref[pl.ds(pl.multiple_of(held * RANGE, RANGE), RANGE), :]
        scales = [
            jnp.where((r < 4) & (c < 4), pairs_ref[held, jnp.minimum(c, 3)], 0).astype(jnp.float32) for c in ranges
        ]
        gains.append(ordered(block, scales))
    row_ids, col_ids = bin_ids(0), bin_ids(1)
    target = ordered(dest_ref[...])
    upper = ordered(split_ref[...])
    keeper = (row_ids == col_ids).astype(jnp.float32)
    moved = jnp.where(row_ids == target, 1.0 - upper, 0.0) + jnp.where(row_ids == target + 1, upper, 0.0)
    coag = (moved - keeper) * ordered(coag_ref[...]) + keeper
    frag = jnp.where(row_ids <= col_ids, jnp.concatenate(gains, axis=0), 0.0) - keeper * ordered(frag_ref[...])
    own = jnp.concatenate([coag[:, 2 * RANGE :], frag[:, 2 * RANGE :]], axis=1)
    for ref, table in ((both_ref, jnp.concatenate([coag, frag], axis=1)), (cols_ref, own), (rows_ref, own.T)):
        high, low = split(table)
        ref[:size] = high
        ref[size : 2 * size] = high
        ref[2 * size :] = low


def widened(ref, rows, lane):
    value = ref[rows, lane : lane + 1]
    return jnp.broadcast_to(value, (value.shape[0], LANES))


def pair(left, right, half):
    lanes = slice(half * RANGE, (half + 1) * RANGE)
    return jnp.concatenate([left[:, lanes], right[:, lanes]], axis=1)


def moved_spans(cuts):
    ends = [0, *(cut - 1 for cut in cuts[1:-1]), cuts[-1]]
    return list(zip(ends, ends[1:]))


def load_shares(shares, t, length, center_ref, lower_ref, upper_ref, side_ref):
    left, right = [ref[pl.ds(start, length + 8), :] for ref, start in shares[2 * t : 2 * t + 2]]
    inward = pair(left[:length], right[:length], 0)
    outward = pair(left[:length], right[:length], 1)
    side = pair(left[length:], right[length:], 0)[:1]
    lower_ref[t] = inward
    upper_ref[t] = outward
    side_ref[t : t + 1] = side
    center_ref[t] = 1.0 - inward - outward - 2.0 * side


def forward_kernel(azimuth, radial, cuts, *refs):
    own_ref, next_ref, far_ref, near_ref, share_ref, own_halo, next_halo, gate_ref, slope_ref, table_ref = refs[:10]
    refs = refs[10:]
    groups = len(cuts) - 1
    moved_refs, second_refs = refs[:groups], refs[groups : 2 * groups]
    center_ref, inward_ref, outward_ref, side_ref, slab, mixed, held, moved_all, second_all, sems = refs[2 * groups :]
    inner = pl.ds(EDGE, radial)
    wide = radial + 16
    outer = pl.ds(8, wide)
    length = radial + 2 * EDGE
    strips = 4 * (azimuth + 4)
    first_rows = RANGE * cuts[1]
    loads = [
        pltpu.make_async_copy(ref.at[pl.ds(first_rows, length + 8)], held.at[k], sems.at[k])
        for k, ref in enumerate((far_ref, near_ref))
    ]
    for load in loads:
        load.start()
    stores = []

    def store(source, target):
        copy = pltpu.make_async_copy(source, target, sems.at[2 + len(stores)])
        copy.start()
        stores.append(copy)

    shares = [None, None, (share_ref, 0), (next_halo, strips + 4 * RANGE)]
    load_shares(shares, 1, length, center_ref, inward_ref, outward_ref, side_ref)

    def place(row, source, other, start, stride):
        bins = jnp.concatenate(
            [source[pl.ds(start, RANGE, stride=stride), :], other[pl.ds(start, RANGE, stride=stride), :]], axis=0
        )
        slab[row, inner, :] = bins.T

    for row, k in ((0, 0), (1, 1), (azimuth + 2, 2), (azimuth + 3, 3)):
        place(row, own_halo, next_halo, strips + k, 4)

    @pl.loop(0, azimuth // BATCH)
    def _(b):
        for k in range(BATCH):
            place(b * BATCH + k + 2, own_ref, next_ref, b * BATCH + k, azimuth)

    for row in range(azimuth + 4):
        cells = slice(4 * row, 4 * row + 4)
        strip = pair(own_halo[cells], next_halo[cells], 1)
        slab[row, pl.ds(EDGE - 2, 2), :] = strip[:2]
        slab[row, pl.ds(EDGE + radial, 2), :] = strip[2:]

    def move(rows):
        parts = []
        for a in rows:
            moved = stencil(
                slab,
                lambda d: (a + d,),
                center_ref[1, outer, :],
                outward_ref[1, pl.ds(7, wide), :],
                inward_ref[1, pl.ds(9, wide), :],
                side_ref[1:2, :],
                8,
                wide,
            )
            parts.append(jnp.concatenate([moved, widened(gate_ref, outer, a) * moved], axis=1))
        result = product(jnp.concatenate(parts, axis=0), table_ref)
        for k, a in enumerate(rows):
            mixed[a, 0, outer, :] = result[k * wide : (k + 1) * wide, :LANES]
            mixed[a, 1, outer, :] = result[k * wide : (k + 1) * wide, LANES:]
        return [part[8 : 8 + radial, :LANES] for part in parts]

    move([1, azimuth + 2])

    for rows in batches(0, azimuth):
        for a, moved in zip(rows, move([a + 2 for a in rows])):
            moved_all[a] = widened(slope_ref, slice(None), a) * moved
    for g, (low, high) in enumerate(moved_spans(cuts)):
        store(moved_all.at[pl.ds(low, high - low)], moved_refs[g])

    for load in loads:
        load.wait()
    shares = [(held.at[0], 0), (held.at[1], 0), (share_ref, 0), (next_halo, strips + 4 * RANGE)]
    load_shares(shares, 0, length, center_ref, inward_ref, outward_ref, side_ref)

    for g, (low, high) in enumerate(zip(cuts, cuts[1:])):
        for rows in batches(low, high):
            for a in rows:
                slope = widened(slope_ref, slice(None), a)
                for t in range(2):
                    second = stencil(
                        mixed,
                        lambda d: (a + 2 + d, t),
                        center_ref[t, inner, :],
                        outward_ref[t, pl.ds(EDGE - 1, radial), :],
                        inward_ref[t, pl.ds(EDGE + 1, radial), :],
                        side_ref[t : t + 1, :],
                        EDGE,
                        radial,
                    )
                    second_all[a, t] = slope * second
            size = len(rows)
            store(second_all.at[pl.ds(rows[0], size)], second_refs[g].at[pl.ds(rows[0] - low, size)])

    for copy in stores:
        copy.wait()


def adjoint_kernel(azimuth, radial, low_row, high_row, offsets, *refs):
    first, last = low_row == 0, high_row == azimuth + 4
    refs = list(refs)

    def take(number):
        taken = refs[:number]
        del refs[:number]
        return taken

    slots = take(4)
    halos = take(4)
    next_sides = slots[3:] if first else take(1)
    center_ref, lower_ref, upper_ref, side_ref = take(4)
    gate_ref, second_ref, moved_ref = take(3)
    table1_ref, table2_ref = take(2)
    carry_second, carry_first, carry_sum = (None, None, None) if first else take(3)
    own_out, next_out, sum_out = take(3)
    keep_second, keep_first = (None, None) if last else take(2)
    second, initial, second_held, moved_held, table_held, sems = refs
    loads = [
        pltpu.make_async_copy(source, target, sems.at[k])
        for k, (source, target) in enumerate(
            ((second_ref, second_held), (moved_ref, moved_held), (table2_ref, table_held))
        )
    ]
    for load in loads:
        load.start()

    inner = pl.ds(EDGE, radial)
    wide = radial + 16
    outer = pl.ds(8, wide)
    base = low_row if first else low_row - 2
    first_low, first_high = (1 if first else low_row - 1), high_row - 1
    first_base = first_low if first else first_low - 2
    out_low, out_high = first_base + 1, first_high - 1
    own_low, own_high = max(low_row, 2), min(high_row, azimuth + 2)

    if not first:
        second[pl.ds(0, 2)] = carry_second[...]
        initial[pl.ds(0, 2)] = carry_first[...]

    cells = slice(4 * low_row, 4 * high_row)
    edges = [halo[cells] for halo in halos]
    edges = product(jnp.concatenate([pair(*edges[:2], 0), pair(*edges[2:], 0)], axis=1), table1_ref)
    for row in range(low_row, high_row):
        piece = edges[4 * (row - low_row) : 4 * (row - low_row) + 4]
        for start, k in ((EDGE - 2, 0), (EDGE + radial, 2)):
            gate = widened(gate_ref, pl.ds(start, 2), row)
            for t in range(2):
                second[row - base, t, pl.ds(start, 2), :] = (
                    piece[k : k + 2, t * LANES : (t + 1) * LANES]
                    + gate * piece[k : k + 2, (t + 2) * LANES : (t + 3) * LANES]
                )

    def bins_of(row):
        if row < 2 or row >= azimuth + 2:
            k = row if row < 2 else row - azimuth
            starts = [(halo, 4 * (azimuth + 4) + k, 4) for halo in halos[:3]]
            starts.append((next_sides[0], next_sides[0].shape[0] - 4 * RANGE + k, 4))
        else:
            starts = [(slot, row - 2 - offset, stride) for slot, (offset, stride) in zip(slots, offsets)]
        return jnp.concatenate([ref[pl.ds(start, RANGE, stride=stride), :] for ref, start, stride in starts], axis=0)

    total = jnp.zeros((radial, LANES), jnp.float32) if first else carry_sum[...]
    for group in batches(low_row, high_row):
        result = product(jnp.concatenate([bins_of(row) for row in group], axis=1), table1_ref, 0)
        if group[0] == low_row:
            loads[0].wait()
        for k, row in enumerate(group):
            part = result[k * radial : (k + 1) * radial]
            gate = widened(gate_ref, inner, row)
            for t in range(2):
                frag = part[:, (t + 2) * LANES : (t + 3) * LANES]
                second[row - base, t, inner, :] = part[:, t * LANES : (t + 1) * LANES] + gate * frag
                if own_low <= row < own_high:
                    total += second_held[row - own_low, t] * frag

    loads[1].wait()
    loads[2].wait()
    for group in batches(first_low, first_high):
        parts = []
        for row in group:
            halves = [
                stencil(
                    second,
                    lambda d: (row - base + d, t),
                    center_ref[t, outer, :],
                    lower_ref[t, outer, :],
                    upper_ref[t, outer, :],
                    side_ref[t : t + 1, :],
                    8,
                    wide,
                )
                for t in range(2)
            ]
            parts.append(jnp.concatenate(halves, axis=1))
        result = product(jnp.concatenate(parts, axis=0), table_held)
        for k, row in enumerate(group):
            part = result[k * wide : (k + 1) * wide]
            frag = part[:, LANES:]
            initial[row - first_base, outer, :] = part[:, :LANES] + widened(gate_ref, outer, row) * frag
            if 2 <= row < azimuth + 2:
                total += moved_held[row - max(first_low, 2)] * frag[8 : 8 + radial]
    if last:
        sum_out[...] = jnp.broadcast_to(jnp.sum(total.T, axis=0, keepdims=True), sum_out.shape)
    else:
        sum_out[...] = total

    for row in range(out_low, out_high):
        result = stencil(
            initial,
            lambda d: (row - first_base + d,),
            center_ref[1, inner, :],
            lower_ref[1, inner, :],
            upper_ref[1, inner, :],
            side_ref[1:2, :],
            EDGE,
            radial,
        ).T
        rows = pl.ds(row - out_low, RANGE, stride=out_high - out_low)
        own_out[rows, :] = result[:RANGE]
        next_out[rows, :] = result[RANGE:]

    if not last:
        keep_second[...] = second[pl.ds(high_row - 2 - base, 2)]
        keep_first[...] = initial[pl.ds(first_high - 2 - first_base, 2)]


def call(kernel, outs, scratch, operands, any_in=(), any_out=(), copies=0):
    def spec(is_any):
        return pl.BlockSpec(memory_space=pl.ANY if is_any else pltpu.VMEM)

    semaphores = [pltpu.SemaphoreType.DMA((copies,))] if copies else []
    return pl.pallas_call(
        kernel,
        out_shape=[jax.ShapeDtypeStruct(o, jnp.float32) for o in outs],
        in_specs=[spec(k in any_in) for k in range(len(operands))],
        out_specs=[spec(k in any_out) for k in range(len(outs))],
        scratch_shapes=[
            pltpu.VMEM(s, jnp.float32) if isinstance(s, tuple) else pltpu.VMEM(s.shape, s.dtype) for s in scratch
        ]
        + semaphores,
        compiler_params=pltpu.CompilerParams(vmem_limit_bytes=VMEM_LIMIT),
    )(*operands)


def per_device(
    density,
    cotangent,
    drift_in,
    drift_out,
    spread,
    dest_bins,
    bott_split,
    coag_rate,
    frag_pairs,
    frag_gain,
    frag_rate,
    collide_speed,
    frag_speed,
    regime,
):
    own_bins, azimuth, radial = density.shape
    place = lax.axis_index("mass")
    phis, rows = lax.axis_size("phi"), lax.axis_size("row")
    cuts = [0, azimuth // 2 + 2, azimuth]
    spans = list(zip(cuts, cuts[1:]))

    def far(x):
        return lax.ppermute(x, "mass", [(0, 2), (2, 1), (1, 0)])

    def near(x):
        return lax.ppermute(x, "mass", [(0, 1), (1, 2)])

    def ending(x):
        return lax.ppermute(x, "mass", [(3, 2)])

    def returning(x):
        return lax.ppermute(x, "mass", [(2, 3)])

    count = azimuth + 4
    length = radial + 2 * EDGE
    share_rows, strip_rows = length + 8, 4 * count

    def flat(x):
        return x.reshape(-1, LANES)

    sides, gate, slope, opening, shares, first_cells, last_cells, late = call(
        functools.partial(opening_kernel, azimuth, radial, cuts[1]),
        [
            (8 * own_bins + 8, LANES),
            (azimuth, radial),
            (radial, LANES),
            (cuts[1] * own_bins + share_rows, LANES),
            (share_rows, LANES),
            (azimuth, 2, LANES),
            (azimuth, 2, LANES),
            (own_bins * (azimuth - cuts[1]), radial),
        ],
        [],
        [
            flat(cotangent),
            flat(density),
            drift_in,
            drift_out,
            spread[None, :],
            collide_speed,
            frag_speed[None, :],
            regime,
        ],
    )
    ring = [(i, (i + 1) % phis) for i in range(phis)]
    other = lax.ppermute(sides, "phi", ring)
    if phis > 2:
        after = lax.ppermute(sides, "phi", [(j, i) for i, j in ring])
        from_last = lax.broadcasted_iota(jnp.int32, other.shape, 0) % 4 < 2
        other = jnp.where(from_last, other, after)

    density_next = ending(density)
    far_first, near_first = far(opening), near(opening)
    left_cells, right_cells, gates = call(
        functools.partial(radial_kernel, azimuth, radial),
        [(2 * count + 8, LANES), (2 * count + 8, LANES), (radial, LANES)],
        [],
        [other, flat(first_cells), flat(last_cells), gate],
    )
    line = [(i, i + 1) for i in range(rows - 1)]
    left = lax.ppermute(left_cells, "row", line)
    right = lax.ppermute(right_cells, "row", [(j, i) for i, j in line])
    gates, density_next = lax.optimization_barrier((gates, density_next))
    long, short, gates = call(
        functools.partial(halo_kernel, azimuth, radial),
        [(strip_rows + 4 * own_bins + share_rows, LANES), (strip_rows + 4 * own_bins, LANES), (length, LANES)],
        [],
        [left, right, other, shares, gates],
    )

    frag_gain, long = lax.optimization_barrier((frag_gain, long))
    vmem = pl.BlockSpec(memory_space=pltpu.VMEM)
    total_bins = frag_gain.shape[0]
    both, own_cols, own_rows = pl.pallas_call(
        table_kernel,
        out_shape=[jax.ShapeDtypeStruct((3 * total_bins, n * total_bins), jnp.bfloat16) for n in (2, 1, 1)],
        in_specs=[vmem] * 5 + [pl.BlockSpec(memory_space=pltpu.SMEM)],
        out_specs=[vmem] * 3,
        compiler_params=pltpu.CompilerParams(vmem_limit_bytes=VMEM_LIMIT),
    )(
        frag_gain,
        dest_bins[None, :],
        bott_split[None, :],
        coag_rate[None, :],
        frag_rate[None, :],
        frag_pairs,
    )

    long_next = ending(long)
    long, other = lax.optimization_barrier((long, other))
    first_next = jnp.concatenate([opening[: own_bins * cuts[1]], other[: 4 * own_bins]], axis=0)
    halo_refs = [far(short), near(short), short, long_next]
    first_next = ending(first_next)
    far_late, near_late = far(late), near(late)

    coefs = [(2, length, LANES)] * 3 + [(2, LANES)]
    products = list(call(
        functools.partial(forward_kernel, azimuth, radial, cuts),
        [(j - i, radial, LANES) for i, j in moved_spans(cuts)]
        + [(j - i, 2, radial, LANES) for i, j in spans]
        + coefs,
        [
            (count, length, LANES),
            (count, 2, length, LANES),
            (2, share_rows, LANES),
            (azimuth, radial, LANES),
            (azimuth, 2, radial, LANES),
        ],
        [
            flat(density),
            flat(density_next),
            far_first,
            near_first,
            shares,
            long,
            long_next,
            gates,
            slope,
            own_rows,
        ],
        any_in=(2, 3),
        any_out=range(2 * len(spans)),
        copies=2 + len(spans) + sum(len(batches(i, j)) for i, j in spans),
    ))
    groups = len(spans)
    products[0], halo_refs[0], halo_refs[1], late = lax.optimization_barrier(
        (products[0], halo_refs[0], halo_refs[1], late)
    )
    gathered = [[far_first, near_first, opening, first_next], [far_late, near_late, late, ending(late)]]
    moved, second, coefs = products[:groups], products[groups : 2 * groups], products[2 * groups :]

    own_outs, next_outs, carry = [], [], []
    for g in range(groups):
        first, last = g == 0, g == groups - 1
        low_row = 0 if first else cuts[g] + 2
        high_row = azimuth + 4 if last else cuts[g + 1] + 2
        new = high_row - low_row
        n_out = (azimuth + 2 if last else high_row - 2) - (2 if first else low_row - 2)
        operands = [*gathered[min(g, 1)]]
        offsets = [(cuts[0], cuts[1]) if first else (cuts[1], azimuth - cuts[1])] * 4
        operands += halo_refs + ([] if first else [first_next])
        operands += [*coefs, gates, second[g], moved[g]]
        held = len(operands) - 2
        operands += [both, own_cols, *carry]
        outs = [(RANGE * n_out, radial), (RANGE * n_out + 8 * first, radial), (8, radial) if last else (radial, LANES)]
        if not last:
            outs += [(2, 2, length, LANES), (2, length, LANES)]
        own_out, next_out, total, *kept = call(
            functools.partial(adjoint_kernel, azimuth, radial, low_row, high_row, offsets),
            outs,
            [
                (new + 2, 2, length, LANES),
                (new + 2, length, LANES),
                second[g].shape,
                moved[g].shape,
                own_cols,
            ],
            operands,
            any_in=(held, held + 1, held + 3),
            copies=3,
        )
        carry = [*kept, total]
        own_outs.append(own_out)
        next_outs.append(returning(next_out))
    speed_gradient = total[0]
    step = 1
    while step < phis:
        speed_gradient += lax.ppermute(speed_gradient, "phi", [(i, i ^ step) for i in range(phis)])
        step *= 2
    size = lax.axis_size("mass")
    shares = [
        lax.ppermute(speed_gradient, "mass", [(i, (i + k) % size) for i in range(size)]) for k in range(1, size)
    ]
    shares = jnp.stack([*reversed(shares), speed_gradient] * 2)
    speed_gradient = jnp.sum(lax.dynamic_slice_in_dim(shares, size - 1 - place, size, 0), axis=0)
    next_outs = lax.optimization_barrier(next_outs)
    result = jnp.concatenate(
        [
            jnp.where(place == 3, there[: here.shape[0]], here).reshape(own_bins, -1, radial)
            for here, there in zip(own_outs, next_outs)
        ],
        axis=1,
    )
    return (result, speed_gradient)


def solution(mesh):
    in_specs = (
        P("mass", "phi", "row"),
        P("mass", "phi", "row"),
        P("mass", None),
        P("mass", None),
        P("mass"),
        P(),
        P(),
        P(),
        P(),
        P(),
        P(),
        P("phi", "row"),
        P("row"),
        P("phi", "row"),
    )
    out_specs = (P("mass", "phi", "row"), P("row"))
    return jax.shard_map(
        per_device, mesh=mesh, in_specs=in_specs, out_specs=out_specs, check_vma=False
    )
```

```python
import functools

import jax
import jax.numpy as jnp
from jax import lax
from jax.experimental import pallas as pl
from jax.experimental.pallas import tpu as pltpu
from jax.sharding import PartitionSpec as P

RANGE = 64
LANES = 128
EDGE = 16
gate_width = 0.5
BATCH = 8
EDGE = 16
gate_width = 0.5
BATCH = 8
VMEM_LIMIT = 56 * 2**20


def split(value):
    high = value.astype(jnp.bfloat16)
    return high, (value - high.astype(jnp.float32)).astype(jnp.bfloat16)


def product(value, table_ref, axis=1):
    high, low = split(value)
    return lax.dot_general(
        jnp.concatenate([high, low, high], axis=axis),
        table_ref[...],
        (((axis,), (0,)), ((), ())),
        preferred_element_type=jnp.float32,
    )


def stencil(slab, index, center, lower, upper, side, start, size):
    rows = pl.ds(start, size)
    return (
        center * slab[(*index(0), rows)]
        + lower * slab[(*index(0), pl.ds(start - 1, size))]
        + upper * slab[(*index(0), pl.ds(start + 1, size))]
        + side * (slab[(*index(-1), rows)] + slab[(*index(1), rows)])
    )


def batches(low, high):
    return [range(i, min(i + BATCH, high)) for i in range(low, high, BATCH)]


def opening_kernel(azimuth, radial, first_rows, *refs):
    cot_ref, den_ref, in_ref, out_ref, spread_ref, collide_ref, speed_ref, regime_ref = refs[:8]
    sides_ref, gate_ref, slope_ref, opening_ref, shares_ref, first_ref, last_ref, late_ref = refs[8:]
    sigma = jax.nn.sigmoid((collide_ref[...] - speed_ref[...]) / gate_width)
    flagged = regime_ref[...].astype(jnp.float32)
    gate = flagged * sigma
    gate_ref[...] = gate
    ahead = (lax.axis_index("mass") < 3).astype(jnp.float32)
    slope = -flagged * sigma * (1.0 - sigma) / gate_width * ahead
    slope_ref[:, :azimuth] = slope.T
    for k, row in enumerate((azimuth - 2, azimuth - 1, 0, 1)):
        source, target = pl.ds(row, RANGE, stride=azimuth), pl.ds(k, RANGE, stride=4)
        sides_ref[target, :] = cot_ref[source, :]
        sides_ref[pl.ds(4 * RANGE + k, RANGE, stride=4), :] = den_ref[source, :]
        sides_ref[8 * RANGE + k : 8 * RANGE + k + 1, :] = gate[row : row + 1]
    sides_ref[8 * RANGE + 4 :, :] = jnp.zeros((4, radial), jnp.float32)

    block, blocks = lax.axis_index("row"), lax.axis_size("row")

    def window(number):
        lanes = pl.ds(pl.multiple_of(number * radial, radial), radial)
        return jnp.concatenate([in_ref[:, lanes], out_ref[:, lanes]], axis=0).T

    before = window(jnp.maximum(block - 1, 0))[radial - EDGE :] * (block > 0).astype(jnp.float32)
    after = window(jnp.minimum(block + 1, blocks - 1))[:EDGE] * (block < blocks - 1).astype(jnp.float32)
    spread = jnp.concatenate([spread_ref[...], spread_ref[...]], axis=1)
    spread = jnp.broadcast_to(spread, (8, LANES))
    shares = jnp.concatenate([before, window(block), after, spread], axis=0)
    shares_ref[...] = shares
    opening_ref[RANGE * first_rows :, :] = shares
    for b in range(RANGE):
        opening_ref[b * first_rows : (b + 1) * first_rows, :] = cot_ref[b * azimuth : b * azimuth + first_rows, :]
        low, high = b * (azimuth - first_rows), (b + 1) * (azimuth - first_rows)
        late_ref[low:high, :] = cot_ref[b * azimuth + first_rows : (b + 1) * azimuth, :]

    @pl.loop(0, azimuth // BATCH)
    def _(b):
        for k in range(BATCH):
            a = b * BATCH + k
            rows = pl.ds(a, RANGE, stride=azimuth)
            wide = jnp.concatenate([cot_ref[rows, :], den_ref[rows, :]], axis=0).T
            first_ref[a] = wide[:2]
            last_ref[a] = wide[radial - 2 :]


def radial_kernel(azimuth, radial, sides_ref, first_ref, last_ref, gate_ref, left_ref, right_ref, table_ref):
    count = azimuth + 4
    gates = jnp.concatenate(
        [
            sides_ref[8 * RANGE : 8 * RANGE + 2, :],
            gate_ref[...],
            sides_ref[8 * RANGE + 2 : 8 * RANGE + 4, :],
            jnp.zeros((LANES - count, radial), jnp.float32),
        ],
        axis=0,
    ).T
    table_ref[...] = gates
    for out_ref, own_ref, start in ((left_ref, last_ref, radial - 2), (right_ref, first_ref, 0)):
        for k, row in ((0, 0), (1, 1), (2, azimuth + 2), (3, azimuth + 3)):
            wide = sides_ref[pl.ds(k, 2 * RANGE, stride=4), :].T
            out_ref[2 * row : 2 * row + 2, :] = wide[start : start + 2]
        out_ref[4 : 4 + 2 * azimuth, :] = own_ref[...]
        out_ref[2 * count : 2 * count + 2, :] = gates[start : start + 2]
        out_ref[2 * count + 2 :, :] = jnp.zeros((6, LANES), jnp.float32)


def halo_kernel(azimuth, radial, left_ref, right_ref, sides_ref, shares_ref, gates_ref, *refs):
    long_ref, short_ref, table_ref = refs
    count = azimuth + 4
    for k in range(2):
        for source, start in ((left_ref, k), (right_ref, 2 + k)):
            cells = source[pl.ds(k, count, stride=2), :]
            long_ref[pl.ds(start, count, stride=4), :] = cells
            short_ref[pl.ds(start, count, stride=4), :] = cells
    strips = 4 * count
    short_ref[strips:, :] = sides_ref[: 4 * RANGE, :]
    long_ref[strips : strips + 4 * RANGE, :] = sides_ref[4 * RANGE : 8 * RANGE, :]
    long_ref[strips + 4 * RANGE :, :] = shares_ref[...]
    table_ref[...] = jnp.zeros(table_ref.shape, jnp.float32)
    table_ref[EDGE - 2 : EDGE, :] = left_ref[2 * count : 2 * count + 2, :]
    table_ref[EDGE : EDGE + radial, :] = gates_ref[...]
    table_ref[EDGE + radial : EDGE + radial + 2, :] = right_ref[2 * count : 2 * count + 2, :]


def slot_ranges():
    place = lax.axis_index("mass")
    return [
        jnp.where(place == 2, 0, jnp.where(place == 3, 4, place + 1)),
        jnp.where((place == 1) | (place == 2), place - 1, 4),
        place,
        jnp.where(place == 2, 3, 4),
    ]


def table_kernel(gain_ref, dest_ref, split_ref, coag_ref, frag_ref, pairs_ref, both_ref, cols_ref, rows_ref):
    ranges = slot_ranges()
    size = 4 * RANGE

    def ordered(value, scales=(1, 1, 1, 1)):
        parts = []
        for r, scale in zip(ranges, scales):
            part = jnp.zeros((value.shape[0], RANGE), value.dtype)
            for q in range(4):
                part = jnp.where(r == q, value[:, q * RANGE : (q + 1) * RANGE], part)
            parts.append(part * scale)
        return jnp.concatenate(parts, axis=1)

    def bin_ids(axis):
        ids = lax.broadcasted_iota(jnp.int32, (size, size), axis)
        shift = jnp.zeros((size, size), jnp.int32)
        for k, r in enumerate(ranges):
            shift = jnp.where((ids >= k * RANGE) & (ids < (k + 1) * RANGE), (r - k) * RANGE, shift)
        return ids + shift

    gains = []
    for r in ranges:
        held = jnp.minimum(r, 3)
        block = gain_ref[pl.ds(pl.multiple_of(held * RANGE, RANGE), RANGE), :]
        scales = [
            jnp.where((r < 4) & (c < 4), pairs_ref[held, jnp.minimum(c, 3)], 0).astype(jnp.float32) for c in ranges
        ]
        gains.append(ordered(block, scales))
    row_ids, col_ids = bin_ids(0), bin_ids(1)
    target = ordered(dest_ref[...])
    upper = ordered(split_ref[...])
    keeper = (row_ids == col_ids).astype(jnp.float32)
    moved = jnp.where(row_ids == target, 1.0 - upper, 0.0) + jnp.where(row_ids == target + 1, upper, 0.0)
    coag = (moved - keeper) * ordered(coag_ref[...]) + keeper
    frag = jnp.where(row_ids <= col_ids, jnp.concatenate(gains, axis=0), 0.0) - keeper * ordered(frag_ref[...])
    own = jnp.concatenate([coag[:, 2 * RANGE :], frag[:, 2 * RANGE :]], axis=1)
    for ref, table in ((both_ref, jnp.concatenate([coag, frag], axis=1)), (cols_ref, own), (rows_ref, own.T)):
        high, low = split(table)
        ref[:size] = high
        ref[size : 2 * size] = high
        ref[2 * size :] = low


def widened(ref, rows, lane):
    value = ref[rows, lane : lane + 1]
    return jnp.broadcast_to(value, (value.shape[0], LANES))


def pair(left, right, half):
    lanes = slice(half * RANGE, (half + 1) * RANGE)
    return jnp.concatenate([left[:, lanes], right[:, lanes]], axis=1)


def moved_spans(cuts):
    ends = [0, *(cut - 1 for cut in cuts[1:-1]), cuts[-1]]
    return list(zip(ends, ends[1:]))


def load_shares(shares, t, length, center_ref, lower_ref, upper_ref, side_ref):
    left, right = [ref[pl.ds(start, length + 8), :] for ref, start in shares[2 * t : 2 * t + 2]]
    inward = pair(left[:length], right[:length], 0)
    outward = pair(left[:length], right[:length], 1)
    side = pair(left[length:], right[length:], 0)[:1]
    lower_ref[t] = inward
    upper_ref[t] = outward
    side_ref[t : t + 1] = side
    center_ref[t] = 1.0 - inward - outward - 2.0 * side


def forward_kernel(azimuth, radial, cuts, *refs):
    own_ref, next_ref, far_ref, near_ref, share_ref, own_halo, next_halo, gate_ref, slope_ref, table_ref = refs[:10]
    refs = refs[10:]
    groups = len(cuts) - 1
    moved_refs, second_refs = refs[:groups], refs[groups : 2 * groups]
    center_ref, inward_ref, outward_ref, side_ref, slab, mixed, held, moved_all, second_all, sems = refs[2 * groups :]
    inner = pl.ds(EDGE, radial)
    wide = radial + 16
    outer = pl.ds(8, wide)
    length = radial + 2 * EDGE
    strips = 4 * (azimuth + 4)
    first_rows = RANGE * cuts[1]
    loads = [
        pltpu.make_async_copy(ref.at[pl.ds(first_rows, length + 8)], held.at[k], sems.at[k])
        for k, ref in enumerate((far_ref, near_ref))
    ]
    for load in loads:
        load.start()
    stores = []

    def store(source, target):
        copy = pltpu.make_async_copy(source, target, sems.at[2 + len(stores)])
        copy.start()
        stores.append(copy)

    shares = [None, None, (share_ref, 0), (next_halo, strips + 4 * RANGE)]
    load_shares(shares, 1, length, center_ref, inward_ref, outward_ref, side_ref)

    def place(row, source, other, start, stride):
        bins = jnp.concatenate(
            [source[pl.ds(start, RANGE, stride=stride), :], other[pl.ds(start, RANGE, stride=stride), :]], axis=0
        )
        slab[row, inner, :] = bins.T

    for row, k in ((0, 0), (1, 1), (azimuth + 2, 2), (azimuth + 3, 3)):
        place(row, own_halo, next_halo, strips + k, 4)

    @pl.loop(0, azimuth // BATCH)
    def _(b):
        for k in range(BATCH):
            place(b * BATCH + k + 2, own_ref, next_ref, b * BATCH + k, azimuth)

    for row in range(azimuth + 4):
        cells = slice(4 * row, 4 * row + 4)
        strip = pair(own_halo[cells], next_halo[cells], 1)
        slab[row, pl.ds(EDGE - 2, 2), :] = strip[:2]
        slab[row, pl.ds(EDGE + radial, 2), :] = strip[2:]

    def move(rows):
        parts = []
        for a in rows:
            moved = stencil(
                slab,
                lambda d: (a + d,),
                center_ref[1, outer, :],
                outward_ref[1, pl.ds(7, wide), :],
                inward_ref[1, pl.ds(9, wide), :],
                side_ref[1:2, :],
                8,
                wide,
            )
            parts.append(jnp.concatenate([moved, widened(gate_ref, outer, a) * moved], axis=1))
        result = product(jnp.concatenate(parts, axis=0), table_ref)
        for k, a in enumerate(rows):
            mixed[a, 0, outer, :] = result[k * wide : (k + 1) * wide, :LANES]
            mixed[a, 1, outer, :] = result[k * wide : (k + 1) * wide, LANES:]
        return [part[8 : 8 + radial, :LANES] for part in parts]

    move([1, azimuth + 2])

    for rows in batches(0, azimuth):
        for a, moved in zip(rows, move([a + 2 for a in rows])):
            moved_all[a] = widened(slope_ref, slice(None), a) * moved
    for g, (low, high) in enumerate(moved_spans(cuts)):
        store(moved_all.at[pl.ds(low, high - low)], moved_refs[g])

    for load in loads:
        load.wait()
    shares = [(held.at[0], 0), (held.at[1], 0), (share_ref, 0), (next_halo, strips + 4 * RANGE)]
    load_shares(shares, 0, length, center_ref, inward_ref, outward_ref, side_ref)

    for g, (low, high) in enumerate(zip(cuts, cuts[1:])):
        for rows in batches(low, high):
            for a in rows:
                slope = widened(slope_ref, slice(None), a)
                for t in range(2):
                    second = stencil(
                        mixed,
                        lambda d: (a + 2 + d, t),
                        center_ref[t, inner, :],
                        outward_ref[t, pl.ds(EDGE - 1, radial), :],
                        inward_ref[t, pl.ds(EDGE + 1, radial), :],
                        side_ref[t : t + 1, :],
                        EDGE,
                        radial,
                    )
                    second_all[a, t] = slope * second
            size = len(rows)
            store(second_all.at[pl.ds(rows[0], size)], second_refs[g].at[pl.ds(rows[0] - low, size)])

    for copy in stores:
        copy.wait()


def adjoint_kernel(azimuth, radial, low_row, high_row, offsets, *refs):
    first, last = low_row == 0, high_row == azimuth + 4
    refs = list(refs)

    def take(number):
        taken = refs[:number]
        del refs[:number]
        return taken

    slots = take(4)
    halos = take(4)
    next_sides = slots[3:] if first else take(1)
    center_ref, lower_ref, upper_ref, side_ref = take(4)
    gate_ref, second_ref, moved_ref = take(3)
    table1_ref, table2_ref = take(2)
    carry_second, carry_first, carry_sum = (None, None, None) if first else take(3)
    own_out, next_out, sum_out = take(3)
    keep_second, keep_first = (None, None) if last else take(2)
    second, initial, second_held, moved_held, table_held, sems = refs
    loads = [
        pltpu.make_async_copy(source, target, sems.at[k])
        for k, (source, target) in enumerate(
            ((second_ref, second_held), (moved_ref, moved_held), (table2_ref, table_held))
        )
    ]
    for load in loads:
        load.start()

    inner = pl.ds(EDGE, radial)
    wide = radial + 16
    outer = pl.ds(8, wide)
    base = low_row if first else low_row - 2
    first_low, first_high = (1 if first else low_row - 1), high_row - 1
    first_base = first_low if first else first_low - 2
    out_low, out_high = first_base + 1, first_high - 1
    own_low, own_high = max(low_row, 2), min(high_row, azimuth + 2)

    if not first:
        second[pl.ds(0, 2)] = carry_second[...]
        initial[pl.ds(0, 2)] = carry_first[...]

    cells = slice(4 * low_row, 4 * high_row)
    edges = [halo[cells] for halo in halos]
    edges = product(jnp.concatenate([pair(*edges[:2], 0), pair(*edges[2:], 0)], axis=1), table1_ref)
    for row in range(low_row, high_row):
        piece = edges[4 * (row - low_row) : 4 * (row - low_row) + 4]
        for start, k in ((EDGE - 2, 0), (EDGE + radial, 2)):
            gate = widened(gate_ref, pl.ds(start, 2), row)
            for t in range(2):
                second[row - base, t, pl.ds(start, 2), :] = (
                    piece[k : k + 2, t * LANES : (t + 1) * LANES]
                    + gate * piece[k : k + 2, (t + 2) * LANES : (t + 3) * LANES]
                )

    def bins_of(row):
        if row < 2 or row >= azimuth + 2:
            k = row if row < 2 else row - azimuth
            starts = [(halo, 4 * (azimuth + 4) + k, 4) for halo in halos[:3]]
            starts.append((next_sides[0], next_sides[0].shape[0] - 4 * RANGE + k, 4))
        else:
            starts = [(slot, row - 2 - offset, stride) for slot, (offset, stride) in zip(slots, offsets)]
        return jnp.concatenate([ref[pl.ds(start, RANGE, stride=stride), :] for ref, start, stride in starts], axis=0)

    total = jnp.zeros((radial, LANES), jnp.float32) if first else carry_sum[...]
    for group in batches(low_row, high_row):
        result = product(jnp.concatenate([bins_of(row) for row in group], axis=1), table1_ref, 0)
        if group[0] == low_row:
            loads[0].wait()
        for k, row in enumerate(group):
            part = result[k * radial : (k + 1) * radial]
            gate = widened(gate_ref, inner, row)
            for t in range(2):
                frag = part[:, (t + 2) * LANES : (t + 3) * LANES]
                second[row - base, t, inner, :] = part[:, t * LANES : (t + 1) * LANES] + gate * frag
                if own_low <= row < own_high:
                    total += second_held[row - own_low, t] * frag

    loads[1].wait()
    loads[2].wait()
    for group in batches(first_low, first_high):
        parts = []
        for row in group:
            halves = [
                stencil(
                    second,
                    lambda d: (row - base + d, t),
                    center_ref[t, outer, :],
                    lower_ref[t, outer, :],
                    upper_ref[t, outer, :],
                    side_ref[t : t + 1, :],
                    8,
                    wide,
                )
                for t in range(2)
            ]
            parts.append(jnp.concatenate(halves, axis=1))
        result = product(jnp.concatenate(parts, axis=0), table_held)
        for k, row in enumerate(group):
            part = result[k * wide : (k + 1) * wide]
            frag = part[:, LANES:]
            initial[row - first_base, outer, :] = part[:, :LANES] + widened(gate_ref, outer, row) * frag
            if 2 <= row < azimuth + 2:
                total += moved_held[row - max(first_low, 2)] * frag[8 : 8 + radial]
    if last:
        sum_out[...] = jnp.broadcast_to(jnp.sum(total.T, axis=0, keepdims=True), sum_out.shape)
    else:
        sum_out[...] = total

    for row in range(out_low, out_high):
        result = stencil(
            initial,
            lambda d: (row - first_base + d,),
            center_ref[1, inner, :],
            lower_ref[1, inner, :],
            upper_ref[1, inner, :],
            side_ref[1:2, :],
            EDGE,
            radial,
        ).T
        rows = pl.ds(row - out_low, RANGE, stride=out_high - out_low)
        own_out[rows, :] = result[:RANGE]
        next_out[rows, :] = result[RANGE:]

    if not last:
        keep_second[...] = second[pl.ds(high_row - 2 - base, 2)]
        keep_first[...] = initial[pl.ds(first_high - 2 - first_base, 2)]


def call(kernel, outs, scratch, operands, any_in=(), any_out=(), copies=0):
    def spec(is_any):
        return pl.BlockSpec(memory_space=pl.ANY if is_any else pltpu.VMEM)

    semaphores = [pltpu.SemaphoreType.DMA((copies,))] if copies else []
    return pl.pallas_call(
        kernel,
        out_shape=[jax.ShapeDtypeStruct(o, jnp.float32) for o in outs],
        in_specs=[spec(k in any_in) for k in range(len(operands))],
        out_specs=[spec(k in any_out) for k in range(len(outs))],
        scratch_shapes=[
            pltpu.VMEM(s, jnp.float32) if isinstance(s, tuple) else pltpu.VMEM(s.shape, s.dtype) for s in scratch
        ]
        + semaphores,
        compiler_params=pltpu.CompilerParams(vmem_limit_bytes=VMEM_LIMIT),
    )(*operands)


def per_device(
    density,
    cotangent,
    drift_in,
    drift_out,
    spread,
    dest_bins,
    bott_split,
    coag_rate,
    frag_pairs,
    frag_gain,
    frag_rate,
    collide_speed,
    frag_speed,
    regime,
):
    own_bins, azimuth, radial = density.shape
    place = lax.axis_index("mass")
    phis, rows = lax.axis_size("phi"), lax.axis_size("row")
    cuts = [0, azimuth // 2 + 2, azimuth]
    spans = list(zip(cuts, cuts[1:]))

    def far(x):
        return lax.ppermute(x, "mass", [(0, 2), (2, 1), (1, 0)])

    def near(x):
        return lax.ppermute(x, "mass", [(0, 1), (1, 2)])

    def ending(x):
        return lax.ppermute(x, "mass", [(3, 2)])

    def returning(x):
        return lax.ppermute(x, "mass", [(2, 3)])

    count = azimuth + 4
    length = radial + 2 * EDGE
    share_rows, strip_rows = length + 8, 4 * count

    def flat(x):
        return x.reshape(-1, LANES)

    sides, gate, slope, opening, shares, first_cells, last_cells, late = call(
        functools.partial(opening_kernel, azimuth, radial, cuts[1]),
        [
            (8 * own_bins + 8, LANES),
            (azimuth, radial),
            (radial, LANES),
            (cuts[1] * own_bins + share_rows, LANES),
            (share_rows, LANES),
            (azimuth, 2, LANES),
            (azimuth, 2, LANES),
            (own_bins * (azimuth - cuts[1]), radial),
        ],
        [],
        [
            flat(cotangent),
            flat(density),
            drift_in,
            drift_out,
            spread[None, :],
            collide_speed,
            frag_speed[None, :],
            regime,
        ],
    )
    ring = [(i, (i + 1) % phis) for i in range(phis)]
    other = lax.ppermute(sides, "phi", ring)
    if phis > 2:
        after = lax.ppermute(sides, "phi", [(j, i) for i, j in ring])
        from_last = lax.broadcasted_iota(jnp.int32, other.shape, 0) % 4 < 2
        other = jnp.where(from_last, other, after)

    density_next = ending(density)
    far_first, near_first = far(opening), near(opening)
    left_cells, right_cells, gates = call(
        functools.partial(radial_kernel, azimuth, radial),
        [(2 * count + 8, LANES), (2 * count + 8, LANES), (radial, LANES)],
        [],
        [other, flat(first_cells), flat(last_cells), gate],
    )
    line = [(i, i + 1) for i in range(rows - 1)]
    left = lax.ppermute(left_cells, "row", line)
    right = lax.ppermute(right_cells, "row", [(j, i) for i, j in line])
    gates, density_next = lax.optimization_barrier((gates, density_next))
    long, short, gates = call(
        functools.partial(halo_kernel, azimuth, radial),
        [(strip_rows + 4 * own_bins + share_rows, LANES), (strip_rows + 4 * own_bins, LANES), (length, LANES)],
        [],
        [left, right, other, shares, gates],
    )

    frag_gain, long = lax.optimization_barrier((frag_gain, long))
    vmem = pl.BlockSpec(memory_space=pltpu.VMEM)
    total_bins = frag_gain.shape[0]
    both, own_cols, own_rows = pl.pallas_call(
        table_kernel,
        out_shape=[jax.ShapeDtypeStruct((3 * total_bins, n * total_bins), jnp.bfloat16) for n in (2, 1, 1)],
        in_specs=[vmem] * 5 + [pl.BlockSpec(memory_space=pltpu.SMEM)],
        out_specs=[vmem] * 3,
        compiler_params=pltpu.CompilerParams(vmem_limit_bytes=VMEM_LIMIT),
    )(
        frag_gain,
        dest_bins[None, :],
        bott_split[None, :],
        coag_rate[None, :],
        frag_rate[None, :],
        frag_pairs,
    )

    long_next = ending(long)
    long, other = lax.optimization_barrier((long, other))
    first_next = jnp.concatenate([opening[: own_bins * cuts[1]], other[: 4 * own_bins]], axis=0)
    halo_refs = [far(short), near(short), short, long_next]
    first_next = ending(first_next)
    far_late, near_late = far(late), near(late)

    coefs = [(2, length, LANES)] * 3 + [(2, LANES)]
    products = list(call(
        functools.partial(forward_kernel, azimuth, radial, cuts),
        [(j - i, radial, LANES) for i, j in moved_spans(cuts)]
        + [(j - i, 2, radial, LANES) for i, j in spans]
        + coefs,
        [
            (count, length, LANES),
            (count, 2, length, LANES),
            (2, share_rows, LANES),
            (azimuth, radial, LANES),
            (azimuth, 2, radial, LANES),
        ],
        [
            flat(density),
            flat(density_next),
            far_first,
            near_first,
            shares,
            long,
            long_next,
            gates,
            slope,
            own_rows,
        ],
        any_in=(2, 3),
        any_out=range(2 * len(spans)),
        copies=2 + len(spans) + sum(len(batches(i, j)) for i, j in spans),
    ))
    groups = len(spans)
    products[0], halo_refs[0], halo_refs[1], late = lax.optimization_barrier(
        (products[0], halo_refs[0], halo_refs[1], late)
    )
    gathered = [[far_first, near_first, opening, first_next], [far_late, near_late, late, ending(late)]]
    moved, second, coefs = products[:groups], products[groups : 2 * groups], products[2 * groups :]

    own_outs, next_outs, carry = [], [], []
    for g in range(groups):
        first, last = g == 0, g == groups - 1
        low_row = 0 if first else cuts[g] + 2
        high_row = azimuth + 4 if last else cuts[g + 1] + 2
        new = high_row - low_row
        n_out = (azimuth + 2 if last else high_row - 2) - (2 if first else low_row - 2)
        operands = [*gathered[min(g, 1)]]
        offsets = [(cuts[0], cuts[1]) if first else (cuts[1], azimuth - cuts[1])] * 4
        operands += halo_refs + ([] if first else [first_next])
        operands += [*coefs, gates, second[g], moved[g]]
        held = len(operands) - 2
        operands += [both, own_cols, *carry]
        outs = [(RANGE * n_out, radial), (RANGE * n_out + 8 * first, radial), (1, radial) if last else (radial, LANES)]
        if not last:
            outs += [(2, 2, length, LANES), (2, length, LANES)]
        own_out, next_out, total, *kept = call(
            functools.partial(adjoint_kernel, azimuth, radial, low_row, high_row, offsets),
            outs,
            [
                (new + 2, 2, length, LANES),
                (new + 2, length, LANES),
                second[g].shape,
                moved[g].shape,
                own_cols,
            ],
            operands,
            any_in=(held, held + 1, held + 3),
            copies=3,
        )
        carry = [*kept, total]
        own_outs.append(own_out)
        next_outs.append(returning(next_out))
    speed_gradient = total
    step = 1
    while step < phis:
        speed_gradient += lax.ppermute(speed_gradient, "phi", [(i, i ^ step) for i in range(phis)])
        step *= 2
    shares = [lax.ppermute(speed_gradient, "mass", [(i, i ^ k) for i in range(4)]) for k in range(1, 4)]
    speed_gradient = ((speed_gradient + shares[0]) + (shares[1] + shares[2]))[0]
    next_outs = lax.optimization_barrier(next_outs)
    result = jnp.concatenate(
        [
            jnp.where(place == 3, there[: here.shape[0]], here).reshape(own_bins, -1, radial)
            for here, there in zip(own_outs, next_outs)
        ],
        axis=1,
    )
    return (result, speed_gradient)


def solution(mesh):
    in_specs = (
        P("mass", "phi", "row"),
        P("mass", "phi", "row"),
        P("mass", None),
        P("mass", None),
        P("mass"),
        P(),
        P(),
        P(),
        P(),
        P(),
        P(),
        P("phi", "row"),
        P("row"),
        P("phi", "row"),
    )
    out_specs = (P("mass", "phi", "row"), P("row"))
    return jax.shard_map(
        per_device, mesh=mesh, in_specs=in_specs, out_specs=out_specs, check_vma=False
    )
```

```python
import functools

import jax
import jax.numpy as jnp
from jax import lax
from jax.experimental import pallas as pl
from jax.experimental.pallas import tpu as pltpu
from jax.sharding import PartitionSpec as P

RANGE = 64
LANES = 128
EDGE = 16
gate_width = 0.5
BATCH = 8
EDGE = 16
gate_width = 0.5
BATCH = 8
VMEM_LIMIT = 56 * 2**20


def split(value):
    high = value.astype(jnp.bfloat16)
    return high, (value - high.astype(jnp.float32)).astype(jnp.bfloat16)


def product(value, table_ref, axis=1):
    high, low = split(value)
    return lax.dot_general(
        jnp.concatenate([high, low, high], axis=axis),
        table_ref[...],
        (((axis,), (0,)), ((), ())),
        preferred_element_type=jnp.float32,
    )


def stencil(slab, index, center, lower, upper, side, start, size):
    rows = pl.ds(start, size)
    return (
        center * slab[(*index(0), rows)]
        + lower * slab[(*index(0), pl.ds(start - 1, size))]
        + upper * slab[(*index(0), pl.ds(start + 1, size))]
        + side * (slab[(*index(-1), rows)] + slab[(*index(1), rows)])
    )


def batches(low, high):
    return [range(i, min(i + BATCH, high)) for i in range(low, high, BATCH)]


def opening_kernel(azimuth, radial, first_rows, *refs):
    cot_ref, den_ref, in_ref, out_ref, spread_ref, collide_ref, speed_ref, regime_ref = refs[:8]
    sides_ref, gate_ref, slope_ref, opening_ref, shares_ref, first_ref, last_ref, late_ref = refs[8:]
    sigma = jax.nn.sigmoid((collide_ref[...] - speed_ref[...]) / gate_width)
    flagged = regime_ref[...].astype(jnp.float32)
    gate = flagged * sigma
    gate_ref[...] = gate
    ahead = (lax.axis_index("mass") < 3).astype(jnp.float32)
    slope = -flagged * sigma * (1.0 - sigma) / gate_width * ahead
    slope_ref[:, :azimuth] = slope.T
    for k, row in enumerate((azimuth - 2, azimuth - 1, 0, 1)):
        source, target = pl.ds(row, RANGE, stride=azimuth), pl.ds(k, RANGE, stride=4)
        sides_ref[target, :] = cot_ref[source, :]
        sides_ref[pl.ds(4 * RANGE + k, RANGE, stride=4), :] = den_ref[source, :]
        sides_ref[8 * RANGE + k : 8 * RANGE + k + 1, :] = gate[row : row + 1]
    sides_ref[8 * RANGE + 4 :, :] = jnp.zeros((4, radial), jnp.float32)

    block, blocks = lax.axis_index("row"), lax.axis_size("row")

    def window(number):
        lanes = pl.ds(pl.multiple_of(number * radial, radial), radial)
        return jnp.concatenate([in_ref[:, lanes], out_ref[:, lanes]], axis=0).T

    before = window(jnp.maximum(block - 1, 0))[radial - EDGE :] * (block > 0).astype(jnp.float32)
    after = window(jnp.minimum(block + 1, blocks - 1))[:EDGE] * (block < blocks - 1).astype(jnp.float32)
    spread = jnp.concatenate([spread_ref[...], spread_ref[...]], axis=1)
    spread = jnp.broadcast_to(spread, (8, LANES))
    shares = jnp.concatenate([before, window(block), after, spread], axis=0)
    shares_ref[...] = shares
    opening_ref[RANGE * first_rows :, :] = shares
    for b in range(RANGE):
        opening_ref[b * first_rows : (b + 1) * first_rows, :] = cot_ref[b * azimuth : b * azimuth + first_rows, :]
        low, high = b * (azimuth - first_rows), (b + 1) * (azimuth - first_rows)
        late_ref[low:high, :] = cot_ref[b * azimuth + first_rows : (b + 1) * azimuth, :]

    @pl.loop(0, azimuth // BATCH)
    def _(b):
        for k in range(BATCH):
            a = b * BATCH + k
            rows = pl.ds(a, RANGE, stride=azimuth)
            wide = jnp.concatenate([cot_ref[rows, :], den_ref[rows, :]], axis=0).T
            first_ref[a] = wide[:2]
            last_ref[a] = wide[radial - 2 :]


def radial_kernel(azimuth, radial, sides_ref, first_ref, last_ref, gate_ref, left_ref, right_ref, table_ref):
    count = azimuth + 4
    gates = jnp.concatenate(
        [
            sides_ref[8 * RANGE : 8 * RANGE + 2, :],
            gate_ref[...],
            sides_ref[8 * RANGE + 2 : 8 * RANGE + 4, :],
            jnp.zeros((LANES - count, radial), jnp.float32),
        ],
        axis=0,
    ).T
    table_ref[...] = gates
    for out_ref, own_ref, start in ((left_ref, last_ref, radial - 2), (right_ref, first_ref, 0)):
        for k, row in ((0, 0), (1, 1), (2, azimuth + 2), (3, azimuth + 3)):
            wide = sides_ref[pl.ds(k, 2 * RANGE, stride=4), :].T
            out_ref[2 * row : 2 * row + 2, :] = wide[start : start + 2]
        out_ref[4 : 4 + 2 * azimuth, :] = own_ref[...]
        out_ref[2 * count : 2 * count + 2, :] = gates[start : start + 2]
        out_ref[2 * count + 2 :, :] = jnp.zeros((6, LANES), jnp.float32)


def halo_kernel(azimuth, radial, left_ref, right_ref, sides_ref, shares_ref, gates_ref, *refs):
    long_ref, short_ref, table_ref = refs
    count = azimuth + 4
    for k in range(2):
        for source, start in ((left_ref, k), (right_ref, 2 + k)):
            cells = source[pl.ds(k, count, stride=2), :]
            long_ref[pl.ds(start, count, stride=4), :] = cells
            short_ref[pl.ds(start, count, stride=4), :] = cells
    strips = 4 * count
    short_ref[strips:, :] = sides_ref[: 4 * RANGE, :]
    long_ref[strips : strips + 4 * RANGE, :] = sides_ref[4 * RANGE : 8 * RANGE, :]
    long_ref[strips + 4 * RANGE :, :] = shares_ref[...]
    table_ref[...] = jnp.zeros(table_ref.shape, jnp.float32)
    table_ref[EDGE - 2 : EDGE, :] = left_ref[2 * count : 2 * count + 2, :]
    table_ref[EDGE : EDGE + radial, :] = gates_ref[...]
    table_ref[EDGE + radial : EDGE + radial + 2, :] = right_ref[2 * count : 2 * count + 2, :]


def slot_ranges():
    place = lax.axis_index("mass")
    return [
        jnp.where(place == 2, 0, jnp.where(place == 3, 4, place + 1)),
        jnp.where((place == 1) | (place == 2), place - 1, 4),
        place,
        jnp.where(place == 2, 3, 4),
    ]


def table_kernel(gain_ref, dest_ref, split_ref, coag_ref, frag_ref, pairs_ref, both_ref, cols_ref, rows_ref):
    ranges = slot_ranges()
    size = 4 * RANGE

    def ordered(value, scales=(1, 1, 1, 1)):
        parts = []
        for r, scale in zip(ranges, scales):
            part = jnp.zeros((value.shape[0], RANGE), value.dtype)
            for q in range(4):
                part = jnp.where(r == q, value[:, q * RANGE : (q + 1) * RANGE], part)
            parts.append(part * scale)
        return jnp.concatenate(parts, axis=1)

    def bin_ids(axis):
        ids = lax.broadcasted_iota(jnp.int32, (size, size), axis)
        shift = jnp.zeros((size, size), jnp.int32)
        for k, r in enumerate(ranges):
            shift = jnp.where((ids >= k * RANGE) & (ids < (k + 1) * RANGE), (r - k) * RANGE, shift)
        return ids + shift

    gains = []
    for r in ranges:
        held = jnp.minimum(r, 3)
        block = gain_ref[pl.ds(pl.multiple_of(held * RANGE, RANGE), RANGE), :]
        scales = [
            jnp.where((r < 4) & (c < 4), pairs_ref[held, jnp.minimum(c, 3)], 0).astype(jnp.float32) for c in ranges
        ]
        gains.append(ordered(block, scales))
    row_ids, col_ids = bin_ids(0), bin_ids(1)
    target = ordered(dest_ref[...])
    upper = ordered(split_ref[...])
    keeper = (row_ids == col_ids).astype(jnp.float32)
    moved = jnp.where(row_ids == target, 1.0 - upper, 0.0) + jnp.where(row_ids == target + 1, upper, 0.0)
    coag = (moved - keeper) * ordered(coag_ref[...]) + keeper
    frag = jnp.where(row_ids <= col_ids, jnp.concatenate(gains, axis=0), 0.0) - keeper * ordered(frag_ref[...])
    own = jnp.concatenate([coag[:, 2 * RANGE :], frag[:, 2 * RANGE :]], axis=1)
    for ref, table in ((both_ref, jnp.concatenate([coag, frag], axis=1)), (cols_ref, own), (rows_ref, own.T)):
        high, low = split(table)
        ref[:size] = high
        ref[size : 2 * size] = high
        ref[2 * size :] = low


def widened(ref, rows, lane):
    value = ref[rows, lane : lane + 1]
    return jnp.broadcast_to(value, (value.shape[0], LANES))


def pair(left, right, half):
    lanes = slice(half * RANGE, (half + 1) * RANGE)
    return jnp.concatenate([left[:, lanes], right[:, lanes]], axis=1)


def moved_spans(cuts):
    ends = [0, *(cut - 1 for cut in cuts[1:-1]), cuts[-1]]
    return list(zip(ends, ends[1:]))


def load_shares(shares, t, length, center_ref, lower_ref, upper_ref, side_ref):
    left, right = [ref[pl.ds(start, length + 8), :] for ref, start in shares[2 * t : 2 * t + 2]]
    inward = pair(left[:length], right[:length], 0)
    outward = pair(left[:length], right[:length], 1)
    side = pair(left[length:], right[length:], 0)[:1]
    lower_ref[t] = inward
    upper_ref[t] = outward
    side_ref[t : t + 1] = side
    center_ref[t] = 1.0 - inward - outward - 2.0 * side


def forward_kernel(azimuth, radial, cuts, *refs):
    own_ref, next_ref, far_ref, near_ref, share_ref, own_halo, next_halo, gate_ref, slope_ref, table_ref = refs[:10]
    refs = refs[10:]
    groups = len(cuts) - 1
    moved_refs, second_refs = refs[:groups], refs[groups : 2 * groups]
    center_ref, inward_ref, outward_ref, side_ref, slab, mixed, held, moved_all, second_all, sems = refs[2 * groups :]
    inner = pl.ds(EDGE, radial)
    wide = radial + 16
    outer = pl.ds(8, wide)
    length = radial + 2 * EDGE
    strips = 4 * (azimuth + 4)
    first_rows = RANGE * cuts[1]
    loads = [
        pltpu.make_async_copy(ref.at[pl.ds(first_rows, length + 8)], held.at[k], sems.at[k])
        for k, ref in enumerate((far_ref, near_ref))
    ]
    for load in loads:
        load.start()
    stores = []

    def store(source, target):
        copy = pltpu.make_async_copy(source, target, sems.at[2 + len(stores)])
        copy.start()
        stores.append(copy)

    shares = [None, None, (share_ref, 0), (next_halo, strips + 4 * RANGE)]
    load_shares(shares, 1, length, center_ref, inward_ref, outward_ref, side_ref)

    def place(row, source, other, start, stride):
        bins = jnp.concatenate(
            [source[pl.ds(start, RANGE, stride=stride), :], other[pl.ds(start, RANGE, stride=stride), :]], axis=0
        )
        slab[row, inner, :] = bins.T

    for row, k in ((0, 0), (1, 1), (azimuth + 2, 2), (azimuth + 3, 3)):
        place(row, own_halo, next_halo, strips + k, 4)

    @pl.loop(0, azimuth // BATCH)
    def _(b):
        for k in range(BATCH):
            place(b * BATCH + k + 2, own_ref, next_ref, b * BATCH + k, azimuth)

    for row in range(azimuth + 4):
        cells = slice(4 * row, 4 * row + 4)
        strip = pair(own_halo[cells], next_halo[cells], 1)
        slab[row, pl.ds(EDGE - 2, 2), :] = strip[:2]
        slab[row, pl.ds(EDGE + radial, 2), :] = strip[2:]

    def move(rows):
        parts = []
        for a in rows:
            moved = stencil(
                slab,
                lambda d: (a + d,),
                center_ref[1, outer, :],
                outward_ref[1, pl.ds(7, wide), :],
                inward_ref[1, pl.ds(9, wide), :],
                side_ref[1:2, :],
                8,
                wide,
            )
            parts.append(jnp.concatenate([moved, widened(gate_ref, outer, a) * moved], axis=1))
        result = product(jnp.concatenate(parts, axis=0), table_ref)
        for k, a in enumerate(rows):
            mixed[a, 0, outer, :] = result[k * wide : (k + 1) * wide, :LANES]
            mixed[a, 1, outer, :] = result[k * wide : (k + 1) * wide, LANES:]
        return [part[8 : 8 + radial, :LANES] for part in parts]

    move([1, azimuth + 2])

    for rows in batches(0, azimuth):
        for a, moved in zip(rows, move([a + 2 for a in rows])):
            moved_all[a] = widened(slope_ref, slice(None), a) * moved
    for g, (low, high) in enumerate(moved_spans(cuts)):
        store(moved_all.at[pl.ds(low, high - low)], moved_refs[g])

    for load in loads:
        load.wait()
    shares = [(held.at[0], 0), (held.at[1], 0), (share_ref, 0), (next_halo, strips + 4 * RANGE)]
    load_shares(shares, 0, length, center_ref, inward_ref, outward_ref, side_ref)

    for g, (low, high) in enumerate(zip(cuts, cuts[1:])):
        for rows in batches(low, high):
            for a in rows:
                slope = widened(slope_ref, slice(None), a)
                for t in range(2):
                    second = stencil(
                        mixed,
                        lambda d: (a + 2 + d, t),
                        center_ref[t, inner, :],
                        outward_ref[t, pl.ds(EDGE - 1, radial), :],
                        inward_ref[t, pl.ds(EDGE + 1, radial), :],
                        side_ref[t : t + 1, :],
                        EDGE,
                        radial,
                    )
                    second_all[a, t] = slope * second
            size = len(rows)
            store(second_all.at[pl.ds(rows[0], size)], second_refs[g].at[pl.ds(rows[0] - low, size)])

    for copy in stores:
        copy.wait()


def adjoint_kernel(azimuth, radial, low_row, high_row, offsets, *refs):
    first, last = low_row == 0, high_row == azimuth + 4
    refs = list(refs)

    def take(number):
        taken = refs[:number]
        del refs[:number]
        return taken

    slots = take(4)
    halos = take(4)
    next_sides = slots[3:] if first else take(1)
    center_ref, lower_ref, upper_ref, side_ref = take(4)
    gate_ref, second_ref, moved_ref = take(3)
    table1_ref, table2_ref = take(2)
    carry_second, carry_first, carry_sum = (None, None, None) if first else take(3)
    own_out, next_out, sum_out = take(3)
    keep_second, keep_first = (None, None) if last else take(2)
    second, initial, second_held, moved_held, table_held, sems = refs
    loads = [
        pltpu.make_async_copy(source, target, sems.at[k])
        for k, (source, target) in enumerate(
            ((second_ref, second_held), (moved_ref, moved_held), (table2_ref, table_held))
        )
    ]
    for load in loads:
        load.start()

    inner = pl.ds(EDGE, radial)
    wide = radial + 16
    outer = pl.ds(8, wide)
    base = low_row if first else low_row - 2
    first_low, first_high = (1 if first else low_row - 1), high_row - 1
    first_base = first_low if first else first_low - 2
    out_low, out_high = first_base + 1, first_high - 1
    own_low, own_high = max(low_row, 2), min(high_row, azimuth + 2)

    if not first:
        second[pl.ds(0, 2)] = carry_second[...]
        initial[pl.ds(0, 2)] = carry_first[...]

    cells = slice(4 * low_row, 4 * high_row)
    edges = [halo[cells] for halo in halos]
    edges = product(jnp.concatenate([pair(*edges[:2], 0), pair(*edges[2:], 0)], axis=1), table1_ref)
    for row in range(low_row, high_row):
        piece = edges[4 * (row - low_row) : 4 * (row - low_row) + 4]
        for start, k in ((EDGE - 2, 0), (EDGE + radial, 2)):
            gate = widened(gate_ref, pl.ds(start, 2), row)
            for t in range(2):
                second[row - base, t, pl.ds(start, 2), :] = (
                    piece[k : k + 2, t * LANES : (t + 1) * LANES]
                    + gate * piece[k : k + 2, (t + 2) * LANES : (t + 3) * LANES]
                )

    def bins_of(row):
        if row < 2 or row >= azimuth + 2:
            k = row if row < 2 else row - azimuth
            starts = [(halo, 4 * (azimuth + 4) + k, 4) for halo in halos[:3]]
            starts.append((next_sides[0], next_sides[0].shape[0] - 4 * RANGE + k, 4))
        else:
            starts = [(slot, row - 2 - offset, stride) for slot, (offset, stride) in zip(slots, offsets)]
        return jnp.concatenate([ref[pl.ds(start, RANGE, stride=stride), :] for ref, start, stride in starts], axis=0)

    total = jnp.zeros((radial, LANES), jnp.float32) if first else carry_sum[...]
    for group in batches(low_row, high_row):
        result = product(jnp.concatenate([bins_of(row) for row in group], axis=1), table1_ref, 0)
        if group[0] == low_row:
            loads[0].wait()
        for k, row in enumerate(group):
            part = result[k * radial : (k + 1) * radial]
            gate = widened(gate_ref, inner, row)
            for t in range(2):
                frag = part[:, (t + 2) * LANES : (t + 3) * LANES]
                second[row - base, t, inner, :] = part[:, t * LANES : (t + 1) * LANES] + gate * frag
                if own_low <= row < own_high:
                    total += second_held[row - own_low, t] * frag

    loads[1].wait()
    loads[2].wait()
    for group in batches(first_low, first_high):
        parts = []
        for row in group:
            halves = [
                stencil(
                    second,
                    lambda d: (row - base + d, t),
                    center_ref[t, outer, :],
                    lower_ref[t, outer, :],
                    upper_ref[t, outer, :],
                    side_ref[t : t + 1, :],
                    8,
                    wide,
                )
                for t in range(2)
            ]
            parts.append(jnp.concatenate(halves, axis=1))
        result = product(jnp.concatenate(parts, axis=0), table_held)
        for k, row in enumerate(group):
            part = result[k * wide : (k + 1) * wide]
            frag = part[:, LANES:]
            initial[row - first_base, outer, :] = part[:, :LANES] + widened(gate_ref, outer, row) * frag
            if 2 <= row < azimuth + 2:
                total += moved_held[row - max(first_low, 2)] * frag[8 : 8 + radial]
    if last:
        sum_out[...] = jnp.broadcast_to(jnp.sum(total.T, axis=0, keepdims=True), sum_out.shape)
    else:
        sum_out[...] = total

    for row in range(out_low, out_high):
        result = stencil(
            initial,
            lambda d: (row - first_base + d,),
            center_ref[1, inner, :],
            lower_ref[1, inner, :],
            upper_ref[1, inner, :],
            side_ref[1:2, :],
            EDGE,
            radial,
        ).T
        rows = pl.ds(row - out_low, RANGE, stride=out_high - out_low)
        own_out[rows, :] = result[:RANGE]
        next_out[rows, :] = result[RANGE:]

    if not last:
        keep_second[...] = second[pl.ds(high_row - 2 - base, 2)]
        keep_first[...] = initial[pl.ds(first_high - 2 - first_base, 2)]


def call(kernel, outs, scratch, operands, any_in=(), any_out=(), copies=0):
    def spec(is_any):
        return pl.BlockSpec(memory_space=pl.ANY if is_any else pltpu.VMEM)

    semaphores = [pltpu.SemaphoreType.DMA((copies,))] if copies else []
    return pl.pallas_call(
        kernel,
        out_shape=[jax.ShapeDtypeStruct(o, jnp.float32) for o in outs],
        in_specs=[spec(k in any_in) for k in range(len(operands))],
        out_specs=[spec(k in any_out) for k in range(len(outs))],
        scratch_shapes=[
            pltpu.VMEM(s, jnp.float32) if isinstance(s, tuple) else pltpu.VMEM(s.shape, s.dtype) for s in scratch
        ]
        + semaphores,
        compiler_params=pltpu.CompilerParams(vmem_limit_bytes=VMEM_LIMIT),
    )(*operands)


def per_device(
    density,
    cotangent,
    drift_in,
    drift_out,
    spread,
    dest_bins,
    bott_split,
    coag_rate,
    frag_pairs,
    frag_gain,
    frag_rate,
    collide_speed,
    frag_speed,
    regime,
):
    own_bins, azimuth, radial = density.shape
    place = lax.axis_index("mass")
    phis, rows = lax.axis_size("phi"), lax.axis_size("row")
    cuts = [0, azimuth // 2 + 2, azimuth]
    spans = list(zip(cuts, cuts[1:]))

    def far(x):
        return lax.ppermute(x, "mass", [(0, 2), (2, 1), (1, 0)])

    def near(x):
        return lax.ppermute(x, "mass", [(0, 1), (1, 2)])

    def ending(x):
        return lax.ppermute(x, "mass", [(3, 2)])

    def returning(x):
        return lax.ppermute(x, "mass", [(2, 3)])

    count = azimuth + 4
    length = radial + 2 * EDGE
    share_rows, strip_rows = length + 8, 4 * count

    def flat(x):
        return x.reshape(-1, LANES)

    sides, gate, slope, opening, shares, first_cells, last_cells, late = call(
        functools.partial(opening_kernel, azimuth, radial, cuts[1]),
        [
            (8 * own_bins + 8, LANES),
            (azimuth, radial),
            (radial, LANES),
            (cuts[1] * own_bins + share_rows, LANES),
            (share_rows, LANES),
            (azimuth, 2, LANES),
            (azimuth, 2, LANES),
            (own_bins * (azimuth - cuts[1]), radial),
        ],
        [],
        [
            flat(cotangent),
            flat(density),
            drift_in,
            drift_out,
            spread[None, :],
            collide_speed,
            frag_speed[None, :],
            regime,
        ],
    )
    ring = [(i, (i + 1) % phis) for i in range(phis)]
    other = lax.ppermute(sides, "phi", ring)
    if phis > 2:
        after = lax.ppermute(sides, "phi", [(j, i) for i, j in ring])
        from_last = lax.broadcasted_iota(jnp.int32, other.shape, 0) % 4 < 2
        other = jnp.where(from_last, other, after)

    density_next = ending(density)
    far_first, near_first = far(opening), near(opening)
    frag_gain, gate = lax.optimization_barrier((frag_gain, gate))
    vmem = pl.BlockSpec(memory_space=pltpu.VMEM)
    total_bins = frag_gain.shape[0]
    both, own_cols, own_rows = pl.pallas_call(
        table_kernel,
        out_shape=[jax.ShapeDtypeStruct((3 * total_bins, n * total_bins), jnp.bfloat16) for n in (2, 1, 1)],
        in_specs=[vmem] * 5 + [pl.BlockSpec(memory_space=pltpu.SMEM)],
        out_specs=[vmem] * 3,
        compiler_params=pltpu.CompilerParams(vmem_limit_bytes=VMEM_LIMIT),
    )(
        frag_gain,
        dest_bins[None, :],
        bott_split[None, :],
        coag_rate[None, :],
        frag_rate[None, :],
        frag_pairs,
    )
    gate, both = lax.optimization_barrier((gate, both))
    left_cells, right_cells, gates = call(
        functools.partial(radial_kernel, azimuth, radial),
        [(2 * count + 8, LANES), (2 * count + 8, LANES), (radial, LANES)],
        [],
        [other, flat(first_cells), flat(last_cells), gate],
    )
    line = [(i, i + 1) for i in range(rows - 1)]
    left = lax.ppermute(left_cells, "row", line)
    right = lax.ppermute(right_cells, "row", [(j, i) for i, j in line])
    gates, density_next = lax.optimization_barrier((gates, density_next))
    long, short, gates = call(
        functools.partial(halo_kernel, azimuth, radial),
        [(strip_rows + 4 * own_bins + share_rows, LANES), (strip_rows + 4 * own_bins, LANES), (length, LANES)],
        [],
        [left, right, other, shares, gates],
    )

    long_next = ending(long)
    long, other = lax.optimization_barrier((long, other))
    first_next = jnp.concatenate([opening[: own_bins * cuts[1]], other[: 4 * own_bins]], axis=0)
    halo_refs = [far(short), near(short), short, long_next]
    first_next = ending(first_next)
    far_late, near_late = far(late), near(late)

    coefs = [(2, length, LANES)] * 3 + [(2, LANES)]
    products = list(call(
        functools.partial(forward_kernel, azimuth, radial, cuts),
        [(j - i, radial, LANES) for i, j in moved_spans(cuts)]
        + [(j - i, 2, radial, LANES) for i, j in spans]
        + coefs,
        [
            (count, length, LANES),
            (count, 2, length, LANES),
            (2, share_rows, LANES),
            (azimuth, radial, LANES),
            (azimuth, 2, radial, LANES),
        ],
        [
            flat(density),
            flat(density_next),
            far_first,
            near_first,
            shares,
            long,
            long_next,
            gates,
            slope,
            own_rows,
        ],
        any_in=(2, 3),
        any_out=range(2 * len(spans)),
        copies=2 + len(spans) + sum(len(batches(i, j)) for i, j in spans),
    ))
    groups = len(spans)
    products[0], halo_refs[0], halo_refs[1], late = lax.optimization_barrier(
        (products[0], halo_refs[0], halo_refs[1], late)
    )
    gathered = [[far_first, near_first, opening, first_next], [far_late, near_late, late, ending(late)]]
    moved, second, coefs = products[:groups], products[groups : 2 * groups], products[2 * groups :]

    own_outs, next_outs, carry = [], [], []
    for g in range(groups):
        first, last = g == 0, g == groups - 1
        low_row = 0 if first else cuts[g] + 2
        high_row = azimuth + 4 if last else cuts[g + 1] + 2
        new = high_row - low_row
        n_out = (azimuth + 2 if last else high_row - 2) - (2 if first else low_row - 2)
        operands = [*gathered[min(g, 1)]]
        offsets = [(cuts[0], cuts[1]) if first else (cuts[1], azimuth - cuts[1])] * 4
        operands += halo_refs + ([] if first else [first_next])
        operands += [*coefs, gates, second[g], moved[g]]
        held = len(operands) - 2
        operands += [both, own_cols, *carry]
        outs = [(RANGE * n_out, radial), (RANGE * n_out + 8 * first, radial), (1, radial) if last else (radial, LANES)]
        if not last:
            outs += [(2, 2, length, LANES), (2, length, LANES)]
        own_out, next_out, total, *kept = call(
            functools.partial(adjoint_kernel, azimuth, radial, low_row, high_row, offsets),
            outs,
            [
                (new + 2, 2, length, LANES),
                (new + 2, length, LANES),
                second[g].shape,
                moved[g].shape,
                own_cols,
            ],
            operands,
            any_in=(held, held + 1, held + 3),
            copies=3,
        )
        carry = [*kept, total]
        own_outs.append(own_out)
        next_outs.append(returning(next_out))
    speed_gradient = total
    step = 1
    while step < phis:
        speed_gradient += lax.ppermute(speed_gradient, "phi", [(i, i ^ step) for i in range(phis)])
        step *= 2
    shares = [lax.ppermute(speed_gradient, "mass", [(i, i ^ k) for i in range(4)]) for k in range(1, 4)]
    speed_gradient = ((speed_gradient + shares[0]) + (shares[1] + shares[2]))[0]
    next_outs = lax.optimization_barrier(next_outs)
    result = jnp.concatenate(
        [
            jnp.where(place == 3, there[: here.shape[0]], here).reshape(own_bins, -1, radial)
            for here, there in zip(own_outs, next_outs)
        ],
        axis=1,
    )
    return (result, speed_gradient)


def solution(mesh):
    in_specs = (
        P("mass", "phi", "row"),
        P("mass", "phi", "row"),
        P("mass", None),
        P("mass", None),
        P("mass"),
        P(),
        P(),
        P(),
        P(),
        P(),
        P(),
        P("phi", "row"),
        P("row"),
        P("phi", "row"),
    )
    out_specs = (P("mass", "phi", "row"), P("row"))
    return jax.shard_map(
        per_device, mesh=mesh, in_specs=in_specs, out_specs=out_specs, check_vma=False
    )
```
